128 devices in a mesh: fsdp: 8 (over z_hi, x), ctx: 2 (over core), tp: 8 (over y, z_lo).
Axes of the slice: x: 4, y: 4, z: 4 (z_hi: 2, z_lo: 2; z = z_hi * 2 + z_lo), core: 2. Of those that a mesh axis runs over, the one named last changes fastest.
Arguments:
- hidden_in: bfloat16 [16384, 1536], P(('fsdp', 'ctx', 'tp')), may hold values from -6 to 6
- cotangent: bfloat16 [16384, 1536], P(('fsdp', 'ctx', 'tp')), may hold values from -6 to 6
- seq_lengths: int32 [16, 4], P(('fsdp', 'ctx')), may hold values from 1 to 770, as said below
- w_qkv: float32 [1536, 2048], P(('fsdp', 'ctx', 'tp')), may hold values from -0.15625 to 0.15625
- m_qkv: float32 [1536, 2048], P(('fsdp', 'ctx', 'tp')), may hold values from -80 to 80
- v_qkv: float32 [1536, 2048], P(('fsdp', 'ctx', 'tp')), may hold values from 868.352 to 3440.64
- b_qkv: float32 [2048], replicated, may hold values from -3 to 3
- m_bias: float32 [2048], replicated, may hold values from -80 to 80
- v_bias: float32 [2048], replicated, may hold values from 868.352 to 3440.64
- w_out: float32 [1536, 1536], P(None, ('fsdp', 'ctx', 'tp')), may hold values from -0.875 to 0.875
- m_out: float32 [1536, 1536], P(None, ('fsdp', 'ctx', 'tp')), may hold values from -24 to 24
- v_out: float32 [1536, 1536], P(None, ('fsdp', 'ctx', 'tp')), may hold values from 78.6432 to 311.296
- w_gate_up: float32 [1536, 2, 8960], P(('fsdp', 'ctx'), None, 'tp'), may hold values from -0.15625 to 0.15625
- m_gate_up: float32 [1536, 2, 8960], P(('fsdp', 'ctx'), None, 'tp'), may hold values from -24 to 24
- v_gate_up: float32 [1536, 2, 8960], P(('fsdp', 'ctx'), None, 'tp'), may hold values from 78.6432 to 311.296
- w_down: float32 [8960, 1536], P('tp', ('fsdp', 'ctx')), may hold values from -0.0625 to 0.0625
- m_down: float32 [8960, 1536], P('tp', ('fsdp', 'ctx')), may hold values from -40 to 40
- v_down: float32 [8960, 1536], P('tp', ('fsdp', 'ctx')), may hold values from 212.992 to 868.352
- gains: float32 [2, 1536], P(None, ('fsdp', 'ctx', 'tp')), may hold values from 0.5 to 1.5
- m_gains: float32 [2, 1536], P(None, ('fsdp', 'ctx', 'tp')), may hold values from -80 to 80
- v_gains: float32 [2, 1536], P(None, ('fsdp', 'ctx', 'tp')), may hold values from 868.352 to 3440.64
Outputs:
- hidden_out: float32 [16384, 1536], P(('fsdp', 'ctx', 'tp'))
- grad_in: float32 [16384, 1536], P(('fsdp', 'ctx', 'tp'))
- qkv_new: float32 [1536, 2048], P(('fsdp', 'ctx', 'tp'))
- qkv_moment: float32 [1536, 2048], P(('fsdp', 'ctx', 'tp'))
- qkv_second: float32 [1536, 2048], P(('fsdp', 'ctx', 'tp'))
- bias_new: float32 [2048], replicated
- bias_moment: float32 [2048], replicated
- bias_second: float32 [2048], replicated
- out_new: float32 [1536, 1536], P(None, ('fsdp', 'ctx', 'tp'))
- out_moment: float32 [1536, 1536], P(None, ('fsdp', 'ctx', 'tp'))
- out_second: float32 [1536, 1536], P(None, ('fsdp', 'ctx', 'tp'))
- gate_up_new: float32 [1536, 2, 8960], P(('fsdp', 'ctx'), None, 'tp')
- gate_up_moment: float32 [1536, 2, 8960], P(('fsdp', 'ctx'), None, 'tp')
- gate_up_second: float32 [1536, 2, 8960], P(('fsdp', 'ctx'), None, 'tp')
- down_new: float32 [8960, 1536], P('tp', ('fsdp', 'ctx'))
- down_moment: float32 [8960, 1536], P('tp', ('fsdp', 'ctx'))
- down_second: float32 [8960, 1536], P('tp', ('fsdp', 'ctx'))
- gains_new: float32 [2, 1536], P(None, ('fsdp', 'ctx', 'tp'))
- gains_moment: float32 [2, 1536], P(None, ('fsdp', 'ctx', 'tp'))
- gains_second: float32 [2, 1536], P(None, ('fsdp', 'ctx', 'tp'))
The draws below stay inside these ranges and needn't reach their ends.
Inputs may be any that keep to these rules, and one draw needn't show every extreme that they name: `seq_lengths`: each row lists the lengths of the 4 sequences packed in order into one group; they sum to 1024. In every row one sequence, neither the first nor the last, is 1024 - 2 * (127) long; the sequences before it together hold 127 tokens, and so do those after it.
All inputs are finite; a program needn't handle non-finite values.
Results may differ from the reference program's by a relative error of at most 0.018.
Values may be sent and summed in bfloat16 or wider, within the bound.
A program may use at most 192 MiB of HBM per device.

```python
import math
import jax
import jax.numpy as jnp
from jax import lax

D = 1536
QUERY_HEADS = 12
KEY_VALUE_HEADS = 2
HEAD_SIZE = 128
FF = 8960
PACKED_TOKENS = 1024
NSEQ = 4
STEP = 10
TOK_DEV = 128
GROUPS = 16
TOKENS = 16384
QKV = 2048


def draw_seq_lengths(key, part):
    key = jax.random.fold_in(key, 7)
    place_key = jax.random.fold_in(key, 11)
    rim_tokens = TOK_DEV - 1
    long_len = PACKED_TOKENS - 2 * rim_tokens
    spare = 2 * rim_tokens + 5
    slots = jnp.arange(NSEQ, dtype=jnp.int32)
    cut_index = jnp.arange(rim_tokens - 1, dtype=jnp.int32)

    def one_row(row_key, before):
        first_key, second_key = jax.random.split(row_key)
        first = jax.random.permutation(first_key, jnp.arange(1, rim_tokens, dtype=jnp.int32))
        second = jax.random.permutation(second_key, jnp.arange(1, rim_tokens, dtype=jnp.int32)) + rim_tokens
        first = jnp.where(cut_index < before - 1, first, spare).astype(jnp.int32)
        second = jnp.where(cut_index < NSEQ - 2 - before, second, spare).astype(jnp.int32)
        joined = jnp.concatenate([first, second, jnp.full((1,), rim_tokens, jnp.int32)])
        cuts = jnp.sort(joined)[:NSEQ - 2].astype(jnp.int32)
        edges = jnp.concatenate([jnp.zeros((1,), jnp.int32), cuts, jnp.full((1,), 2 * rim_tokens, jnp.int32)])
        shorts = (edges[1:] - edges[:-1]).astype(jnp.int32)
        index = jnp.clip(jnp.where(slots > before, slots - 1, slots), 0, NSEQ - 2).astype(jnp.int32)
        picked = jnp.take(shorts, index)
        return jnp.where(slots == before, long_len, picked).astype(jnp.int32)
    row_keys = jax.random.split(key, GROUPS)
    chosen = jax.random.randint(place_key, (GROUPS,), 1, NSEQ - 1).astype(jnp.int32)
    return jax.vmap(one_row)(row_keys, chosen).astype(jnp.int32)


def levels(own_key, dims, shards, low, largest):
    factor_of = 1.0
    for dim, blocks in shards:
        steps = jax.random.uniform(jax.random.fold_in(jax.random.fold_in(own_key, 6), dim), (blocks,), jnp.float32, low / len(shards), largest / len(shards))
        factor_of = factor_of * jnp.repeat(jnp.exp(steps), dims[dim] // blocks).reshape((-1,) + (1,) * (len(dims) - 1 - dim))
    return factor_of


def bell_draw(key, shape, deviation, reach, shards=(), kind=jnp.bfloat16):
    result = jax.random.normal(key, shape, jnp.float32) * deviation
    if len(shards) > 0:
        result = levels(key, shape, shards, -0.22, 0.18) * result
    return jnp.clip(result, min=-reach, max=reach).astype(kind)


def setup_inputs(seed: int = 0) -> dict:
    seeds = jax.random.split(jax.random.key(seed), 22)
    return {
        "hidden_in": bell_draw(seeds[0], (TOKENS, D), 1.0, 6.0, ((0, 128),)),
        "cotangent": bell_draw(seeds[1], (TOKENS, D), 1.0, 6.0, ((0, 128),)),
        "seq_lengths": draw_seq_lengths(jax.random.fold_in(seeds[21], 71), 0),
        "w_qkv": bell_draw(seeds[3], (D, QKV), D ** -0.5, 0.15625, ((0, 128),), jnp.float32),
        "m_qkv": bell_draw(seeds[4], (D, QKV), (0.11 * TOKENS ** 0.5), 80.0, ((0, 128),), jnp.float32),
        "v_qkv": jnp.clip(jnp.exp(math.log(3440.64) - 1.3768156 * jax.random.uniform(seeds[5], (D, QKV), jnp.float32) ** levels(seeds[5], (D, QKV), ((0, 128),), -0.2, 0.2)), 868.352, 3440.64),
        "b_qkv": bell_draw(seeds[6], (QKV,), 0.5, 3.0, (), jnp.float32),
        "m_bias": bell_draw(seeds[7], (QKV,), (0.11 * TOKENS ** 0.5), 80.0, (), jnp.float32),
        "v_bias": jnp.clip(jnp.exp(jax.random.uniform(seeds[8], (QKV,), jnp.float32, math.log(868.352), math.log(3440.64))), 868.352, 3440.64),
        "w_out": bell_draw(seeds[9], (QUERY_HEADS * HEAD_SIZE, D), (QUERY_HEADS * HEAD_SIZE // 32) ** -0.5, 0.875, ((1, 128),), jnp.float32),
        "m_out": bell_draw(seeds[10], (QUERY_HEADS * HEAD_SIZE, D), (0.033 * TOKENS ** 0.5), 24.0, ((1, 128),), jnp.float32),
        "v_out": jnp.clip(jnp.exp(math.log(311.296) - 1.375823 * jax.random.uniform(seeds[11], (QUERY_HEADS * HEAD_SIZE, D), jnp.float32) ** levels(seeds[11], (QUERY_HEADS * HEAD_SIZE, D), ((1, 128),), -0.2, 0.2)), 78.6432, 311.296),
        "w_gate_up": bell_draw(seeds[12], (D, 2, FF), D ** -0.5, 0.15625, ((0, 16), (2, 8)), jnp.float32),
        "m_gate_up": bell_draw(seeds[13], (D, 2, FF), (0.033 * TOKENS ** 0.5), 24.0, ((0, 16), (2, 8)), jnp.float32),
        "v_gate_up": jnp.clip(jnp.exp(math.log(311.296) - 1.375823 * jax.random.uniform(seeds[14], (D, 2, FF), jnp.float32) ** levels(seeds[14], (D, 2, FF), ((0, 16), (2, 8)), -0.2, 0.2)), 78.6432, 311.296),
        "w_down": bell_draw(seeds[15], (FF, D), FF ** -0.5, 0.0625, ((0, 8), (1, 16)), jnp.float32),
        "m_down": bell_draw(seeds[16], (FF, D), (0.055 * TOKENS ** 0.5), 40.0, ((0, 8), (1, 16)), jnp.float32),
        "v_down": jnp.clip(jnp.exp(math.log(868.352) - 1.40534252 * jax.random.uniform(seeds[17], (FF, D), jnp.float32) ** levels(seeds[17], (FF, D), ((0, 8), (1, 16)), -0.2, 0.2)), 212.992, 868.352),
        "gains": jnp.clip(1.0 + 0.1 * jax.random.normal(seeds[18], (2, D), jnp.float32), 0.5, 1.5),
        "m_gains": bell_draw(seeds[19], (2, D), (0.11 * TOKENS ** 0.5), 80.0, ((1, 128),), jnp.float32),
        "v_gains": jnp.clip(jnp.exp(math.log(3440.64) - 1.3768156 * jax.random.uniform(seeds[20], (2, D), jnp.float32) ** levels(seeds[20], (2, D), ((1, 128),), -0.2, 0.2)), 868.352, 3440.64),
    }


@jax.custom_vjp
def lower_precision(v):
    return lax.optimization_barrier(v.astype(jnp.bfloat16)).astype(jnp.float32)

@jax.custom_vjp
def low_back(v):
    return v

def low_keep(v):
    return (lower_precision(v), None)

def low_pass(kept, grad):
    return (grad,)

def back_keep(v):
    return (v, None)

def back_low(kept, grad):
    return (lower_precision(grad),)
lower_precision.defvjp(low_keep, low_pass)
low_back.defvjp(back_keep, back_low)
norm_eps = 1e-06
rope_base = 1000000.0
beta_one = 0.9
beta_two = 0.95
adam_eps = 1e-08
weight_decay = 0.1
rate_qkv = 0.05
rate_out = 0.3
rate_gate_up = 0.05
rate_down = 0.02
rate_small = 0.5
highest = lax.Precision.HIGHEST

def product(left, right):
    return jnp.dot(left, right, precision=highest, preferred_element_type=jnp.float32)

def rms_scale(values):
    return lax.rsqrt(lax.optimization_barrier(jnp.mean(values * values, axis=-1, keepdims=True)) + norm_eps)

def doc_layout(lengths, places):
    ends = jnp.cumsum(lengths).astype(jnp.int32)
    starts = (ends - lengths).astype(jnp.int32)
    doc_ids = lax.optimization_barrier(jnp.sum((ends[None, :] <= places[:, None]).astype(jnp.int32), axis=1)).astype(jnp.int32)
    doc_start = lax.optimization_barrier(jnp.max(jnp.where(starts[None, :] <= places[:, None], starts[None, :], 0), axis=1)).astype(jnp.int32)
    return (doc_ids, (places - doc_start).astype(jnp.int32))

def angles(position, size):
    half = size // 2
    freq = jnp.exp(jnp.arange(half, dtype=jnp.float32) * (-2.0 * math.log(rope_base) / size))
    angle = position.astype(jnp.float32)[:, None] * freq[None, :]
    return (jnp.cos(angle), jnp.sin(angle))

def apply_rotation(values, cosine_table, sine_table):
    half = values.shape[-1] // 2
    front = values[..., :half]
    back = values[..., half:]
    return jnp.concatenate([front * cosine_table - back * sine_table, back * cosine_table + front * sine_table], axis=-1)

def block(inputs, lengths, w_qkv, b_qkv, w_out, w_gate_up, w_down, gains):
    places = jnp.arange(PACKED_TOKENS, dtype=jnp.int32)
    doc_ids, positions = doc_layout(lengths, places)
    allowed = (doc_ids[:, None] == doc_ids[None, :]) & (places[None, :] <= places[:, None])
    cosine_table, sine_table = angles(positions, HEAD_SIZE)
    normed_one = lower_precision(inputs * rms_scale(inputs) * gains[0])
    projected_rows = low_back(product(normed_one, w_qkv) + b_qkv)
    heads_of_queries = projected_rows[:, :QUERY_HEADS * HEAD_SIZE].reshape(PACKED_TOKENS, QUERY_HEADS, HEAD_SIZE).transpose(1, 0, 2)
    heads_of_keys = projected_rows[:, QUERY_HEADS * HEAD_SIZE:(QUERY_HEADS + KEY_VALUE_HEADS) * HEAD_SIZE].reshape(PACKED_TOKENS, KEY_VALUE_HEADS, HEAD_SIZE).transpose(1, 0, 2)
    heads_of_values = lower_precision(projected_rows[:, (QUERY_HEADS + KEY_VALUE_HEADS) * HEAD_SIZE:].reshape(PACKED_TOKENS, KEY_VALUE_HEADS, HEAD_SIZE).transpose(1, 0, 2))
    heads_of_queries = lower_precision(apply_rotation(heads_of_queries, cosine_table, sine_table)).reshape(KEY_VALUE_HEADS, QUERY_HEADS // KEY_VALUE_HEADS, PACKED_TOKENS, HEAD_SIZE)
    heads_of_keys = lower_precision(apply_rotation(heads_of_keys, cosine_table, sine_table))
    scores = low_back(jnp.einsum('kgqd,kjd->kgqj', heads_of_queries, heads_of_keys, precision=highest) * HEAD_SIZE ** (-0.5))
    scores = jnp.where(allowed, scores, -1e+30)
    weights = lower_precision(jax.nn.softmax(scores, axis=-1))
    attended = jnp.einsum('kgqj,kjd->qkgd', weights, heads_of_values, precision=highest).reshape(PACKED_TOKENS, QUERY_HEADS * HEAD_SIZE)
    attended = lower_precision(low_back(attended))
    middle = inputs + low_back(product(attended, w_out))
    normed_two = lower_precision(middle * rms_scale(middle) * gains[1])
    gate_up = low_back(product(normed_two, w_gate_up.reshape(D, 2 * FF)).reshape(PACKED_TOKENS, 2, FF))
    hidden = lower_precision(jax.nn.silu(gate_up[:, 0]) * gate_up[:, 1])
    return middle + low_back(product(hidden, w_down))

def adam_step(weight, moment, second, grad, rate, decay):
    moment = beta_one * moment + (1.0 - beta_one) * grad
    second = beta_two * second + (1.0 - beta_two) * grad * grad
    fix_one = 1.0 - beta_one ** STEP
    fix_two = 1.0 - beta_two ** STEP
    direction = moment / fix_one / (jnp.sqrt(second / fix_two) + adam_eps)
    return (weight - rate * (direction + decay * weight), moment, second)

def reference(hidden_in, cotangent, seq_lengths, w_qkv, m_qkv, v_qkv, b_qkv, m_bias, v_bias, w_out, m_out, v_out, w_gate_up, m_gate_up, v_gate_up, w_down, m_down, v_down, gains, m_gains, v_gains):
    inputs = hidden_in.astype(jnp.float32).reshape(GROUPS, PACKED_TOKENS, D)
    params = (w_qkv, b_qkv, w_out, w_gate_up, w_down, gains)

    def forward(values_in, weights):
        rounded = tuple((lower_precision(item) for item in weights))
        layer = jax.checkpoint(block)

        def one_group(carry, item):
            return (carry, layer(item[0], item[1], rounded[0], rounded[1], rounded[2], rounded[3], rounded[4], rounded[5]))
        return lax.scan(one_group, jnp.zeros((), jnp.float32), (values_in, seq_lengths))[1]
    outputs, pullback = jax.vjp(forward, inputs, params)
    grad_inputs, grads = pullback(cotangent.astype(jnp.float32).reshape(GROUPS, PACKED_TOKENS, D))
    qkv_new, qkv_moment, qkv_second = adam_step(w_qkv, m_qkv, v_qkv, grads[0], rate_qkv, weight_decay)
    bias_new, bias_moment, bias_second = adam_step(b_qkv, m_bias, v_bias, grads[1], rate_small, 0.0)
    out_new, out_moment, out_second = adam_step(w_out, m_out, v_out, grads[2], rate_out, weight_decay)
    gate_up_new, gate_up_moment, gate_up_second = adam_step(w_gate_up, m_gate_up, v_gate_up, grads[3], rate_gate_up, weight_decay)
    down_new, down_moment, down_second = adam_step(w_down, m_down, v_down, grads[4], rate_down, weight_decay)
    gains_new, gains_moment, gains_second = adam_step(gains, m_gains, v_gains, grads[5], rate_small, 0.0)
    return (outputs.reshape(TOKENS, D), grad_inputs.reshape(TOKENS, D), qkv_new, qkv_moment, qkv_second, bias_new, bias_moment, bias_second, out_new, out_moment, out_second, gate_up_new, gate_up_moment, gate_up_second, down_new, down_moment, down_second, gains_new, gains_moment, gains_second)
```

```python
import functools
import math

import jax
import jax.numpy as jnp
from jax import lax
from jax.experimental import pallas as pl
from jax.experimental.pallas import tpu as pltpu
from jax.sharding import PartitionSpec as P

QUERY_HEADS = 12
KEY_VALUE_HEADS = 2
HEAD_SIZE = 128
STEP = 10


norm_eps = 1e-06
rope_base = 1000000.0
beta_one = 0.9
beta_two = 0.95
adam_eps = 1e-08
weight_decay = 0.1
rate_qkv = 0.05
rate_out = 0.3
rate_gate_up = 0.05
rate_down = 0.02
rate_small = 0.5

BF = jnp.bfloat16
F32 = jnp.float32
FS, CX, TP = ALL = ("fsdp", "ctx", "tp")
FF_PAD = 1152


class Place:
    def __init__(self):
        self.f = lax.axis_index(FS)
        self.c = lax.axis_index(CX)
        self.t = lax.axis_index(TP)
        self.zh, self.x = self.f // 4, self.f % 4
        self.y, self.zl = self.t // 2, self.t % 2
        self.z = self.zh * 2 + self.zl

    def at(self, x=0, y=0, z=0, c=0):
        zz = (self.z + z) % 4
        return {
            FS: (zz // 2) * 4 + (self.x + x) % 4,
            CX: (self.c + c) % 2,
            TP: ((self.y + y) % 4) * 2 + zz % 2,
        }

    def partner(self):
        return {FS: self.f, CX: self.c, TP: self.y * 2 + 1 - self.zl}

    def mirror(self):
        return {
            FS: (1 - self.zh) * 4 + self.x,
            CX: self.c,
            TP: self.y * 2 + 1 - self.zl,
        }


def greet(devices):
    barrier = pltpu.get_barrier_semaphore()
    for device in devices:
        pl.semaphore_signal(barrier, inc=1, device_id=device, device_id_type=pl.DeviceIdType.MESH)
    pl.semaphore_wait(barrier, len(devices))


class Net:
    def __init__(self, send_sems, recv_sems):
        self.send_sems, self.recv_sems = send_sems, recv_sems
        self.copies, self.arrived = {}, set()

    def send(self, name, src, dst, device, after=()):
        self.need(*after)
        at = len(self.copies)
        copy = pltpu.make_async_remote_copy(
            src_ref=src,
            dst_ref=dst,
            send_sem=self.send_sems.at[at],
            recv_sem=self.recv_sems.at[at],
            device_id=device,
            device_id_type=pl.DeviceIdType.MESH,
        )
        copy.start()
        self.copies[name] = copy

    def need(self, *names):
        for name in names:
            if name not in self.arrived:
                self.arrived.add(name)
                self.copies[name].wait_recv()

    def finish(self):
        self.need(*self.copies)
        for copy in self.copies.values():
            copy.wait_send()


def lanes(at, size):
    return pl.ds(pl.multiple_of(at * size, 128), size)


def gather_start_kernel(a_in, m_in, c_in, w1, w2, mw, cg, gn, pad, wide, blk, send_sems, recv_sems, local_sems):
    p = Place()
    f, c, t, x, y, z, zl, zh = p.f, p.c, p.t, p.x, p.y, p.z, p.zl, p.zh
    R, L = dict(x=1), dict(x=3)
    greet(
        [p.at(c=1)]
        + [p.at(x=i) for i in (1, 2, 3)]
        + [p.at(y=i) for i in (1, 2, 3)]
        + [p.at(z=i) for i in (1, 2, 3)]
    )
    net = Net(send_sems, recv_sems)
    zp = p.partner()
    tp_ = y * 2 + 1 - zl
    net.send(("a", "z"), a_in, pad.at[t], zp)
    for i in (1, 3, 2):
        net.send(("a", "y", i), a_in, pad.at[t], p.at(y=i))
    own_m = pltpu.make_async_copy(m_in, mw.at[f, c], local_sems.at[0])
    own_c = pltpu.make_async_copy(c_in, cg.at[t], local_sems.at[1])
    own_m.start()
    own_c.start()
    pad[t] = a_in[...]
    top, low = pl.ds(0, 48), pl.ds(48, 48)
    net.send(("m", "z"), m_in, mw.at[f, c], p.at(z=2))
    net.send(("m", "r", 0), m_in.at[top], mw.at[f, c, top], p.at(x=1))
    net.send(("m", "l", 1), m_in.at[low], mw.at[f, c, low], p.at(x=3))
    net.send(("m", "r", 1), m_in.at[low], mw.at[f, c, low], p.at(x=1))
    net.send(("m", "l", 0), m_in.at[top], mw.at[f, c, top], p.at(x=3))
    net.send(("m", "c"), m_in, mw.at[f, c], p.at(c=1))
    for i in (1, 3, 2):
        net.send(("a", "p", i), pad.at[tp_], pad.at[tp_], p.at(y=i), after=[("a", "z")])
    ctop, clow = pl.ds(0, 64), pl.ds(64, 64)
    net.send(("c", "z"), c_in, cg.at[t], zp)
    net.send(("c", "r", 0), c_in.at[ctop], cg.at[t, ctop], p.at(y=1))
    net.send(("c", "l", 1), c_in.at[clow], cg.at[t, clow], p.at(y=3))
    net.send(("c", "r", 1), c_in.at[clow], cg.at[t, clow], p.at(y=1))
    net.send(("c", "l", 0), c_in.at[ctop], cg.at[t, ctop], p.at(y=3))
    net.need(("a", "y", 1), ("a", "y", 2), ("a", "y", 3), ("a", "p", 1), ("a", "p", 2), ("a", "p", 3))
    for i in range(8):
        wide[pl.ds(12 * i, 12), :] = pad[i, pl.ds(0, 12), :].astype(F32)
    blk[...] = wide[...].astype(BF)
    s1 = lanes(zl, 1024)
    s2 = lanes(y, 384)
    b1 = blk.at[:, s1]
    b2 = blk.at[:, pl.ds(pl.multiple_of(2048 + y * 384, 128), 384)]
    own_1 = pltpu.make_async_copy(b1, w1.at[f, c, :, s1], local_sems.at[2])
    own_2 = pltpu.make_async_copy(b2, w2.at[f, c, :, s2], local_sems.at[3])
    bg = blk.at[:, pl.ds(3584, 128)]
    own_g = pltpu.make_async_copy(bg, gn.at[f, c], local_sems.at[4])
    own_1.start()
    own_2.start()
    own_g.start()
    for i in (1, 3, 2):
        net.send((1, "x", i), b1, w1.at[f, c, :, s1], p.at(x=i))
    for i in (1, 3, 2):
        net.send((2, "x", i), b2, w2.at[f, c, :, s2], p.at(x=i))
    for i in (1, 3, 2):
        net.send(("g", "x", i), bg, gn.at[f, c], p.at(x=i))
    def along_z(i, src):
        ff = zh * 4 + (x + i) % 4
        net.send((1, "z", 1, i), src, w1.at[ff, c, :, s1], p.at(z=1))
        net.send((1, "z", 3, i), src, w1.at[ff, c, :, s1], p.at(z=3))

    def on_z(i):
        zz = (z + 3) % 4
        ff = (zz // 2) * 4 + (x + i) % 4
        ref = w1.at[ff, c, top, lanes(zz % 2, 1024)]
        net.send((1, "f", 1, i), ref, ref, p.at(z=1), after=[(1, "z", 1, i)])
        zz = (z + 1) % 4
        ff = (zz // 2) * 4 + (x + i) % 4
        ref = w1.at[ff, c, low, lanes(zz % 2, 1024)]
        net.send((1, "f", 3, i), ref, ref, p.at(z=3), after=[(1, "z", 3, i)])

    along_z(0, b1)
    ff = (1 - zh) * 4 + x
    ref = mw.at[ff, c]
    net.need(("m", "z"))
    net.send(("n", "r", 0), ref.at[top], ref.at[top], p.at(x=1))
    net.send(("n", "l", 1), ref.at[low], ref.at[low], p.at(x=3))
    net.send(("n", "r", 1), ref.at[low], ref.at[low], p.at(x=1))
    net.send(("n", "l", 0), ref.at[top], ref.at[top], p.at(x=3))
    net.need(("c", "z"))
    net.send(("c", "p", 1), cg.at[tp_], cg.at[tp_], p.at(y=1))
    net.send(("c", "p", 3), cg.at[tp_], cg.at[tp_], p.at(y=3))
    for i in (1, 3, 2):
        ff = zh * 4 + (x + 4 - i) % 4
        net.need((1, "x", i))
        along_z((4 - i) % 4, w1.at[ff, c, :, s1])
    on_z(0)
    net.need((2, "x", 1), (2, "x", 2), (2, "x", 3))
    own_2.wait()
    own_zh = pl.ds(zh * 4, 4)
    other_zh = pl.ds((1 - zh) * 4, 4)
    ref = w2.at[own_zh, c, :, s2]
    net.send((2, "m"), ref, ref, p.mirror())
    net.need(("g", "x", 1), ("g", "x", 2), ("g", "x", 3))
    own_g.wait()
    net.send(("g", "m"), gn.at[own_zh, c], gn.at[own_zh, c], p.mirror())
    net.send((2, "y", 1), ref, ref, p.at(y=1))
    net.send((2, "y", 3), ref, ref, p.at(y=3))
    def m_on(tag, ff_of):
        ref = mw.at[ff_of((x + 3) % 4), c, top]
        net.send((tag, "f", 1), ref, ref, p.at(x=1), after=[(tag, "r", 0)])
        ref = mw.at[ff_of((x + 1) % 4), c, low]
        net.send((tag, "f", 3), ref, ref, p.at(x=3), after=[(tag, "l", 1)])

    m_on("m", lambda xx: zh * 4 + xx)
    ref = cg.at[((y + 3) % 4) * 2 + zl, ctop]
    net.send(("c", "f", 1), ref, ref, p.at(y=1), after=[("c", "r", 0)])
    ref = cg.at[((y + 1) % 4) * 2 + zl, clow]
    net.send(("c", "f", 3), ref, ref, p.at(y=3), after=[("c", "l", 1)])
    for i in (3, 1, 2):
        on_z(i)
    ref = w2.at[other_zh, c, :, s2]
    net.need((2, "m"))
    net.send((2, "o", 1), ref, ref, p.at(y=1))
    net.send((2, "o", 3), ref, ref, p.at(y=3))
    ref = cg.at[((y + 2) % 4) * 2 + zl]
    net.send(("c", "o"), ref, ref, zp, after=[("c", "f", 1), ("c", "f", 3)])
    m_on("n", lambda xx: (1 - zh) * 4 + xx)
    for k, part in (("y", own_zh), ("o", other_zh)):
        ref = w2.at[part, c, top, lanes((y + 3) % 4, 384)]
        net.send((2, k, "f", 1), ref, ref, p.at(y=1), after=[(2, k, 1)])
        ref = w2.at[part, c, low, lanes((y + 1) % 4, 384)]
        net.send((2, k, "f", 3), ref, ref, p.at(y=3), after=[(2, k, 3)])
    sib = p.at(c=1)
    own_1.wait()

    def core_1(k, dz, after):
        zz = (z + dz) % 4
        ref = w1.at[pl.ds((zz // 2) * 4, 4), c, :, lanes(zz % 2, 1024)]
        net.send((1, "c", k), ref, ref, sib, after=after)

    xs = range(4)
    core_1(0, 0, [(1, "x", 1), (1, "x", 2), (1, "x", 3)])
    core_1(1, 3, [(1, "z", 1, i) for i in xs])
    core_1(2, 1, [(1, "z", 3, i) for i in xs])

    def core_m(k, ff, after):
        net.send(("m", "c", k), mw.at[ff, c], mw.at[ff, c], sib, after=after)

    core_m(0, (1 - zh) * 4 + x, [])
    core_m(1, zh * 4 + (x + 3) % 4, [("m", "r", 0), ("m", "r", 1)])
    core_m(2, zh * 4 + (x + 1) % 4, [("m", "l", 0), ("m", "l", 1)])

    def core_2(k, yy, after):
        ref = w2.at[:, c, :, lanes(yy, 384)]
        net.send((2, "c", k), ref, ref, sib, after=after)

    core_2(0, y, [])
    net.send(("g", "c"), gn.at[:, c], gn.at[:, c], sib, after=[("g", "m")])
    core_2(1, (y + 3) % 4, [(2, "y", 1), (2, "o", 1)])
    core_2(2, (y + 1) % 4, [(2, "y", 3), (2, "o", 3)])
    core_m(3, zh * 4 + (x + 2) % 4, [("m", "f", 1), ("m", "f", 3)])
    core_1(3, 2, [(1, "f", 1, i) for i in xs] + [(1, "f", 3, i) for i in xs])
    core_2(3, (y + 2) % 4, [(2, "y", "f", 1), (2, "y", "f", 3), (2, "o", "f", 1), (2, "o", "f", 3)])
    core_m(4, (1 - zh) * 4 + (x + 3) % 4, [("n", "r", 0), ("n", "r", 1)])
    core_m(5, (1 - zh) * 4 + (x + 1) % 4, [("n", "l", 0), ("n", "l", 1)])
    core_m(6, (1 - zh) * 4 + (x + 2) % 4, [("n", "f", 1), ("n", "f", 3)])
    net.finish()
    own_m.wait()
    own_c.wait()


def gather_start(a_in, m_in, c_in):
    n = 82
    vm = pl.BlockSpec(memory_space=pltpu.VMEM)
    hbm = pl.BlockSpec(memory_space=pl.ANY)
    return pl.pallas_call(
        gather_start_kernel,
        out_shape=(
            jax.ShapeDtypeStruct((8, 2, 96, 2048), BF),
            jax.ShapeDtypeStruct((8, 2, 96, 1536), BF),
            jax.ShapeDtypeStruct((8, 2, 96, 3456), BF),
            jax.ShapeDtypeStruct((8, 128, 1536), BF),
            jax.ShapeDtypeStruct((8, 2, 96, 128), BF),
        ),
        in_specs=[vm, hbm, hbm],
        out_specs=(hbm,) * 5,
        scratch_shapes=[
            pltpu.VMEM((8, 16, 3712), BF),
            pltpu.VMEM((96, 3712), F32),
            pltpu.VMEM((96, 3712), BF),
            pltpu.SemaphoreType.DMA((n,)),
            pltpu.SemaphoreType.DMA((n,)),
            pltpu.SemaphoreType.DMA((5,)),
        ],
        name="gather_start",
        compiler_params=pltpu.CompilerParams(
            collective_id=0, has_side_effects=True, vmem_limit_bytes=40 << 20
        ),
    )(a_in, m_in, c_in)


def each(n, body):
    def step(i, carry):
        body(i)
        return carry

    lax.fori_loop(0, n, step, 0)


def add_rows(dst, first, others, rows, step=16):
    def body(i):
        at = pl.ds(pl.multiple_of(i * step, step), step)
        total = first[at, :].astype(F32)
        for other in others:
            total += other[at, :].astype(F32)
        dst[at, :] = total.astype(dst.dtype)

    each(rows // step, body)


def in_turn(flows):
    flows = list(flows)
    while flows:
        flows = [flow for flow in flows if next(flow, "end") != "end"]


def tp_gather_flow(net, p, tag, own, out, rows):
    y, zl, t = p.y, p.zl, p.t
    tq = y * 2 + 1 - zl
    zp = p.partner()
    top, low = pl.ds(0, rows // 2), pl.ds(rows // 2, rows // 2)
    net.send((tag, "z"), own, out.at[t], zp)
    net.send((tag, "r", 0), own.at[top], out.at[t, top], p.at(y=1))
    net.send((tag, "l", 1), own.at[low], out.at[t, low], p.at(y=3))
    net.send((tag, "r", 1), own.at[low], out.at[t, low], p.at(y=1))
    net.send((tag, "l", 0), own.at[top], out.at[t, top], p.at(y=3))
    yield
    net.need((tag, "z"))
    net.send((tag, "p", 1), out.at[tq], out.at[tq], p.at(y=1))
    net.send((tag, "p", 3), out.at[tq], out.at[tq], p.at(y=3))
    yield
    ref = out.at[((y + 3) % 4) * 2 + zl, top]
    net.send((tag, "f", 1), ref, ref, p.at(y=1), after=[(tag, "r", 0)])
    ref = out.at[((y + 1) % 4) * 2 + zl, low]
    net.send((tag, "f", 3), ref, ref, p.at(y=3), after=[(tag, "l", 1)])
    yield
    ref = out.at[((y + 2) % 4) * 2 + zl]
    net.send((tag, "o"), ref, ref, zp, after=[(tag, "f", 1), (tag, "f", 3)])


def tp_gather_kernel(own, out, send_sems, recv_sems, local_sem):
    p = Place()
    greet([p.partner(), p.at(y=1), p.at(y=3)])
    net = Net(send_sems, recv_sems)
    copy = pltpu.make_async_copy(own, out.at[p.t], local_sem)
    copy.start()
    in_turn([tp_gather_flow(net, p, "g", own, out, own.shape[0])])
    net.finish()
    copy.wait()


def tp_gather(value, cid, name):
    rows, width = value.shape
    hbm = pl.BlockSpec(memory_space=pl.ANY)
    return pl.pallas_call(
        tp_gather_kernel,
        out_shape=jax.ShapeDtypeStruct((8, rows, width), value.dtype),
        in_specs=[hbm],
        out_specs=hbm,
        scratch_shapes=[
            pltpu.SemaphoreType.DMA((10,)),
            pltpu.SemaphoreType.DMA((10,)),
            pltpu.SemaphoreType.DMA,
        ],
        name=name,
        compiler_params=pltpu.CompilerParams(collective_id=cid, has_side_effects=True),
    )(value)


def tp_sum_flow(net, p, tag, part, out, bufs, chunks):
    ro, rp1, rp3, rh1, rh3, rw1, rw3, rq, sb, sq, s1, s3 = bufs
    y, zl, t = p.y, p.zl, p.t
    zp = p.partner()
    rows, width = out.shape
    half = rows // 2
    top, low = pl.ds(0, half), pl.ds(half, half)
    w = width // chunks
    cols = [(k, pl.ds(k * w, w)) for k in range(chunks)]

    def mine(i):
        return part.at[((y + i) % 4) * 2 + zl]

    def theirs(i):
        return part.at[((y + i) % 4) * 2 + 1 - zl]

    for k, at in cols:
        net.send((tag, "o", k), theirs(2).at[:, at], ro.at[:, at], zp)
    for k, at in cols:
        net.send((tag, "p", 1, k), theirs(1).at[:, at], rp1.at[:, at], p.at(y=1))
        net.send((tag, "p", 3, k), theirs(3).at[:, at], rp3.at[:, at], p.at(y=3))
    yield
    for k, at in cols:
        net.need((tag, "o", k))
        add_rows(sb.at[:, at], mine(2).at[:, at], [ro.at[:, at]], rows)
        net.send((tag, "h", 1, k), sb.at[low, at], rh1.at[:, at], p.at(y=1))
        net.send((tag, "h", 3, k), sb.at[top, at], rh3.at[:, at], p.at(y=3))
    yield
    for k, at in cols:
        net.need((tag, "p", 1, k), (tag, "p", 3, k))
        add_rows(sq.at[:, at], theirs(0).at[:, at], [rp1.at[:, at], rp3.at[:, at]], rows)
        net.send((tag, "q", k), sq.at[:, at], rq.at[:, at], zp)
    yield
    for k, at in cols:
        net.need((tag, "h", 1, k))
        s1[top, at] = mine(1)[top, at]
        add_rows(s1.at[low, at], mine(1).at[low, at], [rh1.at[:, at]], half)
        net.send((tag, "w", 1, k), s1.at[:, at], rw1.at[:, at], p.at(y=1))
        net.need((tag, "h", 3, k))
        s3[low, at] = mine(3)[low, at]
        add_rows(s3.at[top, at], mine(3).at[top, at], [rh3.at[:, at]], half)
        net.send((tag, "w", 3, k), s3.at[:, at], rw3.at[:, at], p.at(y=3))
    yield
    for k, at in cols:
        net.need((tag, "q", k), (tag, "w", 1, k), (tag, "w", 3, k))
        add_rows(
            out.at[:, at], mine(0).at[:, at], [rq.at[:, at], rw1.at[:, at], rw3.at[:, at]], rows
        )


def tp_sum_kernel(n, chunks, *refs):
    parts, outs, rest = refs[:n], refs[n : 2 * n], refs[2 * n :]
    bufs, (send_sems, recv_sems) = rest[: 12 * n], rest[12 * n :]
    p = Place()
    greet([p.partner(), p.at(y=1), p.at(y=3)])
    net = Net(send_sems, recv_sems)
    in_turn(
        [
            tp_sum_flow(net, p, ("s", i), parts[i], outs[i], bufs[12 * i : 12 * i + 12], chunks)
            for i in range(n)
        ]
    )
    net.finish()


def tp_sum(parts, cid, name, chunks):
    n = len(parts)
    vm = pl.BlockSpec(memory_space=pltpu.VMEM)
    scratch = []
    for a in parts:
        _, rows, width = a.shape
        whole, half = pltpu.VMEM((rows, width), BF), pltpu.VMEM((rows // 2, width), BF)
        scratch += [whole] * 3 + [half] * 2 + [whole] * 7
    sems = 8 * chunks * n
    return pl.pallas_call(
        functools.partial(tp_sum_kernel, n, chunks),
        out_shape=tuple(jax.ShapeDtypeStruct(a.shape[1:], F32) for a in parts),
        in_specs=[vm] * n,
        out_specs=(vm,) * n,
        scratch_shapes=scratch
        + [pltpu.SemaphoreType.DMA((sems,)), pltpu.SemaphoreType.DMA((sems,))],
        name=name,
        compiler_params=pltpu.CompilerParams(
            collective_id=cid, has_side_effects=True, vmem_limit_bytes=40 << 20
        ),
    )(*parts)


def weight_flow(net, p, tag, g, acc, rc, rh1, rh3, rw1, rw3, rz, out, local):
    x, zh, c = p.x, p.zh, p.c
    sib = p.at(c=1)
    top, low = pl.ds(0, 48), pl.ds(48, 48)
    sides = (("o", 1 - zh), ("s", zh))
    own = pltpu.make_async_copy(g.at[:, c], acc, local)
    own.start()

    def at(i, side):
        return side * 4 + (x + i) % 4

    for i in (2, 3, 1, 0):
        for s, side in sides:
            b = at(i, side)
            net.send((tag, "c", i, s), g.at[b, 1 - c], rc.at[b], sib)
    own.wait()
    yield
    for k, (s, side) in enumerate(sides):
        b = at(2, side)
        net.need((tag, "c", 2, s))
        add_rows(acc.at[b], acc.at[b], [rc.at[b]], 96)
        net.send((tag, "h", 1, s), acc.at[b, low], rh1.at[k], p.at(x=1))
        net.send((tag, "h", 3, s), acc.at[b, top], rh3.at[k], p.at(x=3))
        yield
    for k, (s, side) in enumerate(sides):
        b = at(1, side)
        net.need((tag, "c", 1, s))
        add_rows(acc.at[b], acc.at[b], [rc.at[b]], 96)
        net.need((tag, "h", 1, s))
        add_rows(acc.at[b, low], acc.at[b, low], [rh1.at[k]], 48)
        net.send((tag, "w", 1, s), acc.at[b], rw1.at[k], p.at(x=1))
        b = at(3, side)
        net.need((tag, "c", 3, s))
        add_rows(acc.at[b], acc.at[b], [rc.at[b]], 96)
        net.need((tag, "h", 3, s))
        add_rows(acc.at[b, top], acc.at[b, top], [rh3.at[k]], 48)
        net.send((tag, "w", 3, s), acc.at[b], rw3.at[k], p.at(x=3))
        yield
    b = at(0, 1 - zh)
    net.need((tag, "c", 0, "o"), (tag, "w", 1, "o"), (tag, "w", 3, "o"))
    add_rows(acc.at[b], acc.at[b], [rc.at[b], rw1.at[0], rw3.at[0]], 96)
    net.send((tag, "z"), acc.at[b], rz, p.at(z=2))
    yield
    b = at(0, zh)
    net.need((tag, "c", 0, "s"), (tag, "w", 1, "s"), (tag, "w", 3, "s"), (tag, "z"))
    add_rows(out, acc.at[b], [rc.at[b], rw1.at[1], rw3.at[1], rz], 96)


def attn_flow(net, p, tag, g, acc, rc, rh1, rh3, rw1, rw3, ring, block, count, width, local):
    c = p.c
    sib = p.at(c=1)
    top, low = pl.ds(0, 48), pl.ds(48, 48)
    own = pltpu.make_async_copy(g.at[:, c], acc, local)
    own.start()

    def view(ref, i):
        first, cols = block(i)
        return ref.at[pl.ds(first, count), :, cols]

    for i in (2, 3, 1, 0):
        first, cols = block(i)
        net.send(
            (tag, "c", i), g.at[pl.ds(first, count), 1 - c, :, cols], view(rc, i), sib
        )
    own.wait()
    yield

    def add(dst, others, rows, skip=0):
        def body(i):
            def one(k):
                at = pl.ds(pl.multiple_of(k * 16, 16), 16)
                to = pl.ds(pl.multiple_of(k * 16 + skip, 16), 16)
                total = dst[i, to, :].astype(F32)
                for other in others:
                    total += other[i, at, :].astype(F32)
                dst[i, to, :] = total.astype(BF)

            each(rows // 16, one)

        each(count, body)

    b = view(acc, 2)
    net.need((tag, "c", 2))
    add(b, [view(rc, 2)], 96)
    net.send((tag, "h", 1), b.at[:, low], rh1, ring(1))
    net.send((tag, "h", 3), b.at[:, top], rh3, ring(3))
    yield
    b = view(acc, 1)
    net.need((tag, "c", 1))
    add(b, [view(rc, 1)], 96)
    net.need((tag, "h", 1))
    add(b, [rh1], 48, 48)
    net.send((tag, "w", 1), b, rw1, ring(1))
    b = view(acc, 3)
    net.need((tag, "c", 3))
    add(b, [view(rc, 3)], 96)
    net.need((tag, "h", 3))
    add(b, [rh3], 48, 0)
    net.send((tag, "w", 3), b, rw3, ring(3))
    yield
    b = view(acc, 0)
    net.need((tag, "c", 0), (tag, "w", 1), (tag, "w", 3))
    add(b, [view(rc, 0), rw1, rw3], 96)
    yield


def after_x(net, p, tag, src, rx, total):
    x = p.x
    for i in (1, 3, 2):
        net.send((tag, "x", i), src.at[(x + i) % 4], rx.at[i - 1], p.at(x=i))
    yield
    net.need((tag, "x", 1), (tag, "x", 2), (tag, "x", 3))
    add_rows(total, src.at[x], [rx.at[0], rx.at[1], rx.at[2]], 96)


def qkv_flow(net, p, g, acc, rc, rh1, rh3, rw1, rw3, rx, total, local):
    def block(i):
        zz = (p.z + i) % 4
        return (zz // 2) * 4, lanes(zz % 2, 1024)

    yield from attn_flow(
        net, p, "1", g, acc, rc, rh1, rh3, rw1, rw3, lambda i: p.at(z=i), block, 4, 1024, local
    )
    src = acc.at[pl.ds(p.zh * 4, 4), :, lanes(p.zl, 1024)]
    yield from after_x(net, p, "1", src, rx, total)


def out_flow(net, p, g, acc, rc, rh1, rh3, rw1, rw3, rm, rx, total, local):
    def block(i):
        return 0, lanes((p.y + i) % 4, 384)

    yield from attn_flow(
        net, p, "2", g, acc, rc, rh1, rh3, rw1, rw3, lambda i: p.at(y=i), block, 8, 384, local
    )
    cols = lanes(p.y, 384)
    net.send((2, "m"), acc.at[pl.ds((1 - p.zh) * 4, 4), :, cols], rm, p.mirror())
    yield
    net.need((2, "m"))
    src = acc.at[pl.ds(p.zh * 4, 4), :, cols]

    def body(i):
        add_rows(src.at[i], src.at[i], [rm.at[i]], 96)

    each(4, body)
    yield from after_x(net, p, "2", src, rx, total)


def small_flow(net, p, src, out, rc, rings):
    net.send(("t", "c"), src, rc, p.at(c=1))
    yield
    net.need(("t", "c"))
    out[...] = src[...] + rc[...]
    for k, (ring, place) in enumerate(zip(rings, (p.x, p.y, p.z))):
        ring[place] = out[...]
        for i in (1, 3, 2):
            step = {"xyz"[k]: i}
            net.send(("t", k, i), ring.at[place], ring.at[place], p.at(**step))
        yield
        net.need(("t", k, 1), ("t", k, 2), ("t", k, 3))
        out[...] = ring[0] + ring[1] + ring[2] + ring[3]


def owner_sum_kernel(
    g1, g2, ga, gb, small, o1, o2, oa, ob, os, *rest
):
    (
        acc1, rc1, h11, h13, w11, w13, rx1, tot1,
        acc2, rc2, h21, h23, w21, w23, rm2, rx2, tot2,
        acca, rca, ha1, ha3, wa1, wa3, rza,
        accb, rcb, hb1, hb3, wb1, wb3, rzb,
        pads, fins, rcs, rs1, rs2, rs3, send_sems, recv_sems, local_sems,
    ) = rest
    p = Place()
    t = p.t
    tp_all = [{FS: p.f, CX: p.c, TP: (t + i) % 8} for i in range(1, 8)]
    greet(
        [p.at(c=1)]
        + [p.at(x=i) for i in (1, 2, 3)]
        + tp_all
        + [p.mirror(), p.at(z=2)]
    )
    net = Net(send_sems, recv_sems)

    def attention():
        yield from in_step(
            qkv_flow(net, p, g1, acc1, rc1, h11, h13, w11, w13, rx1, tot1, local_sems.at[0]),
            out_flow(net, p, g2, acc2, rc2, h21, h23, w21, w23, rm2, rx2, tot2, local_sems.at[1]),
        )
        for i in range(8):
            rows = pl.ds(12 * i, 12)
            pads[i, pl.ds(0, 12), pl.ds(0, 1024)] = tot1[rows, :].astype(BF)
            pads[i, pl.ds(0, 12), pl.ds(1024, 384)] = tot2[rows, :].astype(BF)
            pads[i, pl.ds(12, 4), :] = jnp.zeros((4, 1408), BF)
        for i in range(1, 8):
            net.send(("f", i), pads.at[(t + i) % 8], fins.at[t], tp_all[i - 1])
        fins[t] = pads[t]
        yield

    in_turn(
        [
            attention(),
            weight_flow(net, p, "a", ga, acca, rca, ha1, ha3, wa1, wa3, rza, oa, local_sems.at[2]),
            small_flow(net, p, small, os, rcs, (rs1, rs2, rs3)),
            weight_flow(net, p, "b", gb, accb, rcb, hb1, hb3, wb1, wb3, rzb, ob, local_sems.at[3]),
        ]
    )
    net.need(*[("f", i) for i in range(1, 8)])
    for k in range(2):
        total = fins[k, :, pl.ds(0, 1024)].astype(F32)
        for yy in range(1, 4):
            total += fins[2 * yy + k, :, pl.ds(0, 1024)].astype(F32)
        o1[:, pl.ds(1024 * k, 1024)] = total
    for yy in range(4):
        total = fins[2 * yy, :, pl.ds(1024, 384)].astype(F32)
        total += fins[2 * yy + 1, :, pl.ds(1024, 384)].astype(F32)
        o2[:, pl.ds(384 * yy, 384)] = total
    net.finish()


def in_step(*flows):
    flows = list(flows)
    while flows:
        flows = [flow for flow in flows if next(flow, "end") != "end"]
        yield


def owner_sum(g1, g2, ga, gb, small, cid=1, name="owner_sum"):
    vm = pl.BlockSpec(memory_space=pltpu.VMEM)
    hbm = pl.BlockSpec(memory_space=pl.ANY)
    V = lambda *s: pltpu.VMEM(s, BF)
    scratch = [
        V(8, 96, 2048), V(8, 96, 2048),
        V(4, 48, 1024), V(4, 48, 1024), V(4, 96, 1024), V(4, 96, 1024), V(3, 96, 1024),
        pltpu.VMEM((96, 1024), F32),
        V(8, 96, 1536), V(8, 96, 1536),
        V(8, 48, 384), V(8, 48, 384), V(8, 96, 384), V(8, 96, 384), V(4, 96, 384), V(3, 96, 384),
        pltpu.VMEM((96, 384), F32),
    ]
    for w in (ga.shape[-1], gb.shape[-1]):
        scratch += [
            V(8, 96, w), V(8, 96, w), V(2, 48, w), V(2, 48, w), V(2, 96, w), V(2, 96, w), V(96, w),
        ]
    scratch += [V(8, 16, 1408), V(8, 16, 1408)]
    tiny = small.shape
    scratch += [pltpu.VMEM(tiny, F32)] + [pltpu.VMEM((4, *tiny), F32)] * 3
    n = 90
    scratch += [
        pltpu.SemaphoreType.DMA((n,)), pltpu.SemaphoreType.DMA((n,)), pltpu.SemaphoreType.DMA((4,)),
    ]
    S = lambda *s: jax.ShapeDtypeStruct(s, F32)
    return pl.pallas_call(
        owner_sum_kernel,
        out_shape=(S(16, 2048), S(16, 1536), S(96, ga.shape[-1]), S(96, gb.shape[-1]), S(*tiny)),
        in_specs=[hbm] * 4 + [vm],
        out_specs=(vm,) * 5,
        scratch_shapes=scratch,
        name=name,
        compiler_params=pltpu.CompilerParams(
            collective_id=cid, has_side_effects=True, vmem_limit_bytes=56 << 20
        ),
    )(g1, g2, ga, gb, small)


def rms_scale(values):
    return lax.rsqrt(jnp.mean(values * values, axis=-1, keepdims=True) + norm_eps)


def doc_layout(lengths, places):
    ends = jnp.cumsum(lengths)
    starts = ends - lengths
    doc_ids = jnp.sum((ends[None, :] <= places[:, None]).astype(jnp.int32), axis=1)
    doc_start = jnp.max(jnp.where(starts[None, :] <= places[:, None], starts[None, :], 0), axis=1)
    return (doc_ids, places - doc_start)


def angles(position, size):
    half = size // 2
    freq = jnp.exp(jnp.arange(half, dtype=jnp.float32) * (-2.0 * math.log(rope_base) / size))
    angle = position.astype(jnp.float32)[:, None] * freq[None, :]
    return (jnp.cos(angle), jnp.sin(angle))


def apply_rotation(values, cosine_table, sine_table):
    half = values.shape[-1] // 2
    front = values[..., :half]
    back = values[..., half:]
    return jnp.concatenate(
        [front * cosine_table - back * sine_table, back * cosine_table + front * sine_table],
        axis=-1,
    )


def norm_back(grad_norm, values, scale, gain):
    scaled = grad_norm * gain
    grad_gain = jnp.sum(grad_norm * values * scale, axis=0)
    value_gradients = scale * scaled - values * scale * scale * scale * jnp.mean(
        scaled * values, axis=-1, keepdims=True
    )
    return (value_gradients, grad_gain)


def adam_step(weight, moment, second, grad, rate, decay):
    moment = beta_one * moment + (1.0 - beta_one) * grad
    second = beta_two * second + (1.0 - beta_two) * grad * grad
    fix_one = 1.0 - beta_one**STEP
    fix_two = 1.0 - beta_two**STEP
    direction = moment / fix_one / (jnp.sqrt(second / fix_two) + adam_eps)
    return (weight - rate * (direction + decay * weight), moment, second)


def matmul(left, right, left_dim, right_dim):
    return lax.dot_general(
        left, right, (((left_dim,), (right_dim,)), ((), ())), preferred_element_type=F32
    )


def on_device(
    hidden_in,
    cotangent,
    seq_lengths,
    w_qkv,
    m_qkv,
    v_qkv,
    b_qkv,
    m_bias,
    v_bias,
    w_out,
    m_out,
    v_out,
    w_gate_up,
    m_gate_up,
    v_gate_up,
    w_down,
    m_down,
    v_down,
    gains,
    m_gains,
    v_gains,
):
    token_rows = hidden_in.shape[0]
    model_width = hidden_in.shape[1]
    tp_count = lax.axis_size(TP)
    packed_length = token_rows * tp_count
    queries_per_group = QUERY_HEADS // KEY_VALUE_HEADS
    query_columns = QUERY_HEADS * HEAD_SIZE
    key_columns = (QUERY_HEADS + KEY_VALUE_HEADS) * HEAD_SIZE
    score_scale = HEAD_SIZE ** (-0.5)
    ff_dev = w_gate_up.shape[2]
    own_places = lax.axis_index(TP) * token_rows + jnp.arange(token_rows, dtype=jnp.int32)
    key_places = jnp.arange(packed_length, dtype=jnp.int32)
    own_docs, own_pos = doc_layout(seq_lengths[0], own_places)
    key_docs = doc_layout(seq_lengths[0], key_places)[0]
    allowed = (own_docs[:, None] == key_docs[None, :]) & (
        key_places[None, :] <= own_places[:, None]
    )
    cosine_table, sine_table = angles(own_pos, HEAD_SIZE)
    cosine_table = cosine_table[:, None, :]
    sine_table = sine_table[:, None, :]
    attn_shard = jnp.concatenate(
        [w_qkv.astype(BF), w_out.astype(BF).T, gains.astype(BF).T], axis=1
    )
    attn_shard = jnp.pad(attn_shard, ((0, 4), (0, 126)))
    side = ((0, 0), (0, FF_PAD - ff_dev))
    mlp_shard = jnp.concatenate(
        [
            jnp.pad(w_gate_up[:, 0].astype(BF), side),
            jnp.pad(w_gate_up[:, 1].astype(BF), side),
            jnp.pad(w_down.astype(BF).T, side),
        ],
        axis=1,
    )
    qkv_full, out_turned, mlp_full, grad_group, gains_tile = gather_start(
        attn_shard, mlp_shard, cotangent
    )
    gains_full = gains_tile.reshape(model_width, -1)[:, :2].astype(F32).T
    qkv_full = qkv_full.reshape(model_width, -1)
    out_turned = out_turned.reshape(model_width, -1)
    mlp_full = mlp_full.reshape(model_width, -1)
    gate_up_full, down_turned = mlp_full[:, : 2 * FF_PAD], mlp_full[:, 2 * FF_PAD :]
    grad_group = grad_group.reshape(packed_length, model_width)
    bias_full = b_qkv.astype(BF)
    inputs = hidden_in.astype(F32)
    scale_one = rms_scale(inputs)
    normed_one = (inputs * scale_one * gains_full[0]).astype(BF)
    projected_rows = matmul(normed_one, qkv_full, 1, 0) + bias_full.astype(F32)
    query_rows = apply_rotation(
        projected_rows[:, :query_columns].reshape(token_rows, QUERY_HEADS, HEAD_SIZE),
        cosine_table,
        sine_table,
    ).astype(BF)
    local_keys = apply_rotation(
        projected_rows[:, query_columns:key_columns].reshape(
            token_rows, KEY_VALUE_HEADS, HEAD_SIZE
        ),
        cosine_table,
        sine_table,
    ).astype(BF)
    values_own = projected_rows[:, key_columns:].astype(BF)
    kv_columns = KEY_VALUE_HEADS * HEAD_SIZE
    keys_values = tp_gather(
        jnp.concatenate([local_keys.reshape(token_rows, kv_columns), values_own], axis=1),
        2,
        "keys_values",
    ).reshape(packed_length, 2 * kv_columns)
    heads_of_queries = query_rows.reshape(token_rows, KEY_VALUE_HEADS, queries_per_group, HEAD_SIZE)
    heads_of_keys = keys_values[:, :kv_columns].reshape(packed_length, KEY_VALUE_HEADS, HEAD_SIZE)
    heads_of_values = keys_values[:, kv_columns:].reshape(
        packed_length, KEY_VALUE_HEADS, HEAD_SIZE
    )

    def masked_scores():
        raw = (
            jnp.einsum(
                "qkgd,jkd->kgqj",
                heads_of_queries,
                heads_of_keys,
                preferred_element_type=F32,
            )
            * score_scale
        )
        return jnp.where(allowed, raw, -1e30)

    scores = masked_scores()
    row_top = jnp.max(scores, axis=-1, keepdims=True)
    exp_scores = jnp.exp(scores - row_top)
    row_total = jnp.sum(exp_scores, axis=-1, keepdims=True)
    log_total = row_top + jnp.log(row_total)
    probs = (exp_scores / row_total).astype(BF)
    attended = jnp.einsum("kgqj,jkd->qkgd", probs, heads_of_values, preferred_element_type=F32)
    attended = attended.reshape(token_rows, query_columns).astype(BF)
    middle = inputs + matmul(attended, out_turned, 1, 1)
    scale_two = rms_scale(middle)
    normed_two = (middle * scale_two * gains_full[1]).astype(BF)
    normed_group = tp_gather(normed_two, 3, "normed_two").reshape(packed_length, model_width)
    gate_up = matmul(normed_group, gate_up_full, 1, 0)
    gate, up_part = gate_up[:, :FF_PAD], gate_up[:, FF_PAD:]
    sigma = jax.nn.sigmoid(gate)
    activated = gate * sigma
    hidden = (activated * up_part).astype(BF)
    grad_hidden = matmul(grad_group, down_turned, 1, 0)
    grad_gate = (grad_hidden * up_part * sigma * (1.0 + gate * (1.0 - sigma))).astype(BF)
    grad_up = (grad_hidden * activated).astype(BF)
    grad_gate_up = jnp.concatenate([grad_gate, grad_up], axis=1)
    blocks = (tp_count, token_rows, model_width)
    (grad_normed_two,) = tp_sum(
        [matmul(grad_gate_up, gate_up_full, 1, 1).astype(BF).reshape(blocks)],
        4,
        "grad_normed_two",
        2,
    )
    (down_sum,) = tp_sum(
        [matmul(hidden, down_turned, 1, 1).astype(BF).reshape(blocks)], 5, "hidden_out", 2
    )
    hidden_out = middle + down_sum
    grad_w_gate_up = matmul(normed_group, grad_gate_up, 0, 0).astype(BF)
    grad_w_down = matmul(grad_group, hidden, 0, 0).astype(BF)
    grad_two, grad_gain_two = norm_back(grad_normed_two, middle, scale_two, gains_full[1])
    grad_middle = cotangent.astype(F32) + grad_two
    grad_proj = grad_middle.astype(BF)
    attention_gradient = matmul(grad_proj, out_turned, 1, 0).astype(BF)
    head_gradients = attention_gradient.reshape(
        token_rows, KEY_VALUE_HEADS, queries_per_group, HEAD_SIZE
    )
    probs_full = jnp.exp(masked_scores() - log_total)
    grad_probs = jnp.einsum(
        "qkgd,jkd->kgqj", head_gradients, heads_of_values, preferred_element_type=F32
    )
    grad_scores = (
        probs_full * (grad_probs - jnp.sum(probs_full * grad_probs, axis=-1, keepdims=True))
    ).astype(BF)
    value_gradients = jnp.einsum(
        "kgqj,qkgd->jkd", probs, head_gradients, preferred_element_type=F32
    )
    grad_queries = (
        jnp.einsum("kgqj,jkd->qkgd", grad_scores, heads_of_keys, preferred_element_type=F32)
        * score_scale
    )
    key_gradients = (
        jnp.einsum("kgqj,qkgd->jkd", grad_scores, heads_of_queries, preferred_element_type=F32)
        * score_scale
    )
    (grad_keys_values,) = tp_sum(
        [
            jnp.concatenate(
                [
                    key_gradients.reshape(packed_length, kv_columns),
                    value_gradients.reshape(packed_length, kv_columns),
                ],
                axis=1,
            )
            .astype(BF)
            .reshape(tp_count, token_rows, 2 * kv_columns)
        ],
        6,
        "grad_keys_values",
        1,
    )
    back_queries = apply_rotation(
        grad_queries.reshape(token_rows, QUERY_HEADS, HEAD_SIZE), cosine_table, -sine_table
    ).reshape(token_rows, query_columns)
    key_pullback = apply_rotation(
        grad_keys_values[:, :kv_columns].reshape(token_rows, KEY_VALUE_HEADS, HEAD_SIZE),
        cosine_table,
        -sine_table,
    ).reshape(token_rows, kv_columns)
    grad_qkv = jnp.concatenate(
        [back_queries, key_pullback, grad_keys_values[:, kv_columns:]], axis=1
    ).astype(BF)
    grad_bias = jnp.sum(grad_qkv.astype(F32), axis=0)
    grad_normed_one = matmul(grad_qkv, qkv_full, 1, 1)
    grad_one, grad_gain_one = norm_back(grad_normed_one, inputs, scale_one, gains_full[0])
    grad_in = grad_middle + grad_one
    small = jnp.concatenate([grad_bias, grad_gain_one, grad_gain_two]).reshape(-1, 128)
    grad_w_qkv = matmul(normed_one, grad_qkv, 0, 0).astype(BF)
    grad_w_out = matmul(grad_proj, attended, 0, 0).astype(BF)
    owned_qkv, owned_out, owned_gate_up, owned_down, small = owner_sum(
        grad_w_qkv.reshape(8, 2, 96, -1),
        grad_w_out.reshape(8, 2, 96, -1),
        grad_w_gate_up.reshape(8, 2, 96, -1),
        grad_w_down.reshape(8, 2, 96, -1),
        small,
    )
    small = small.reshape(-1)
    summed_bias = small[: grad_bias.shape[0]]
    summed_gains = small[grad_bias.shape[0] :].reshape(2, model_width)
    own_gains = gains.shape[1]
    owned_gains = lax.dynamic_slice_in_dim(
        summed_gains, lax.axis_index(ALL) * own_gains, own_gains, axis=1
    )
    own_rows = w_qkv.shape[0]
    owned_qkv = owned_qkv[:own_rows]
    owned_out = owned_out[:own_rows].T
    owned_gate_up = jnp.stack(
        [owned_gate_up[:, :ff_dev], owned_gate_up[:, FF_PAD : FF_PAD + ff_dev]], axis=1
    )
    owned_down = owned_down[:, :ff_dev].T
    qkv_new, qkv_moment, qkv_second = adam_step(
        w_qkv, m_qkv, v_qkv, owned_qkv, rate_qkv, weight_decay
    )
    bias_new, bias_moment, bias_second = adam_step(
        b_qkv, m_bias, v_bias, summed_bias, rate_small, 0.0
    )
    out_new, out_moment, out_second = adam_step(
        w_out, m_out, v_out, owned_out, rate_out, weight_decay
    )
    gate_up_new, gate_up_moment, gate_up_second = adam_step(
        w_gate_up, m_gate_up, v_gate_up, owned_gate_up, rate_gate_up, weight_decay
    )
    down_new, down_moment, down_second = adam_step(
        w_down, m_down, v_down, owned_down, rate_down, weight_decay
    )
    gains_new, gains_moment, gains_second = adam_step(
        gains, m_gains, v_gains, owned_gains, rate_small, 0.0
    )
    return (
        hidden_out,
        grad_in,
        qkv_new,
        qkv_moment,
        qkv_second,
        bias_new,
        bias_moment,
        bias_second,
        out_new,
        out_moment,
        out_second,
        gate_up_new,
        gate_up_moment,
        gate_up_second,
        down_new,
        down_moment,
        down_second,
        gains_new,
        gains_moment,
        gains_second,
    )


def solution(mesh):
    placed = (
        P((FS, CX, TP), None),
        P((FS, CX, TP), None),
        P((FS, CX), None),
        P((FS, CX, TP), None),
        P((FS, CX, TP), None),
        P((FS, CX, TP), None),
        P(),
        P(),
        P(),
        P(None, (FS, CX, TP)),
        P(None, (FS, CX, TP)),
        P(None, (FS, CX, TP)),
        P((FS, CX), None, TP),
        P((FS, CX), None, TP),
        P((FS, CX), None, TP),
        P(TP, (FS, CX)),
        P(TP, (FS, CX)),
        P(TP, (FS, CX)),
        P(None, (FS, CX, TP)),
        P(None, (FS, CX, TP)),
        P(None, (FS, CX, TP)),
    )
    return jax.shard_map(
        on_device,
        mesh=mesh,
        in_specs=placed,
        out_specs=(
            P((FS, CX, TP), None),
            P((FS, CX, TP), None),
            P((FS, CX, TP), None),
            P((FS, CX, TP), None),
            P((FS, CX, TP), None),
            P(),
            P(),
            P(),
            P(None, (FS, CX, TP)),
            P(None, (FS, CX, TP)),
            P(None, (FS, CX, TP)),
            P((FS, CX), None, TP),
            P((FS, CX), None, TP),
            P((FS, CX), None, TP),
            P(TP, (FS, CX)),
            P(TP, (FS, CX)),
            P(TP, (FS, CX)),
            P(None, (FS, CX, TP)),
            P(None, (FS, CX, TP)),
            P(None, (FS, CX, TP)),
        ),
        check_vma=False,
    )
```

```python
import functools
import math

import jax
import jax.numpy as jnp
from jax import lax
from jax.experimental import pallas as pl
from jax.experimental.pallas import tpu as pltpu
from jax.sharding import PartitionSpec as P

QUERY_HEADS = 12
KEY_VALUE_HEADS = 2
HEAD_SIZE = 128
STEP = 10


norm_eps = 1e-06
rope_base = 1000000.0
beta_one = 0.9
beta_two = 0.95
adam_eps = 1e-08
weight_decay = 0.1
rate_qkv = 0.05
rate_out = 0.3
rate_gate_up = 0.05
rate_down = 0.02
rate_small = 0.5

BF = jnp.bfloat16
F32 = jnp.float32
FS, CX, TP = ALL = ("fsdp", "ctx", "tp")
FF_PAD = 1152


class Place:
    def __init__(self):
        self.f = lax.axis_index(FS)
        self.c = lax.axis_index(CX)
        self.t = lax.axis_index(TP)
        self.zh, self.x = self.f // 4, self.f % 4
        self.y, self.zl = self.t // 2, self.t % 2
        self.z = self.zh * 2 + self.zl

    def at(self, x=0, y=0, z=0, c=0):
        zz = (self.z + z) % 4
        return {
            FS: (zz // 2) * 4 + (self.x + x) % 4,
            CX: (self.c + c) % 2,
            TP: ((self.y + y) % 4) * 2 + zz % 2,
        }

    def partner(self):
        return {FS: self.f, CX: self.c, TP: self.y * 2 + 1 - self.zl}

    def mirror(self):
        return {
            FS: (1 - self.zh) * 4 + self.x,
            CX: self.c,
            TP: self.y * 2 + 1 - self.zl,
        }


def greet(devices):
    barrier = pltpu.get_barrier_semaphore()
    for device in devices:
        pl.semaphore_signal(barrier, inc=1, device_id=device, device_id_type=pl.DeviceIdType.MESH)
    pl.semaphore_wait(barrier, len(devices))


class Net:
    def __init__(self, send_sems, recv_sems):
        self.send_sems, self.recv_sems = send_sems, recv_sems
        self.copies, self.arrived = {}, set()

    def send(self, name, src, dst, device, after=()):
        self.need(*after)
        at = len(self.copies)
        copy = pltpu.make_async_remote_copy(
            src_ref=src,
            dst_ref=dst,
            send_sem=self.send_sems.at[at],
            recv_sem=self.recv_sems.at[at],
            device_id=device,
            device_id_type=pl.DeviceIdType.MESH,
        )
        copy.start()
        self.copies[name] = copy

    def need(self, *names):
        for name in names:
            if name not in self.arrived:
                self.arrived.add(name)
                self.copies[name].wait_recv()

    def finish(self):
        self.need(*self.copies)
        for copy in self.copies.values():
            copy.wait_send()


def lanes(at, size):
    return pl.ds(pl.multiple_of(at * size, 128), size)


def gather_start_kernel(a_in, m_in, c_in, w1, w2, mw, cg, gn, pad, wide, blk, send_sems, recv_sems, local_sems):
    p = Place()
    f, c, t, x, y, z, zl, zh = p.f, p.c, p.t, p.x, p.y, p.z, p.zl, p.zh
    R, L = dict(x=1), dict(x=3)
    greet(
        [p.at(c=1)]
        + [p.at(x=i) for i in (1, 2, 3)]
        + [p.at(y=i) for i in (1, 2, 3)]
        + [p.at(z=i) for i in (1, 2, 3)]
    )
    net = Net(send_sems, recv_sems)
    zp = p.partner()
    tp_ = y * 2 + 1 - zl
    net.send(("a", "z"), a_in, pad.at[t], zp)
    for i in (1, 3, 2):
        net.send(("a", "y", i), a_in, pad.at[t], p.at(y=i))
    own_m = pltpu.make_async_copy(m_in, mw.at[f, c], local_sems.at[0])
    own_c = pltpu.make_async_copy(c_in, cg.at[t], local_sems.at[1])
    own_m.start()
    own_c.start()
    pad[t] = a_in[...]
    top, low = pl.ds(0, 48), pl.ds(48, 48)
    net.send(("m", "z"), m_in, mw.at[f, c], p.at(z=2))
    net.send(("m", "r", 0), m_in.at[top], mw.at[f, c, top], p.at(x=1))
    net.send(("m", "l", 1), m_in.at[low], mw.at[f, c, low], p.at(x=3))
    net.send(("m", "r", 1), m_in.at[low], mw.at[f, c, low], p.at(x=1))
    net.send(("m", "l", 0), m_in.at[top], mw.at[f, c, top], p.at(x=3))
    net.send(("m", "c"), m_in, mw.at[f, c], p.at(c=1))
    for i in (1, 3, 2):
        net.send(("a", "p", i), pad.at[tp_], pad.at[tp_], p.at(y=i), after=[("a", "z")])
    ctop, clow = pl.ds(0, 64), pl.ds(64, 64)
    net.send(("c", "z"), c_in, cg.at[t], zp)
    net.send(("c", "r", 0), c_in.at[ctop], cg.at[t, ctop], p.at(y=1))
    net.send(("c", "l", 1), c_in.at[clow], cg.at[t, clow], p.at(y=3))
    net.send(("c", "r", 1), c_in.at[clow], cg.at[t, clow], p.at(y=1))
    net.send(("c", "l", 0), c_in.at[ctop], cg.at[t, ctop], p.at(y=3))
    net.need(("a", "y", 1), ("a", "y", 2), ("a", "y", 3), ("a", "p", 1), ("a", "p", 2), ("a", "p", 3))
    for i in range(8):
        wide[pl.ds(12 * i, 12), :] = pad[i, pl.ds(0, 12), :].astype(F32)
    blk[...] = wide[...].astype(BF)
    s1 = lanes(zl, 1024)
    s2 = lanes(y, 384)
    b1 = blk.at[:, s1]
    b2 = blk.at[:, pl.ds(pl.multiple_of(2048 + y * 384, 128), 384)]
    own_1 = pltpu.make_async_copy(b1, w1.at[f, c, :, s1], local_sems.at[2])
    own_2 = pltpu.make_async_copy(b2, w2.at[f, c, :, s2], local_sems.at[3])
    bg = blk.at[:, pl.ds(3584, 128)]
    own_g = pltpu.make_async_copy(bg, gn.at[f, c], local_sems.at[4])
    own_1.start()
    own_2.start()
    own_g.start()
    for i in (1, 3, 2):
        net.send((1, "x", i), b1, w1.at[f, c, :, s1], p.at(x=i))
    for i in (1, 3, 2):
        net.send((2, "x", i), b2, w2.at[f, c, :, s2], p.at(x=i))
    for i in (1, 3, 2):
        net.send(("g", "x", i), bg, gn.at[f, c], p.at(x=i))
    def along_z(i, src):
        ff = zh * 4 + (x + i) % 4
        net.send((1, "z", 1, i), src, w1.at[ff, c, :, s1], p.at(z=1))
        net.send((1, "z", 3, i), src, w1.at[ff, c, :, s1], p.at(z=3))

    def on_z(i):
        zz = (z + 3) % 4
        ff = (zz // 2) * 4 + (x + i) % 4
        ref = w1.at[ff, c, top, lanes(zz % 2, 1024)]
        net.send((1, "f", 1, i), ref, ref, p.at(z=1), after=[(1, "z", 1, i)])
        zz = (z + 1) % 4
        ff = (zz // 2) * 4 + (x + i) % 4
        ref = w1.at[ff, c, low, lanes(zz % 2, 1024)]
        net.send((1, "f", 3, i), ref, ref, p.at(z=3), after=[(1, "z", 3, i)])

    along_z(0, b1)
    ff = (1 - zh) * 4 + x
    ref = mw.at[ff, c]
    net.need(("m", "z"))
    net.send(("n", "r", 0), ref.at[top], ref.at[top], p.at(x=1))
    net.send(("n", "l", 1), ref.at[low], ref.at[low], p.at(x=3))
    net.send(("n", "r", 1), ref.at[low], ref.at[low], p.at(x=1))
    net.send(("n", "l", 0), ref.at[top], ref.at[top], p.at(x=3))
    net.need(("c", "z"))
    net.send(("c", "p", 1), cg.at[tp_], cg.at[tp_], p.at(y=1))
    net.send(("c", "p", 3), cg.at[tp_], cg.at[tp_], p.at(y=3))
    for i in (1, 3, 2):
        ff = zh * 4 + (x + 4 - i) % 4
        net.need((1, "x", i))
        along_z((4 - i) % 4, w1.at[ff, c, :, s1])
    on_z(0)
    net.need((2, "x", 1), (2, "x", 2), (2, "x", 3))
    own_2.wait()
    own_zh = pl.ds(zh * 4, 4)
    other_zh = pl.ds((1 - zh) * 4, 4)
    ref = w2.at[own_zh, c, :, s2]
    net.send((2, "m"), ref, ref, p.mirror())
    net.need(("g", "x", 1), ("g", "x", 2), ("g", "x", 3))
    own_g.wait()
    net.send(("g", "m"), gn.at[own_zh, c], gn.at[own_zh, c], p.mirror())
    net.send((2, "y", 1), ref, ref, p.at(y=1))
    net.send((2, "y", 3), ref, ref, p.at(y=3))
    def m_on(tag, ff_of):
        ref = mw.at[ff_of((x + 3) % 4), c, top]
        net.send((tag, "f", 1), ref, ref, p.at(x=1), after=[(tag, "r", 0)])
        ref = mw.at[ff_of((x + 1) % 4), c, low]
        net.send((tag, "f", 3), ref, ref, p.at(x=3), after=[(tag, "l", 1)])

    m_on("m", lambda xx: zh * 4 + xx)
    ref = cg.at[((y + 3) % 4) * 2 + zl, ctop]
    net.send(("c", "f", 1), ref, ref, p.at(y=1), after=[("c", "r", 0)])
    ref = cg.at[((y + 1) % 4) * 2 + zl, clow]
    net.send(("c", "f", 3), ref, ref, p.at(y=3), after=[("c", "l", 1)])
    for i in (3, 1, 2):
        on_z(i)
    ref = w2.at[other_zh, c, :, s2]
    net.need((2, "m"))
    net.send((2, "o", 1), ref, ref, p.at(y=1))
    net.send((2, "o", 3), ref, ref, p.at(y=3))
    ref = cg.at[((y + 2) % 4) * 2 + zl]
    net.send(("c", "o"), ref, ref, zp, after=[("c", "f", 1), ("c", "f", 3)])
    m_on("n", lambda xx: (1 - zh) * 4 + xx)
    for k, part in (("y", own_zh), ("o", other_zh)):
        ref = w2.at[part, c, top, lanes((y + 3) % 4, 384)]
        net.send((2, k, "f", 1), ref, ref, p.at(y=1), after=[(2, k, 1)])
        ref = w2.at[part, c, low, lanes((y + 1) % 4, 384)]
        net.send((2, k, "f", 3), ref, ref, p.at(y=3), after=[(2, k, 3)])
    sib = p.at(c=1)
    own_1.wait()

    def core_1(k, dz, after):
        zz = (z + dz) % 4
        ref = w1.at[pl.ds((zz // 2) * 4, 4), c, :, lanes(zz % 2, 1024)]
        net.send((1, "c", k), ref, ref, sib, after=after)

    xs = range(4)
    core_1(0, 0, [(1, "x", 1), (1, "x", 2), (1, "x", 3)])
    core_1(1, 3, [(1, "z", 1, i) for i in xs])
    core_1(2, 1, [(1, "z", 3, i) for i in xs])

    def core_m(k, ff, after):
        net.send(("m", "c", k), mw.at[ff, c], mw.at[ff, c], sib, after=after)

    core_m(0, (1 - zh) * 4 + x, [])
    core_m(1, zh * 4 + (x + 3) % 4, [("m", "r", 0), ("m", "r", 1)])
    core_m(2, zh * 4 + (x + 1) % 4, [("m", "l", 0), ("m", "l", 1)])

    def core_2(k, yy, after):
        ref = w2.at[:, c, :, lanes(yy, 384)]
        net.send((2, "c", k), ref, ref, sib, after=after)

    core_2(0, y, [])
    net.send(("g", "c"), gn.at[:, c], gn.at[:, c], sib, after=[("g", "m")])
    core_2(1, (y + 3) % 4, [(2, "y", 1), (2, "o", 1)])
    core_2(2, (y + 1) % 4, [(2, "y", 3), (2, "o", 3)])
    core_m(3, zh * 4 + (x + 2) % 4, [("m", "f", 1), ("m", "f", 3)])
    core_1(3, 2, [(1, "f", 1, i) for i in xs] + [(1, "f", 3, i) for i in xs])
    core_2(3, (y + 2) % 4, [(2, "y", "f", 1), (2, "y", "f", 3), (2, "o", "f", 1), (2, "o", "f", 3)])
    core_m(4, (1 - zh) * 4 + (x + 3) % 4, [("n", "r", 0), ("n", "r", 1)])
    core_m(5, (1 - zh) * 4 + (x + 1) % 4, [("n", "l", 0), ("n", "l", 1)])
    core_m(6, (1 - zh) * 4 + (x + 2) % 4, [("n", "f", 1), ("n", "f", 3)])
    net.finish()
    own_m.wait()
    own_c.wait()


def gather_start(a_in, m_in, c_in):
    n = 82
    vm = pl.BlockSpec(memory_space=pltpu.VMEM)
    hbm = pl.BlockSpec(memory_space=pl.ANY)
    return pl.pallas_call(
        gather_start_kernel,
        out_shape=(
            jax.ShapeDtypeStruct((8, 2, 96, 2048), BF),
            jax.ShapeDtypeStruct((8, 2, 96, 1536), BF),
            jax.ShapeDtypeStruct((8, 2, 96, 3456), BF),
            jax.ShapeDtypeStruct((8, 128, 1536), BF),
            jax.ShapeDtypeStruct((8, 2, 96, 128), BF),
        ),
        in_specs=[vm, hbm, hbm],
        out_specs=(hbm,) * 5,
        scratch_shapes=[
            pltpu.VMEM((8, 16, 3712), BF),
            pltpu.VMEM((96, 3712), F32),
            pltpu.VMEM((96, 3712), BF),
            pltpu.SemaphoreType.DMA((n,)),
            pltpu.SemaphoreType.DMA((n,)),
            pltpu.SemaphoreType.DMA((5,)),
        ],
        name="gather_start",
        compiler_params=pltpu.CompilerParams(
            collective_id=0, has_side_effects=True, vmem_limit_bytes=40 << 20
        ),
    )(a_in, m_in, c_in)


def each(n, body):
    def step(i, carry):
        body(i)
        return carry

    lax.fori_loop(0, n, step, 0)


def add_rows(dst, first, others, rows, step=16):
    def body(i):
        at = pl.ds(pl.multiple_of(i * step, step), step)
        total = first[at, :].astype(F32)
        for other in others:
            total += other[at, :].astype(F32)
        dst[at, :] = total.astype(dst.dtype)

    each(rows // step, body)


def advance(flow):
    next(flow, None)


def in_turn(flows):
    flows = list(flows)
    while flows:
        flows = [flow for flow in flows if next(flow, "end") != "end"]


def tp_gather_flow(net, p, tag, own, out, rows):
    y, zl, t = p.y, p.zl, p.t
    tq = y * 2 + 1 - zl
    zp = p.partner()
    top, low = pl.ds(0, rows // 2), pl.ds(rows // 2, rows // 2)
    net.send((tag, "z"), own, out.at[t], zp)
    net.send((tag, "r", 0), own.at[top], out.at[t, top], p.at(y=1))
    net.send((tag, "l", 1), own.at[low], out.at[t, low], p.at(y=3))
    net.send((tag, "r", 1), own.at[low], out.at[t, low], p.at(y=1))
    net.send((tag, "l", 0), own.at[top], out.at[t, top], p.at(y=3))
    yield
    net.need((tag, "z"))
    net.send((tag, "p", 1), out.at[tq], out.at[tq], p.at(y=1))
    net.send((tag, "p", 3), out.at[tq], out.at[tq], p.at(y=3))
    yield
    ref = out.at[((y + 3) % 4) * 2 + zl, top]
    net.send((tag, "f", 1), ref, ref, p.at(y=1), after=[(tag, "r", 0)])
    ref = out.at[((y + 1) % 4) * 2 + zl, low]
    net.send((tag, "f", 3), ref, ref, p.at(y=3), after=[(tag, "l", 1)])
    yield
    ref = out.at[((y + 2) % 4) * 2 + zl]
    net.send((tag, "o"), ref, ref, zp, after=[(tag, "f", 1), (tag, "f", 3)])


def tp_gather_kernel(own, out, send_sems, recv_sems, local_sem):
    p = Place()
    greet([p.partner(), p.at(y=1), p.at(y=3)])
    net = Net(send_sems, recv_sems)
    copy = pltpu.make_async_copy(own, out.at[p.t], local_sem)
    copy.start()
    in_turn([tp_gather_flow(net, p, "g", own, out, own.shape[0])])
    net.finish()
    copy.wait()


def tp_gather(value, cid, name):
    rows, width = value.shape
    hbm = pl.BlockSpec(memory_space=pl.ANY)
    return pl.pallas_call(
        tp_gather_kernel,
        out_shape=jax.ShapeDtypeStruct((8, rows, width), value.dtype),
        in_specs=[hbm],
        out_specs=hbm,
        scratch_shapes=[
            pltpu.SemaphoreType.DMA((10,)),
            pltpu.SemaphoreType.DMA((10,)),
            pltpu.SemaphoreType.DMA,
        ],
        name=name,
        compiler_params=pltpu.CompilerParams(collective_id=cid, has_side_effects=True),
    )(value)


def sum_side(net, p, tag, part, bufs, cols, i):
    src = part.at[((p.y + i) % 4) * 2 + 1 - p.zl]
    dst = bufs[1 if i == 1 else 2]
    for k, at in cols:
        net.send((tag, "p", i, k), src.at[:, at], dst.at[:, at], p.at(y=i))


def split_cols(width, chunks):
    w = width // chunks
    return [(k, pl.ds(k * w, w)) for k in range(chunks)]


def tp_sum_flow(net, p, tag, part, out, bufs, chunks, sent=False, loads=None, base=None):
    ro, rp1, rp3, rh1, rh3, rw1, rw3, rq, sb, sq, s1, s3 = bufs
    y, zl, t = p.y, p.zl, p.t
    zp = p.partner()
    rows, width = out.shape
    half = rows // 2
    top, low = pl.ds(0, half), pl.ds(half, half)
    cols = split_cols(width, chunks)

    def mine(i):
        return part.at[((y + i) % 4) * 2 + zl]

    def theirs(i):
        return part.at[((y + i) % 4) * 2 + 1 - zl]

    far, cross, right, left, own = mine(2), theirs(0), mine(1), mine(3), mine(0)
    copies = []
    if loads is not None:
        wanted = zip((far, cross, right, left, own), (sb, sq, s1, s3, loads[0]))
        copies = [
            pltpu.make_async_copy(src, dst, loads[1].at[i]) for i, (src, dst) in enumerate(wanted)
        ]
        far, cross, right, left, own = sb, sq, s1, s3, loads[0]
    for copy in copies:
        copy.start()
    for k, at in cols:
        net.send((tag, "o", k), theirs(2).at[:, at], ro.at[:, at], zp)
    if not sent:
        for i in (1, 3):
            sum_side(net, p, tag, part, bufs, cols, i)
    for copy in copies:
        copy.wait()
    yield
    for k, at in cols:
        net.need((tag, "o", k))
        add_rows(sb.at[:, at], far.at[:, at], [ro.at[:, at]], rows)
        net.send((tag, "h", 1, k), sb.at[low, at], rh1.at[:, at], p.at(y=1))
        net.send((tag, "h", 3, k), sb.at[top, at], rh3.at[:, at], p.at(y=3))
    yield
    for k, at in cols:
        net.need((tag, "p", 1, k), (tag, "p", 3, k))
        add_rows(sq.at[:, at], cross.at[:, at], [rp1.at[:, at], rp3.at[:, at]], rows)
        net.send((tag, "q", k), sq.at[:, at], rq.at[:, at], zp)
    yield
    for k, at in cols:
        net.need((tag, "h", 1, k))
        if loads is None:
            s1[top, at] = right[top, at]
            s3[low, at] = left[low, at]
        add_rows(s1.at[low, at], right.at[low, at], [rh1.at[:, at]], half)
        net.send((tag, "w", 1, k), s1.at[:, at], rw1.at[:, at], p.at(y=1))
        net.need((tag, "h", 3, k))
        add_rows(s3.at[top, at], left.at[top, at], [rh3.at[:, at]], half)
        net.send((tag, "w", 3, k), s3.at[:, at], rw3.at[:, at], p.at(y=3))
    yield
    for k, at in cols:
        net.need((tag, "q", k), (tag, "w", 1, k), (tag, "w", 3, k))
        others = [rq.at[:, at], rw1.at[:, at], rw3.at[:, at]]
        if base is not None:
            others.append(base.at[:, at])
        add_rows(out.at[:, at], own.at[:, at], others, rows)


def dots(left, right, left_dim, right_dim):
    return lax.dot_general(
        left, right, (((left_dim,), (right_dim,)), ((), ())), preferred_element_type=F32
    )


def feed_forward_kernel(
    own, cot, weights, gn, hp, dgu, dd, xs, gu, gh, hid, ggu, part, *rest
):
    bufs, (send_sems, recv_sems, local_sem) = rest[:12], rest[12:]
    p = Place()
    y, zl = p.y, p.zl
    greet([p.partner(), p.at(y=1), p.at(y=3)])
    net = Net(send_sems, recv_sems)
    copy = pltpu.make_async_copy(own, xs.at[p.t], local_sem)
    copy.start()
    gather = tp_gather_flow(net, p, "g", own, xs, own.shape[0])
    summed = tp_sum_flow(net, p, "s", part, gn, bufs, 2, sent=True)
    cols = split_cols(gn.shape[1], 2)
    advance(gather)
    gate_up_at, down_at = pl.ds(0, 2 * FF_PAD), pl.ds(2 * FF_PAD, FF_PAD)

    def grad_hidden(i):
        at = pl.ds(i * 2, 2)
        gh[pl.ds(pl.multiple_of(i * 256, 256), 256), :] = dots(
            cot[at].reshape(256, -1), weights[:, down_at], 1, 0
        )

    each(4, grad_hidden)
    advance(gather)
    advance(gather)
    copy.wait()

    def pair(i):
        column = (y + i) % 4
        blocks = pl.ds(column * 2, 2)
        first = column * 256

        def products(j):
            at = pl.ds(pl.multiple_of(j * 768, 128), 768)
            gu[:, at] = dots(xs[blocks].reshape(256, -1), weights[:, at], 1, 0)

        each(3, products)

        def gates(j):
            at = pl.ds(pl.multiple_of(j * 16, 16), 16)
            to = pl.ds(pl.multiple_of(first + j * 16, 16), 16)
            gate, up = gu[at, pl.ds(0, FF_PAD)], gu[at, pl.ds(FF_PAD, FF_PAD)]
            grad = gh[to, :]
            sigma = jax.nn.sigmoid(gate)
            activated = gate * sigma
            hid[to, :] = (activated * up).astype(BF)
            ggu[to, pl.ds(0, FF_PAD)] = (
                grad * up * sigma * (1.0 + gate * (1.0 - sigma))
            ).astype(BF)
            ggu[to, pl.ds(FF_PAD, FF_PAD)] = (grad * activated).astype(BF)

        each(16, gates)
        rows = pl.ds(pl.multiple_of(first, 256), 256)

        def back(j):
            at = pl.ds(pl.multiple_of(j * 512, 512), 512)
            total = dots(ggu[rows, :], weights[at, gate_up_at], 1, 1)
            part[blocks, :, at] = total.astype(BF).reshape(2, 128, 512)

        each(3, back)

    pair(0)
    advance(gather)
    net.need(("g", "r", 0), ("g", "r", 1), ("g", "p", 1))
    pair(3)
    sum_side(net, p, "s", part, bufs, cols, 3)
    net.need(("g", "l", 0), ("g", "l", 1), ("g", "p", 3))
    pair(1)
    sum_side(net, p, "s", part, bufs, cols, 1)
    net.need(("g", "o"))
    pair(2)
    advance(summed)

    def hidden_out(j):
        at = pl.ds(pl.multiple_of(j * 512, 512), 512)
        total = dots(hid[...], weights[at, down_at], 1, 1)
        hp[:, :, at] = total.astype(BF).reshape(8, 128, 512)

    each(3, hidden_out)
    advance(summed)
    advance(summed)

    def grad_down(j):
        at = pl.ds(pl.multiple_of(j * 512, 512), 512)
        dd[at, :] = dots(cot[:, :, at].reshape(1024, 512), hid[...], 0, 0).astype(BF)

    each(3, grad_down)
    advance(summed)

    def grad_gate_up(j):
        at = pl.ds(pl.multiple_of(j * 512, 512), 512)

        def columns(k):
            to = pl.ds(pl.multiple_of(k * 768, 128), 768)
            dgu[at, to] = dots(xs[:, :, at].reshape(1024, 512), ggu[:, to], 0, 0).astype(BF)

        each(3, columns)

    each(3, grad_gate_up)
    advance(summed)
    net.finish()


def feed_forward(own, cot, weights, cid=3, name="feed_forward"):
    vm = pl.BlockSpec(memory_space=pltpu.VMEM)
    hbm = pl.BlockSpec(memory_space=pl.ANY)
    rows, width = own.shape
    V = lambda *s: pltpu.VMEM(s, BF)
    whole, half = V(rows, width), V(rows // 2, width)
    B = lambda *s: jax.ShapeDtypeStruct(s, BF)
    n = 30
    return pl.pallas_call(
        feed_forward_kernel,
        out_shape=(
            jax.ShapeDtypeStruct((rows, width), F32),
            B(8, rows, width),
            B(width, 2 * FF_PAD),
            B(width, FF_PAD),
        ),
        in_specs=[vm] * 3,
        out_specs=(vm,) * 4,
        scratch_shapes=[
            V(8, rows, width),
            pltpu.VMEM((256, 2 * FF_PAD), F32),
            pltpu.VMEM((1024, FF_PAD), F32),
            V(1024, FF_PAD),
            V(1024, 2 * FF_PAD),
            V(8, rows, width),
        ]
        + [whole] * 3
        + [half] * 2
        + [whole] * 7
        + [
            pltpu.SemaphoreType.DMA((n,)),
            pltpu.SemaphoreType.DMA((n,)),
            pltpu.SemaphoreType.DMA,
        ],
        name=name,
        compiler_params=pltpu.CompilerParams(
            collective_id=cid, has_side_effects=True, vmem_limit_bytes=60 << 20
        ),
    )(own, cot, weights)


def weight_flow(net, p, tag, g, acc, rc, rh1, rh3, rw1, rw3, rz, out, local):
    x, zh, c = p.x, p.zh, p.c
    sib = p.at(c=1)
    top, low = pl.ds(0, 48), pl.ds(48, 48)
    sides = (("o", 1 - zh), ("s", zh))
    own = pltpu.make_async_copy(g.at[:, c], acc, local)
    own.start()

    def at(i, side):
        return side * 4 + (x + i) % 4

    for i in (2, 3, 1, 0):
        for s, side in sides:
            b = at(i, side)
            net.send((tag, "c", i, s), g.at[b, 1 - c], rc.at[b], sib)
    own.wait()
    yield
    for k, (s, side) in enumerate(sides):
        b = at(2, side)
        net.need((tag, "c", 2, s))
        add_rows(acc.at[b], acc.at[b], [rc.at[b]], 96)
        net.send((tag, "h", 1, s), acc.at[b, low], rh1.at[k], p.at(x=1))
        net.send((tag, "h", 3, s), acc.at[b, top], rh3.at[k], p.at(x=3))
    yield
    for s, side in sides:
        for i in (1, 3):
            b = at(i, side)
            net.need((tag, "c", i, s))
            add_rows(acc.at[b], acc.at[b], [rc.at[b]], 96)
    yield
    for k, (s, side) in enumerate(sides):
        b = at(1, side)
        net.need((tag, "h", 1, s))
        add_rows(acc.at[b, low], acc.at[b, low], [rh1.at[k]], 48)
        net.send((tag, "w", 1, s), acc.at[b], rw1.at[k], p.at(x=1))
        b = at(3, side)
        net.need((tag, "h", 3, s))
        add_rows(acc.at[b, top], acc.at[b, top], [rh3.at[k]], 48)
        net.send((tag, "w", 3, s), acc.at[b], rw3.at[k], p.at(x=3))
        yield
    b = at(0, 1 - zh)
    net.need((tag, "c", 0, "o"), (tag, "w", 1, "o"), (tag, "w", 3, "o"))
    add_rows(acc.at[b], acc.at[b], [rc.at[b], rw1.at[0], rw3.at[0]], 96)
    net.send((tag, "z"), acc.at[b], rz, p.at(z=2))
    yield
    b = at(0, zh)
    net.need((tag, "c", 0, "s"), (tag, "w", 1, "s"), (tag, "w", 3, "s"), (tag, "z"))
    add_rows(out, acc.at[b], [rc.at[b], rw1.at[1], rw3.at[1], rz], 96)


def small_flow(net, p, src, out, rc, rings):
    net.send(("t", "c"), src, rc, p.at(c=1))
    yield
    net.need(("t", "c"))
    out[...] = src[...] + rc[...]
    for k, (ring, place) in enumerate(zip(rings, (p.x, p.y, p.z))):
        ring[place] = out[...]
        for i in (1, 3, 2):
            step = {"xyz"[k]: i}
            net.send(("t", k, i), ring.at[place], ring.at[place], p.at(**step))
        yield
        net.need(("t", k, 1), ("t", k, 2), ("t", k, 3))
        out[...] = ring[0] + ring[1] + ring[2] + ring[3]


def ring_sum_flow(net, p, tag, g, rc, rh1, rh3, rw1, rw3, ring, block, count):
    c = p.c
    sib = p.at(c=1)
    top, low = pl.ds(0, 48), pl.ds(48, 48)

    def mine(i):
        first, cols = block(i)
        return g.at[pl.ds(first, count), c, :, cols]

    def theirs(i):
        first, cols = block(i)
        return g.at[pl.ds(first, count), 1 - c, :, cols]

    def landed(i):
        first, cols = block(i)
        return rc.at[pl.ds(first, count), :, cols]

    for i in (2, 3, 1, 0):
        net.send((tag, "c", i), theirs(i), landed(i), sib)
    yield

    def add(dst, others, rows, skip=0):
        def body(i):
            def one(k):
                at = pl.ds(pl.multiple_of(k * 16, 16), 16)
                to = pl.ds(pl.multiple_of(k * 16 + skip, 16), 16)
                total = dst[i, to, :].astype(F32)
                for other in others:
                    total += other[i, at, :].astype(F32)
                dst[i, to, :] = total.astype(BF)

            each(rows // 16, one)

        each(count, body)

    b = mine(2)
    net.need((tag, "c", 2))
    add(b, [landed(2)], 96)
    net.send((tag, "h", 1), b.at[:, low], rh1, ring(1))
    net.send((tag, "h", 3), b.at[:, top], rh3, ring(3))
    yield
    for i in (1, 3):
        net.need((tag, "c", i))
        add(mine(i), [landed(i)], 96)
    yield
    for i, came, skip in ((1, rh1, 48), (3, rh3, 0)):
        net.need((tag, "h", i))
        add(mine(i), [came], 48, skip)
        net.send((tag, "w", i), mine(i), rw1 if i == 1 else rw3, ring(i))
    yield
    net.need((tag, "c", 0), (tag, "w", 1), (tag, "w", 3))
    add(mine(0), [landed(0), rw1, rw3], 96)


def along_x(net, p, tag, src, rx, total):
    x = p.x
    for i in (1, 3, 2):
        net.send((tag, "x", i), src.at[(x + i) % 4], rx.at[i - 1], p.at(x=i))
    yield
    net.need((tag, "x", 1), (tag, "x", 2), (tag, "x", 3))
    add_rows(total, src.at[x], [rx.at[0], rx.at[1], rx.at[2]], 96)


def z_flow(net, p, tag, g, bufs, total, width):
    rc, rh1, rh3, rw1, rw3, rx = bufs

    def block(i):
        zz = (p.z + i) % 4
        return (zz // 2) * 4, lanes(zz % 2, width)

    yield from ring_sum_flow(
        net, p, tag, g, rc, rh1, rh3, rw1, rw3, lambda i: p.at(z=i), block, 4
    )
    src = g.at[pl.ds(p.zh * 4, 4), p.c, :, lanes(p.zl, width)]
    yield from along_x(net, p, tag, src, rx, total)


def y_flow(net, p, tag, g, bufs, total, width, begin):
    rc, rh1, rh3, rw1, rw3, rm, rx = bufs

    def cols(i):
        return pl.ds(pl.multiple_of(begin + ((p.y + i) % 4) * width, 128), width)

    view = rc if begin == 0 else None
    yield from ring_sum_flow(
        net,
        p,
        tag,
        g.at[:, :, :, pl.ds(begin, 4 * width)] if begin else g,
        rc,
        rh1,
        rh3,
        rw1,
        rw3,
        lambda i: p.at(y=i),
        lambda i: (0, lanes((p.y + i) % 4, width)),
        8,
    )
    net.send((tag, "m"), g.at[pl.ds((1 - p.zh) * 4, 4), p.c, :, cols(0)], rm, p.mirror())
    yield
    net.need((tag, "m"))
    src = g.at[pl.ds(p.zh * 4, 4), p.c, :, cols(0)]

    def body(i):
        add_rows(src.at[i], src.at[i], [rm.at[i]], 96)

    each(4, body)
    yield from along_x(net, p, tag, src, rx, total)


def tp_scatter(net, p, tag, totals, pads, fins, to):
    t = p.t
    at = 0
    for total in totals:
        width = total.shape[1]
        for i in range(8):
            pads[i, pl.ds(0, 12), pl.ds(at, width)] = total[pl.ds(12 * i, 12), :].astype(BF)
            pads[i, pl.ds(12, 4), pl.ds(at, width)] = jnp.zeros((4, width), BF)
        at += width
    for i in range(1, 8):
        net.send((tag, "f", i), pads.at[(t + i) % 8], fins.at[t], to[i - 1])
    fins[t] = pads[t]


def norm_back_rows(grad, values, gain, base, out, grad_gain):
    grad_gain[...] = jnp.zeros_like(grad_gain)

    def body(i):
        at = pl.ds(pl.multiple_of(i * 16, 16), 16)
        v = values[at, :].astype(F32)
        g = grad[at, :]
        r = lax.rsqrt(jnp.mean(v * v, axis=-1, keepdims=True) + norm_eps)
        a = g * gain
        grad_gain[...] += jnp.sum(g * v * r, axis=0, keepdims=True)
        back = r * a - v * r * r * r * jnp.mean(a * v, axis=-1, keepdims=True)
        out[at, :] = base[at, :].astype(F32) + back

    each(grad.shape[0] // 16, body)


def backward_kernel(*refs):
    (
        ga, gb, hp, w2t, w1, probs,
        gn, middle, cot, hidden_in, normed, attended, queries, kv, cos, sin, gains,
    ) = refs[:17]
    h_out, grad_in, o1, o2, oa, ob, small = refs[17:24]
    rest = list(refs[24:])

    def take(n):
        out = rest[:n]
        del rest[:n]
        return out

    m_bufs = [take(7), take(7)]
    q_bufs, q_total = take(6), take(1)[0]
    k_bufs, k_total = take(7), take(1)[0]
    o_bufs, o_total = take(7), take(1)[0]
    hp_bufs, hp_own = take(12), take(1)[0]
    kv_bufs, kv_part, kv_sum = take(12), take(1)[0], take(1)[0]
    rcs, rs1, rs2, rs3 = take(4)
    pad_o, fin_o, pad_q, fin_q = take(4)
    wide, deep, g1, g_mid, g_proj, g_att, g_qkv, ds, stack_q, stack_a = take(10)
    gain_two, gain_one, part_small, gno = take(4)
    send_sems, recv_sems, local_sems, hp_sems = take(4)

    p = Place()
    t, c = p.t, p.c
    tp_all = [{FS: p.f, CX: p.c, TP: (t + i) % 8} for i in range(1, 8)]
    greet(
        [p.at(c=1)] + [p.at(x=i) for i in (1, 2, 3)] + tp_all + [p.mirror(), p.at(z=2)]
    )
    net = Net(send_sems, recv_sems)
    load_w2 = pltpu.make_async_copy(w2t, wide, local_sems.at[2])
    load_w2.start()
    load_p = pltpu.make_async_copy(probs, deep, local_sems.at[3])
    load_p.start()
    flow_a = weight_flow(net, p, "a", ga, *m_bufs[0], oa, local_sems.at[0])
    flow_b = weight_flow(net, p, "b", gb, *m_bufs[1], ob, local_sems.at[1])
    advance(flow_a)
    advance(flow_b)
    flow_h = tp_sum_flow(
        net, p, "h", hp, h_out, hp_bufs, 2, loads=(hp_own, hp_sems), base=middle
    )
    advance(flow_h)
    advance(flow_a)
    advance(flow_b)
    advance(flow_a)
    advance(flow_b)
    norm_back_rows(gn, middle, gains[pl.ds(1, 1), :], cot, g_mid, gain_two)
    g_proj[...] = g_mid[...].astype(BF)
    load_w2.wait()

    def grad_attended(j):
        at = pl.ds(pl.multiple_of(j * 512, 512), 512)
        g_att[:, at] = dots(g_proj[...], wide[:, at], 1, 0).astype(BF)

    each(3, grad_attended)
    g2 = wide

    def grad_out(j):
        at = pl.ds(pl.multiple_of(j * 384, 128), 384)
        g2[pl.ds(pl.multiple_of(j * 384, 128), 384), :] = dots(
            g_proj[:, at], attended[...], 0, 0
        ).astype(BF)

    each(4, grad_out)
    advance(flow_h)
    g2_blocks = g2.reshape(8, 2, 96, 1536)
    flow_o = y_flow(net, p, 2, g2_blocks, o_bufs, o_total, 384, 0)
    advance(flow_o)
    load_p.wait()
    scale = HEAD_SIZE**-0.5
    size = HEAD_SIZE
    for group in range(KEY_VALUE_HEADS):
        keys = kv.at[:, pl.ds(group * size, size)]
        values = kv.at[:, pl.ds((KEY_VALUE_HEADS + group) * size, size)]

        def head(j):
            h = group * 6 + j
            at = pl.ds(pl.multiple_of(h * size, size), size)
            rows = pl.ds(pl.multiple_of(j * size, size), size)
            grad = dots(g_att[:, at], values[...], 1, 1)
            weight = deep[at, :].astype(F32)
            inner = jnp.sum(weight * grad, axis=-1, keepdims=True)
            ds[rows, :] = (weight * (grad - inner)).astype(BF)
            back = dots(ds[rows, :], keys[...], 1, 0) * scale
            turned = back * cos[...] - pltpu.roll(back, size // 2, 1) * sin[...]
            g_qkv[:, at] = turned.astype(BF)
            stack_q[rows, :] = queries[:, at]
            stack_a[rows, :] = g_att[:, at]

        each(6, head)

        def sums(j):
            at = pl.ds(pl.multiple_of(j * 256, 256), 256)
            grad = dots(ds[:, at], stack_q[...], 0, 0) * scale
            kv_part[pl.ds(j * 2, 2), :, pl.ds(group * size, size)] = (
                grad.astype(BF).reshape(2, 128, size)
            )
            rows = pl.ds(group * 6 * size, 6 * size)
            grad = dots(deep[rows, at], stack_a[...], 0, 0)
            kv_part[pl.ds(j * 2, 2), :, pl.ds((KEY_VALUE_HEADS + group) * size, size)] = (
                grad.astype(BF).reshape(2, 128, size)
            )

        each(4, sums)
    flow_k = tp_sum_flow(net, p, "k", kv_part, kv_sum, kv_bufs, 1)
    advance(flow_k)
    load_w1 = [
        pltpu.make_async_copy(w1.at[:, pl.ds(1024 * i, 1024)], deep, local_sems.at[3 + i])
        for i in range(2)
    ]
    load_w1[0].start()

    def grad_w(at, first, count):
        def body(j):
            d = pl.ds(pl.multiple_of(j * 384, 128), 384)
            total = dots(normed[:, d], g_qkv[:, at], 0, 0)
            g1[pl.ds(j * 2, 2), :, :, at] = total.astype(BF).reshape(2, 2, 96, count)

        each(4, body)

    grad_w(pl.ds(0, 1024), 0, 1024)
    flow_q = z_flow(net, p, 1, g1, q_bufs, q_total, 512)
    advance(flow_q)
    advance(flow_o)
    advance(flow_k)
    advance(flow_q)
    advance(flow_o)
    grad_w(pl.ds(1024, 512), 1024, 512)
    advance(flow_k)
    advance(flow_h)
    advance(flow_q)
    advance(flow_a)
    advance(flow_b)
    advance(flow_k)
    advance(flow_h)
    advance(flow_o)
    advance(flow_q)
    advance(flow_k)
    for i in range(KEY_VALUE_HEADS):
        at = pl.ds(i * size, size)
        to = pl.ds((QUERY_HEADS + i) * size, size)
        back = kv_sum[:, at]
        turned = back * cos[...] - pltpu.roll(back, size // 2, 1) * sin[...]
        g_qkv[:, to] = turned.astype(BF)
    at = pl.ds((QUERY_HEADS + KEY_VALUE_HEADS) * size, KEY_VALUE_HEADS * size)
    g_qkv[:, at] = kv_sum[:, pl.ds(KEY_VALUE_HEADS * size, KEY_VALUE_HEADS * size)].astype(BF)
    grad_w(pl.ds(1536, 512), 1536, 512)
    flow_v = y_flow(net, p, 3, g1, k_bufs, k_total, 256, 1024)
    advance(flow_v)
    advance(flow_v)
    advance(flow_v)
    load_w1[0].wait()

    def normed_back(i):
        def body(j):
            at = pl.ds(pl.multiple_of(j * 512, 512), 512)
            total = dots(g_qkv[:, pl.ds(1024 * i, 1024)], deep[at, :], 1, 1)
            gno[:, at] = total if i == 0 else gno[:, at] + total

        each(3, body)

    normed_back(0)
    load_w1[1].start()
    advance(flow_a)
    advance(flow_b)
    load_w1[1].wait()
    normed_back(1)
    norm_back_rows(gno, hidden_in, gains[pl.ds(0, 1), :], g_mid, grad_in, gain_one)
    bias = jnp.sum(g_qkv[...].astype(F32), axis=0, keepdims=True)
    for i in range(16):
        part_small[pl.ds(i, 1), :] = bias[:, i * 128 : i * 128 + 128]
    for i in range(12):
        part_small[pl.ds(16 + i, 1), :] = gain_one[:, pl.ds(i * 128, 128)]
        part_small[pl.ds(28 + i, 1), :] = gain_two[:, pl.ds(i * 128, 128)]
    flow_t = small_flow(net, p, part_small, small, rcs, (rs1, rs2, rs3))
    advance(flow_t)
    advance(flow_v)
    advance(flow_o)
    advance(flow_q)
    advance(flow_t)
    advance(flow_o)
    advance(flow_o)
    tp_scatter(net, p, 2, [o_total], pad_o, fin_o, tp_all)
    advance(flow_q)
    advance(flow_t)
    advance(flow_a)
    advance(flow_b)
    advance(flow_v)
    advance(flow_h)
    advance(flow_t)
    advance(flow_a)
    advance(flow_b)
    advance(flow_v)
    advance(flow_a)
    advance(flow_b)
    advance(flow_v)
    advance(flow_t)
    tp_scatter(net, p, 1, [q_total, k_total], pad_q, fin_q, tp_all)
    for flow in (flow_a, flow_b, flow_h, flow_o, flow_k, flow_q, flow_v, flow_t):
        for _ in flow:
            pass
    for yy in range(4):
        at = pl.ds(384 * yy, 384)
        if yy == 0:
            net.need(*[(2, "f", i) for i in range(1, 8)])
        o2[:, at] = fin_o[2 * yy].astype(F32) + fin_o[2 * yy + 1].astype(F32)
    net.need(*[(1, "f", i) for i in range(1, 8)])
    for k in range(2):
        at = pl.ds(0, 512)
        total = fin_q[k, :, at].astype(F32)
        for yy in range(1, 4):
            total += fin_q[2 * yy + k, :, at].astype(F32)
        o1[:, pl.ds(512 * k, 512)] = total
    for yy in range(4):
        at = pl.ds(512, 256)
        total = fin_q[2 * yy, :, at].astype(F32) + fin_q[2 * yy + 1, :, at].astype(F32)
        o1[:, pl.ds(1024 + 256 * yy, 256)] = total
    net.finish()


def backward(far, near, cid=1, name="backward"):
    vm = pl.BlockSpec(memory_space=pltpu.VMEM)
    hbm = pl.BlockSpec(memory_space=pl.ANY)
    V = lambda *s: pltpu.VMEM(s, BF)
    W = lambda *s: pltpu.VMEM(s, F32)
    scratch = []
    for w in (far[0].shape[-1], far[1].shape[-1]):
        scratch += [
            V(8, 96, w), V(8, 96, w), V(2, 48, w), V(2, 48, w), V(2, 96, w), V(2, 96, w), V(96, w),
        ]
    scratch += [
        V(8, 96, 1024), V(4, 48, 512), V(4, 48, 512), V(4, 96, 512), V(4, 96, 512), V(3, 96, 512),
        W(96, 512),
    ]
    for w in (256, 384):
        scratch += [
            V(8, 96, 4 * w), V(8, 48, w), V(8, 48, w), V(8, 96, w), V(8, 96, w), V(4, 96, w),
            V(3, 96, w), W(96, w),
        ]
    whole, half = V(128, 1536), V(64, 1536)
    scratch += [whole] * 3 + [half] * 2 + [whole] * 7 + [whole]
    whole, half = V(128, 512), V(64, 512)
    scratch += [whole] * 3 + [half] * 2 + [whole] * 7 + [V(8, 128, 512), W(128, 512)]
    scratch += [W(40, 128)] + [W(4, 40, 128)] * 3
    scratch += [V(8, 16, 384)] * 2 + [V(8, 16, 768)] * 2
    scratch += [
        V(1536, 1536), V(1536, 1024), V(8, 2, 96, 2048), W(128, 1536), V(128, 1536), V(128, 1536),
        V(128, 2048), V(768, 1024), V(768, 128), V(768, 128),
        W(1, 1536), W(1, 1536), W(40, 128), W(128, 1536),
    ]
    n = 120
    scratch += [
        pltpu.SemaphoreType.DMA((n,)), pltpu.SemaphoreType.DMA((n,)), pltpu.SemaphoreType.DMA((6,)),
        pltpu.SemaphoreType.DMA((5,)),
    ]
    S = lambda *s: jax.ShapeDtypeStruct(s, F32)
    return pl.pallas_call(
        backward_kernel,
        out_shape=(
            S(128, 1536), S(128, 1536), S(16, 2048), S(16, 1536),
            S(96, far[0].shape[-1]), S(96, far[1].shape[-1]), S(40, 128),
        ),
        in_specs=[hbm] * len(far) + [vm] * len(near),
        out_specs=(vm,) * 7,
        scratch_shapes=scratch,
        name=name,
        compiler_params=pltpu.CompilerParams(
            collective_id=cid, has_side_effects=True, vmem_limit_bytes=62 << 20
        ),
    )(*far, *near)


def rms_scale(values):
    return lax.rsqrt(jnp.mean(values * values, axis=-1, keepdims=True) + norm_eps)


def doc_layout(lengths, places):
    ends = jnp.cumsum(lengths)
    starts = ends - lengths
    doc_ids = jnp.sum((ends[None, :] <= places[:, None]).astype(jnp.int32), axis=1)
    doc_start = jnp.max(jnp.where(starts[None, :] <= places[:, None], starts[None, :], 0), axis=1)
    return (doc_ids, places - doc_start)


def angles(position, size):
    half = size // 2
    freq = jnp.exp(jnp.arange(half, dtype=jnp.float32) * (-2.0 * math.log(rope_base) / size))
    angle = position.astype(jnp.float32)[:, None] * freq[None, :]
    return (jnp.cos(angle), jnp.sin(angle))


def apply_rotation(values, cosine_table, sine_table):
    half = values.shape[-1] // 2
    front = values[..., :half]
    back = values[..., half:]
    return jnp.concatenate(
        [front * cosine_table - back * sine_table, back * cosine_table + front * sine_table],
        axis=-1,
    )


def adam_step(weight, moment, second, grad, rate, decay):
    moment = beta_one * moment + (1.0 - beta_one) * grad
    second = beta_two * second + (1.0 - beta_two) * grad * grad
    fix_one = 1.0 - beta_one**STEP
    fix_two = 1.0 - beta_two**STEP
    direction = moment / fix_one / (jnp.sqrt(second / fix_two) + adam_eps)
    return (weight - rate * (direction + decay * weight), moment, second)


def matmul(left, right, left_dim, right_dim):
    return lax.dot_general(
        left, right, (((left_dim,), (right_dim,)), ((), ())), preferred_element_type=F32
    )


def on_device(
    hidden_in,
    cotangent,
    seq_lengths,
    w_qkv,
    m_qkv,
    v_qkv,
    b_qkv,
    m_bias,
    v_bias,
    w_out,
    m_out,
    v_out,
    w_gate_up,
    m_gate_up,
    v_gate_up,
    w_down,
    m_down,
    v_down,
    gains,
    m_gains,
    v_gains,
):
    token_rows = hidden_in.shape[0]
    model_width = hidden_in.shape[1]
    tp_count = lax.axis_size(TP)
    packed_length = token_rows * tp_count
    queries_per_group = QUERY_HEADS // KEY_VALUE_HEADS
    query_columns = QUERY_HEADS * HEAD_SIZE
    key_columns = (QUERY_HEADS + KEY_VALUE_HEADS) * HEAD_SIZE
    score_scale = HEAD_SIZE ** (-0.5)
    ff_dev = w_gate_up.shape[2]
    own_places = lax.axis_index(TP) * token_rows + jnp.arange(token_rows, dtype=jnp.int32)
    key_places = jnp.arange(packed_length, dtype=jnp.int32)
    own_docs, own_pos = doc_layout(seq_lengths[0], own_places)
    key_docs = doc_layout(seq_lengths[0], key_places)[0]
    allowed = (own_docs[:, None] == key_docs[None, :]) & (
        key_places[None, :] <= own_places[:, None]
    )
    cosine_table, sine_table = angles(own_pos, HEAD_SIZE)
    cosine_table = cosine_table[:, None, :]
    sine_table = sine_table[:, None, :]
    attn_shard = jnp.concatenate(
        [w_qkv.astype(BF), w_out.astype(BF).T, gains.astype(BF).T], axis=1
    )
    attn_shard = jnp.pad(attn_shard, ((0, 4), (0, 126)))
    side = ((0, 0), (0, FF_PAD - ff_dev))
    mlp_shard = jnp.concatenate(
        [
            jnp.pad(w_gate_up[:, 0].astype(BF), side),
            jnp.pad(w_gate_up[:, 1].astype(BF), side),
            jnp.pad(w_down.astype(BF).T, side),
        ],
        axis=1,
    )
    qkv_full, out_turned, mlp_full, grad_group, gains_tile = gather_start(
        attn_shard, mlp_shard, cotangent
    )
    gains_full = gains_tile.reshape(model_width, -1)[:, :2].astype(F32).T
    qkv_full = qkv_full.reshape(model_width, -1)
    out_turned = out_turned.reshape(model_width, -1)
    mlp_full = mlp_full.reshape(model_width, -1)
    bias_full = b_qkv.astype(BF)
    inputs = hidden_in.astype(F32)
    scale_one = rms_scale(inputs)
    normed_one = (inputs * scale_one * gains_full[0]).astype(BF)
    projected_rows = matmul(normed_one, qkv_full, 1, 0) + bias_full.astype(F32)
    query_rows = apply_rotation(
        projected_rows[:, :query_columns].reshape(token_rows, QUERY_HEADS, HEAD_SIZE),
        cosine_table,
        sine_table,
    ).astype(BF)
    local_keys = apply_rotation(
        projected_rows[:, query_columns:key_columns].reshape(
            token_rows, KEY_VALUE_HEADS, HEAD_SIZE
        ),
        cosine_table,
        sine_table,
    ).astype(BF)
    values_own = projected_rows[:, key_columns:].astype(BF)
    kv_columns = KEY_VALUE_HEADS * HEAD_SIZE
    keys_values = tp_gather(
        jnp.concatenate([local_keys.reshape(token_rows, kv_columns), values_own], axis=1),
        2,
        "keys_values",
    ).reshape(packed_length, 2 * kv_columns)
    heads_of_queries = query_rows.reshape(token_rows, KEY_VALUE_HEADS, queries_per_group, HEAD_SIZE)
    heads_of_keys = keys_values[:, :kv_columns].reshape(packed_length, KEY_VALUE_HEADS, HEAD_SIZE)
    heads_of_values = keys_values[:, kv_columns:].reshape(
        packed_length, KEY_VALUE_HEADS, HEAD_SIZE
    )

    def masked_scores():
        raw = (
            jnp.einsum(
                "qkgd,jkd->kgqj",
                heads_of_queries,
                heads_of_keys,
                preferred_element_type=F32,
            )
            * score_scale
        )
        return jnp.where(allowed, raw, -1e30)

    scores = masked_scores()
    row_top = jnp.max(scores, axis=-1, keepdims=True)
    exp_scores = jnp.exp(scores - row_top)
    row_total = jnp.sum(exp_scores, axis=-1, keepdims=True)
    probs = (exp_scores / row_total).astype(BF)
    attended = jnp.einsum("kgqj,jkd->qkgd", probs, heads_of_values, preferred_element_type=F32)
    attended = attended.reshape(token_rows, query_columns).astype(BF)
    middle = inputs + matmul(attended, out_turned, 1, 1)
    scale_two = rms_scale(middle)
    normed_two = (middle * scale_two * gains_full[1]).astype(BF)
    grad_normed_two, down_parts, grad_w_gate_up, grad_w_down = feed_forward(
        normed_two, grad_group, mlp_full
    )
    cos_row = cosine_table.reshape(token_rows, -1)
    sin_row = sine_table.reshape(token_rows, -1)
    hidden_out, grad_in, owned_qkv, owned_out, owned_gate_up, owned_down, small = backward(
        [
            grad_w_gate_up.reshape(8, 2, 96, -1),
            grad_w_down.reshape(8, 2, 96, -1),
            down_parts,
            out_turned,
            qkv_full,
            probs.reshape(QUERY_HEADS * token_rows, packed_length),
        ],
        [
            grad_normed_two,
            middle,
            cotangent,
            hidden_in,
            normed_one,
            attended,
            query_rows.reshape(token_rows, query_columns),
            keys_values,
            jnp.concatenate([cos_row, cos_row], axis=1),
            jnp.concatenate([-sin_row, sin_row], axis=1),
            gains_full,
        ],
    )
    small = small.reshape(-1)
    summed_bias = small[: b_qkv.shape[0]]
    summed_gains = small[b_qkv.shape[0] :].reshape(2, model_width)
    own_gains = gains.shape[1]
    owned_gains = lax.dynamic_slice_in_dim(
        summed_gains, lax.axis_index(ALL) * own_gains, own_gains, axis=1
    )
    own_rows = w_qkv.shape[0]
    owned_qkv = owned_qkv[:own_rows]
    owned_out = owned_out[:own_rows].T
    owned_gate_up = jnp.stack(
        [owned_gate_up[:, :ff_dev], owned_gate_up[:, FF_PAD : FF_PAD + ff_dev]], axis=1
    )
    owned_down = owned_down[:, :ff_dev].T
    qkv_new, qkv_moment, qkv_second = adam_step(
        w_qkv, m_qkv, v_qkv, owned_qkv, rate_qkv, weight_decay
    )
    bias_new, bias_moment, bias_second = adam_step(
        b_qkv, m_bias, v_bias, summed_bias, rate_small, 0.0
    )
    out_new, out_moment, out_second = adam_step(
        w_out, m_out, v_out, owned_out, rate_out, weight_decay
    )
    gate_up_new, gate_up_moment, gate_up_second = adam_step(
        w_gate_up, m_gate_up, v_gate_up, owned_gate_up, rate_gate_up, weight_decay
    )
    down_new, down_moment, down_second = adam_step(
        w_down, m_down, v_down, owned_down, rate_down, weight_decay
    )
    gains_new, gains_moment, gains_second = adam_step(
        gains, m_gains, v_gains, owned_gains, rate_small, 0.0
    )
    return (
        hidden_out,
        grad_in,
        qkv_new,
        qkv_moment,
        qkv_second,
        bias_new,
        bias_moment,
        bias_second,
        out_new,
        out_moment,
        out_second,
        gate_up_new,
        gate_up_moment,
        gate_up_second,
        down_new,
        down_moment,
        down_second,
        gains_new,
        gains_moment,
        gains_second,
    )


def solution(mesh):
    placed = (
        P((FS, CX, TP), None),
        P((FS, CX, TP), None),
        P((FS, CX), None),
        P((FS, CX, TP), None),
        P((FS, CX, TP), None),
        P((FS, CX, TP), None),
        P(),
        P(),
        P(),
        P(None, (FS, CX, TP)),
        P(None, (FS, CX, TP)),
        P(None, (FS, CX, TP)),
        P((FS, CX), None, TP),
        P((FS, CX), None, TP),
        P((FS, CX), None, TP),
        P(TP, (FS, CX)),
        P(TP, (FS, CX)),
        P(TP, (FS, CX)),
        P(None, (FS, CX, TP)),
        P(None, (FS, CX, TP)),
        P(None, (FS, CX, TP)),
    )
    return jax.shard_map(
        on_device,
        mesh=mesh,
        in_specs=placed,
        out_specs=(
            P((FS, CX, TP), None),
            P((FS, CX, TP), None),
            P((FS, CX, TP), None),
            P((FS, CX, TP), None),
            P((FS, CX, TP), None),
            P(),
            P(),
            P(),
            P(None, (FS, CX, TP)),
            P(None, (FS, CX, TP)),
            P(None, (FS, CX, TP)),
            P((FS, CX), None, TP),
            P((FS, CX), None, TP),
            P((FS, CX), None, TP),
            P(TP, (FS, CX)),
            P(TP, (FS, CX)),
            P(TP, (FS, CX)),
            P(None, (FS, CX, TP)),
            P(None, (FS, CX, TP)),
            P(None, (FS, CX, TP)),
        ),
        check_vma=False,
    )
```

```python
import functools
import math

import jax
import jax.numpy as jnp
from jax import lax
from jax.experimental import pallas as pl
from jax.experimental.pallas import tpu as pltpu
from jax.sharding import PartitionSpec as P

QUERY_HEADS = 12
KEY_VALUE_HEADS = 2
HEAD_SIZE = 128
STEP = 10


norm_eps = 1e-06
rope_base = 1000000.0
beta_one = 0.9
beta_two = 0.95
adam_eps = 1e-08
weight_decay = 0.1
rate_qkv = 0.05
rate_out = 0.3
rate_gate_up = 0.05
rate_down = 0.02
rate_small = 0.5

BF = jnp.bfloat16
F32 = jnp.float32
FS, CX, TP = ALL = ("fsdp", "ctx", "tp")
FF_PAD = 1152
FORWARD_ORDER = (
    "mm", "", "cc", "2o1mo2g", "", "", "co", "", "", "g1m2m", "", "o", "", "2", "", "g", "", "",
    "c", "m", "kkmkk", "", "11", "m", "c", "", "", "", "mom", "", "kg", "", "co2", "o", "", "m",
    "", "", "", "", "", "", "", "", "", "", "mc",
)
BACKWARD_ORDER = (
    "ah", "", "", "aoa", "", "o", "", "k", "oo", "", "qkbk", "a", "aq", "", "b", "q", "r", "",
    "", "vrqbkvor", "", "", "", "", "", "", "", "", "t", "bh", "", "o", "", "", "h", "t", "v",
    "", "", "r", "", "vhtr", "", "", "a", "q", "b", "t", "", "t", "", "", "qk", "", "h", "r",
    "", "", "", "b",
)


class Place:
    def __init__(self):
        self.f = lax.axis_index(FS)
        self.c = lax.axis_index(CX)
        self.t = lax.axis_index(TP)
        self.zh, self.x = self.f // 4, self.f % 4
        self.y, self.zl = self.t // 2, self.t % 2
        self.z = self.zh * 2 + self.zl

    def at(self, x=0, y=0, z=0, c=0):
        zz = (self.z + z) % 4
        return {
            FS: (zz // 2) * 4 + (self.x + x) % 4,
            CX: (self.c + c) % 2,
            TP: ((self.y + y) % 4) * 2 + zz % 2,
        }

    def partner(self):
        return {FS: self.f, CX: self.c, TP: self.y * 2 + 1 - self.zl}

    def mirror(self, x=0):
        return {
            FS: (1 - self.zh) * 4 + (self.x + x) % 4,
            CX: self.c,
            TP: self.y * 2 + 1 - self.zl,
        }


def greet(devices):
    barrier = pltpu.get_barrier_semaphore()
    for device in devices:
        pl.semaphore_signal(barrier, inc=1, device_id=device, device_id_type=pl.DeviceIdType.MESH)
    pl.semaphore_wait(barrier, len(devices))


class Steps:
    def __init__(self, order):
        self.flows, self.order, self.at = {}, order, 0

    def add(self, name, flow):
        self.flows[name] = flow

    def point(self):
        for name in self.order[self.at]:
            if name in self.flows:
                next(self.flows[name], None)
        self.at += 1

    def finish(self, *names):
        for name in names:
            for _ in self.flows[name]:
                pass


class Loads:
    def __init__(self, sems):
        self.sems, self.used, self.copies = sems, 0, {}

    def start(self, name, src, dst):
        copy = pltpu.make_async_copy(src, dst, self.sems.at[self.used])
        self.used += 1
        copy.start()
        self.copies[name] = copy

    def need(self, *names):
        for name in names:
            self.copies.pop(name).wait()


class Net:
    def __init__(self, send_sems, recv_sems):
        self.send_sems, self.recv_sems = send_sems, recv_sems
        self.copies, self.arrived = {}, set()

    def send(self, name, src, dst, device, after=()):
        self.need(*after)
        at = len(self.copies)
        copy = pltpu.make_async_remote_copy(
            src_ref=src,
            dst_ref=dst,
            send_sem=self.send_sems.at[at],
            recv_sem=self.recv_sems.at[at],
            device_id=device,
            device_id_type=pl.DeviceIdType.MESH,
        )
        copy.start()
        self.copies[name] = copy

    def need(self, *names):
        for name in names:
            if name not in self.arrived:
                self.arrived.add(name)
                self.copies[name].wait_recv()

    def finish(self):
        self.need(*self.copies)
        for copy in self.copies.values():
            copy.wait_send()


def lanes(at, size):
    return pl.ds(pl.multiple_of(at * size, 128), size)


def each(n, body):
    def step(i, carry):
        body(i)
        return carry

    lax.fori_loop(0, n, step, 0)


def add_rows(dst, first, others, rows):
    width = dst.shape[-1]
    step = max(k for k in range(16, rows + 1, 16) if rows % k == 0 and (k * width <= 49152 or k == 16))

    def body(i):
        at = pl.ds(pl.multiple_of(i * step, 16), step)
        if len(others) == 1 and dst.dtype == BF:
            dst[at, :] = first[at, :] + others[0][at, :]
        else:
            total = first[at, :].astype(F32)
            for other in others:
                total += other[at, :].astype(F32)
            dst[at, :] = total.astype(dst.dtype)

    if step == rows:
        body(0)
    else:
        each(rows // step, body)


def advance(*flows):
    for flow in flows:
        next(flow, None)


def tp_gather_flow(net, p, tag, own, out, rows):
    y, zl, t = p.y, p.zl, p.t
    tq = y * 2 + 1 - zl
    zp = p.partner()
    top, low = pl.ds(0, rows // 2), pl.ds(rows // 2, rows // 2)
    net.send((tag, "z"), own, out.at[t], zp)
    net.send((tag, "r", 0), own.at[top], out.at[t, top], p.at(y=1))
    net.send((tag, "l", 1), own.at[low], out.at[t, low], p.at(y=3))
    net.send((tag, "r", 1), own.at[low], out.at[t, low], p.at(y=1))
    net.send((tag, "l", 0), own.at[top], out.at[t, top], p.at(y=3))
    yield
    net.need((tag, "z"))
    net.send((tag, "p", 1), out.at[tq], out.at[tq], p.at(y=1))
    net.send((tag, "p", 3), out.at[tq], out.at[tq], p.at(y=3))
    yield
    ref = out.at[((y + 3) % 4) * 2 + zl, top]
    net.send((tag, "f", 1), ref, ref, p.at(y=1), after=[(tag, "r", 0)])
    ref = out.at[((y + 1) % 4) * 2 + zl, low]
    net.send((tag, "f", 3), ref, ref, p.at(y=3), after=[(tag, "l", 1)])
    yield
    ref = out.at[((y + 2) % 4) * 2 + zl]
    net.send((tag, "o"), ref, ref, zp, after=[(tag, "f", 1), (tag, "f", 3)])


def sum_side(net, p, tag, part, bufs, cols, i):
    src = part.at[((p.y + i) % 4) * 2 + 1 - p.zl]
    dst = bufs[1 if i == 1 else 2]
    for k, at in cols:
        net.send((tag, "p", i, k), src.at[:, at], dst.at[:, at], p.at(y=i))


def split_cols(width, chunks):
    w = width // chunks
    return [(k, pl.ds(k * w, w)) for k in range(chunks)]


def tp_sum_flow(net, p, tag, part, out, bufs, chunks, sent=False, loads=None, base=None):
    ro, rp1, rp3, rh1, rh3, rw1, rw3, rq, sb, sq, s1, s3 = bufs
    y, zl, t = p.y, p.zl, p.t
    zp = p.partner()
    rows, width = out.shape
    half = rows // 2
    top, low = pl.ds(0, half), pl.ds(half, half)
    cols = split_cols(width, chunks)

    def mine(i):
        return part.at[((y + i) % 4) * 2 + zl]

    def theirs(i):
        return part.at[((y + i) % 4) * 2 + 1 - zl]

    far, cross, right, left, own = mine(2), theirs(0), mine(1), mine(3), mine(0)
    copies = []
    if loads is not None:
        wanted = zip((far, cross, right, left, own), (sb, sq, s1, s3, loads[0]))
        copies = [
            pltpu.make_async_copy(src, dst, loads[1].at[i]) for i, (src, dst) in enumerate(wanted)
        ]
        far, cross, right, left, own = sb, sq, s1, s3, loads[0]
    for copy in copies:
        copy.start()
    for k, at in cols:
        net.send((tag, "o", k), theirs(2).at[:, at], ro.at[:, at], zp)
    if not sent:
        for i in (1, 3):
            sum_side(net, p, tag, part, bufs, cols, i)
    yield
    for copy in copies:
        copy.wait()
    for k, at in cols:
        net.need((tag, "o", k))
        add_rows(sb.at[:, at], far.at[:, at], [ro.at[:, at]], rows)
        net.send((tag, "h", 1, k), sb.at[low, at], rh1.at[:, at], p.at(y=1))
        net.send((tag, "h", 3, k), sb.at[top, at], rh3.at[:, at], p.at(y=3))
    yield
    for k, at in cols:
        net.need((tag, "p", 1, k), (tag, "p", 3, k))
        add_rows(sq.at[:, at], cross.at[:, at], [rp1.at[:, at], rp3.at[:, at]], rows)
        net.send((tag, "q", k), sq.at[:, at], rq.at[:, at], zp)
    yield
    for k, at in cols:
        net.need((tag, "h", 1, k))
        if loads is None:
            s1[top, at] = right[top, at]
            s3[low, at] = left[low, at]
        add_rows(s1.at[low, at], right.at[low, at], [rh1.at[:, at]], half)
        net.send((tag, "w", 1, k), s1.at[:, at], rw1.at[:, at], p.at(y=1))
        net.need((tag, "h", 3, k))
        add_rows(s3.at[top, at], left.at[top, at], [rh3.at[:, at]], half)
        net.send((tag, "w", 3, k), s3.at[:, at], rw3.at[:, at], p.at(y=3))
    yield
    for k, at in cols:
        net.need((tag, "q", k), (tag, "w", 1, k), (tag, "w", 3, k))
        others = [rq.at[:, at], rw1.at[:, at], rw3.at[:, at]]
        if base is not None:
            others.append(base.at[:, at])
        add_rows(out.at[:, at], own.at[:, at], others, rows)


def dots(left, right, left_dim, right_dim):
    return lax.dot_general(
        left, right, (((left_dim,), (right_dim,)), ((), ())), preferred_element_type=F32
    )


def feed_forward_kernel(
    own, cot_in, weights_in, gn, hp_out, gu_out, dn_out,
    cot, weights, xs, gu, gh, hid, ggu, part, hp, dgu, dd, rgu, rdd, *rest,
):
    bufs, (send_sems, recv_sems, load_sems, store_sems) = rest[:12], rest[12:]
    p = Place()
    y, zl, c = p.y, p.zl, p.c
    sib = p.at(c=1)
    loads, stores = Loads(load_sems), Loads(store_sems)
    loads.start("x", own, xs.at[p.t])
    loads.start("c", cot_in, cot)
    loads.start("w", weights_in, weights)
    greet([sib, p.partner(), p.at(y=1), p.at(y=3)])
    net = Net(send_sems, recv_sems)
    gather = tp_gather_flow(net, p, "g", own, xs, own.shape[0])
    summed = tp_sum_flow(net, p, "s", part, gn, bufs, 2, sent=True)
    cols = split_cols(gn.shape[1], 2)
    advance(gather)
    gate_up_at, down_at = pl.ds(0, 2 * FF_PAD), pl.ds(2 * FF_PAD, FF_PAD)
    loads.need("c", "w")

    def grad_hidden(i):
        at = pl.ds(i * 2, 2)
        gh[pl.ds(pl.multiple_of(i * 256, 256), 256), :] = dots(
            cot[at].reshape(256, -1), weights[:, down_at], 1, 0
        )

    each(4, grad_hidden)
    advance(gather)
    loads.need("x")

    def pair(one, two):
        def both(ref):
            return jnp.concatenate([ref[one], ref[two]], axis=0)

        def products(j):
            at = pl.ds(pl.multiple_of(j * 768, 128), 768)
            gu[:, at] = dots(both(xs), weights[:, at], 1, 0)

        each(3, products)
        for k, block in enumerate((one, two)):

            def gates(j):
                at = pl.ds(pl.multiple_of(k * 128 + j * 16, 16), 16)
                to = pl.ds(pl.multiple_of(j * 16, 16), 16)
                row = pl.ds(pl.multiple_of(block * 128 + j * 16, 16), 16)
                gate, up = gu[at, pl.ds(0, FF_PAD)], gu[at, pl.ds(FF_PAD, FF_PAD)]
                grad = gh[row, :]
                sigma = jax.nn.sigmoid(gate)
                activated = gate * sigma
                hid[block, to, :] = (activated * up).astype(BF)
                ggu[block, to, pl.ds(0, FF_PAD)] = (
                    grad * up * sigma * (1.0 + gate * (1.0 - sigma))
                ).astype(BF)
                ggu[block, to, pl.ds(FF_PAD, FF_PAD)] = (grad * activated).astype(BF)

            each(8, gates)

        def back(j):
            at = pl.ds(pl.multiple_of(j * 512, 512), 512)
            total = dots(both(ggu), weights[at, gate_up_at], 1, 1).astype(BF)
            part[one, :, at] = total[:128]
            part[two, :, at] = total[128:]

        each(3, back)

    def mine(i):
        return ((y + i) % 4) * 2 + zl

    def theirs(i):
        return ((y + i) % 4) * 2 + 1 - zl

    pair(mine(0), theirs(0))
    advance(gather)
    net.need(("g", "r", 0), ("g", "r", 1), ("g", "l", 0), ("g", "l", 1))
    pair(mine(1), mine(3))
    advance(gather)
    net.need(("g", "p", 1), ("g", "p", 3))
    pair(theirs(1), theirs(3))
    for i in (1, 3):
        sum_side(net, p, "s", part, bufs, cols, i)
    net.need(("g", "o"))
    pair(mine(2), theirs(2))
    advance(summed)

    def hidden_out(j):
        at = pl.ds(pl.multiple_of(j * 512, 512), 512)
        total = dots(hid[...].reshape(1024, -1), weights[at, down_at], 1, 1)
        hp[:, :, at] = total.astype(BF).reshape(8, 128, 512)

    each(3, hidden_out)
    stores.start("h", hp, hp_out)
    advance(summed)
    advance(summed)

    def grad_down(j):
        at = pl.ds(pl.multiple_of(j * 384, 128), 384)
        total = dots(cot[:, :, at].reshape(1024, 384), hid[...].reshape(1024, -1), 0, 0)
        dd[pl.ds(j * 2, 2)] = total.astype(BF).reshape(2, 2, 96, FF_PAD)

    each(4, grad_down)
    net.send("d", dd.at[:, 1 - c], rdd, sib)
    advance(summed)

    def halves(ref, came, k):
        for f in (2 * k, 2 * k + 1):
            add_rows(ref.at[f, c], ref.at[f, c], [came.at[f]], 96)

    for k in range(4):
        two = pl.ds(k * 2, 2)

        def columns(j):
            at, to = pl.ds(k * 384, 384), pl.ds(pl.multiple_of(j * 768, 128), 768)
            left, right = xs[:, :, at].reshape(1024, 384), ggu[:, :, to].reshape(1024, 768)
            dgu[two, :, :, to] = dots(left, right, 0, 0).astype(BF).reshape(2, 2, 96, 768)

        each(3, columns)
        net.send(("e", k), dgu.at[two, 1 - c], rgu.at[two], sib)
        if k == 0:
            net.need("d")
        halves(dd, rdd, k)
        if k == 3:
            stores.start("d", dd.at[:, c], dn_out)
        if k > 0:
            net.need(("e", k - 1))
            halves(dgu, rgu, k - 1)
        if k == 2:
            advance(summed)
    net.need(("e", 3))
    halves(dgu, rgu, 3)
    stores.start("g", dgu.at[:, c], gu_out)
    stores.need("h", "d", "g")
    net.finish()


def feed_forward(own, cot, weights, cid=3, name="feed_forward"):
    vm = pl.BlockSpec(memory_space=pltpu.VMEM)
    hbm = pl.BlockSpec(memory_space=pl.ANY)
    rows, width = own.shape
    V = lambda *s: pltpu.VMEM(s, BF)
    whole, half = V(rows, width), V(rows // 2, width)
    B = lambda *s: jax.ShapeDtypeStruct(s, BF)
    D = pltpu.SemaphoreType.DMA
    n = 36
    return pl.pallas_call(
        feed_forward_kernel,
        out_shape=(
            jax.ShapeDtypeStruct((rows, width), F32),
            B(8, rows, width),
            B(8, 96, 2 * FF_PAD),
            B(8, 96, FF_PAD),
        ),
        in_specs=[hbm] * 3,
        out_specs=(vm, hbm, hbm, hbm),
        scratch_shapes=[
            V(8, rows, width),
            V(width, 3 * FF_PAD),
            V(8, rows, width),
            pltpu.VMEM((256, 2 * FF_PAD), F32),
            pltpu.VMEM((1024, FF_PAD), F32),
            V(8, 128, FF_PAD),
            V(8, 128, 2 * FF_PAD),
            V(8, rows, width),
            V(8, rows, width),
            V(8, 2, 96, 2 * FF_PAD),
            V(8, 2, 96, FF_PAD),
            V(8, 96, 2 * FF_PAD),
            V(8, 96, FF_PAD),
        ]
        + [whole] * 3
        + [half] * 2
        + [whole] * 7
        + [D((n,)), D((n,)), D((3,)), D((3,))],
        name=name,
        compiler_params=pltpu.CompilerParams(
            collective_id=cid, has_side_effects=True, vmem_limit_bytes=63 << 20
        ),
    )(own, cot, weights)


def weight_flow(net, p, tag, g, acc, rh1, rh3, rw1, rw3, rz, out, local):
    x, zh = p.x, p.zh
    top, low = pl.ds(0, 48), pl.ds(48, 48)
    sides = (("o", 1 - zh), ("s", zh))
    own = pltpu.make_async_copy(g, acc, local)
    own.start()

    def at(i, side):
        return side * 4 + (x + i) % 4

    for k, (s, side) in enumerate(sides):
        b = at(2, side)
        net.send((tag, "h", 1, s), g.at[b, low], rh1.at[k], p.at(x=1))
        net.send((tag, "h", 3, s), g.at[b, top], rh3.at[k], p.at(x=3))
        yield
    own.wait()
    for k, (s, side) in enumerate(sides):
        b = at(1, side)
        net.need((tag, "h", 1, s))
        add_rows(acc.at[b, low], acc.at[b, low], [rh1.at[k]], 48)
        net.send((tag, "w", 1, s), acc.at[b], rw1.at[k], p.at(x=1))
        b = at(3, side)
        net.need((tag, "h", 3, s))
        add_rows(acc.at[b, top], acc.at[b, top], [rh3.at[k]], 48)
        net.send((tag, "w", 3, s), acc.at[b], rw3.at[k], p.at(x=3))
        yield
    b = at(0, 1 - zh)
    net.need((tag, "w", 1, "o"), (tag, "w", 3, "o"))
    add_rows(acc.at[b], acc.at[b], [rw1.at[0], rw3.at[0]], 96)
    net.send((tag, "z"), acc.at[b], rz, p.at(z=2))
    yield
    b = at(0, zh)
    net.need((tag, "w", 1, "s"), (tag, "w", 3, "s"), (tag, "z"))
    add_rows(out, acc.at[b], [rw1.at[1], rw3.at[1], rz], 96)


def small_flow(net, p, src, out, rc, rings):
    net.send(("t", "c"), src, rc, p.at(c=1))
    yield
    net.need(("t", "c"))
    out[...] = src[...] + rc[...]
    for k, (ring, place) in enumerate(zip(rings, (p.x, p.y, p.z))):
        ring[place] = out[...]
        for i in (1, 3, 2):
            step = {"xyz"[k]: i}
            net.send(("t", k, i), ring.at[place], ring.at[place], p.at(**step))
        yield
        net.need(("t", k, 1), ("t", k, 2), ("t", k, 3))
        out[...] = ring[0] + ring[1] + ring[2] + ring[3]


def ring_sum_flow(net, p, tag, g, rc, rh1, rh3, rw1, rw3, ring, block, count):
    c = p.c
    sib = p.at(c=1)
    top, low = pl.ds(0, 48), pl.ds(48, 48)

    def mine(i):
        first, cols = block(i)
        return g.at[pl.ds(first, count), c, :, cols]

    def theirs(i):
        first, cols = block(i)
        return g.at[pl.ds(first, count), 1 - c, :, cols]

    def landed(i):
        first, cols = block(i)
        return rc.at[pl.ds(first, count), :, cols]

    def add(dst, others, rows, skip=0):
        def body(i):
            to = dst.at[i, pl.ds(skip, rows)]
            add_rows(to, to, [other.at[i] for other in others], rows)

        each(count, body)

    for i in (2, 3, 1, 0):
        net.send((tag, "c", i), theirs(i), landed(i), sib)
    yield
    b = mine(2)
    net.need((tag, "c", 2))
    add(b, [landed(2)], 96)
    net.send((tag, "h", 1), b.at[:, low], rh1, ring(1))
    net.send((tag, "h", 3), b.at[:, top], rh3, ring(3))
    yield
    for i in (1, 3):
        net.need((tag, "c", i))
        add(mine(i), [landed(i)], 96)
    yield
    for i, came, skip in ((1, rh1, 48), (3, rh3, 0)):
        net.need((tag, "h", i))
        add(mine(i), [came], 48, skip)
        net.send((tag, "w", i), mine(i), rw1 if i == 1 else rw3, ring(i))
    yield
    net.need((tag, "c", 0), (tag, "w", 1), (tag, "w", 3))
    add(mine(0), [landed(0), rw1, rw3], 96)


def along_x(net, p, tag, src, rx, total):
    x = p.x
    for i in (1, 3, 2):
        net.send((tag, "x", i), src.at[(x + i) % 4], rx.at[i - 1], p.at(x=i))
    yield
    net.need((tag, "x", 1), (tag, "x", 2), (tag, "x", 3))
    add_rows(total, src.at[x], [rx.at[0], rx.at[1], rx.at[2]], 96)


def z_flow(net, p, tag, g, bufs, total, width):
    rc, rh1, rh3, rw1, rw3, rx = bufs

    def block(i):
        zz = (p.z + i) % 4
        return (zz // 2) * 4, lanes(zz % 2, width)

    yield from ring_sum_flow(
        net, p, tag, g, rc, rh1, rh3, rw1, rw3, lambda i: p.at(z=i), block, 4
    )
    src = g.at[pl.ds(p.zh * 4, 4), p.c, :, lanes(p.zl, width)]
    yield from along_x(net, p, tag, src, rx, total)


def cross_sum(net, p, tag, src, rx, total):
    x, zh = p.x, p.zh
    for i in (0, 1, 3, 2):
        ref = src.at[(1 - zh) * 4 + (x + i) % 4]
        net.send((tag, "m", i), ref, rx.at[3 + i], p.mirror(i))
    for i in (1, 3, 2):
        net.send((tag, "x", i), src.at[zh * 4 + (x + i) % 4], rx.at[i - 1], p.at(x=i))
    yield
    net.need(*[(tag, "m", i) for i in range(4)], *[(tag, "x", i) for i in range(1, 4)])
    add_rows(total, src.at[p.f], [rx.at[i] for i in range(7)], 96)


def y_flow(net, p, tag, g, bufs, total, width, begin):
    rc, rh1, rh3, rw1, rw3, rx = bufs
    part = g.at[:, :, :, pl.ds(begin, 4 * width)] if begin else g
    yield from ring_sum_flow(
        net,
        p,
        tag,
        part,
        rc,
        rh1,
        rh3,
        rw1,
        rw3,
        lambda i: p.at(y=i),
        lambda i: (0, lanes((p.y + i) % 4, width)),
        8,
    )
    yield from cross_sum(net, p, tag, part.at[:, p.c, :, lanes(p.y, width)], rx, total)


def y_direct_flow(net, p, tag, g, bufs, total, width, begin):
    rc, ry, rx = bufs
    part = g.at[:, :, :, pl.ds(begin, 4 * width)]
    mine, theirs = part.at[:, p.c], part.at[:, 1 - p.c]
    for i in (2, 1, 3, 0):
        cols = lanes((p.y + i) % 4, width)
        net.send((tag, "c", i), theirs.at[:, :, cols], rc.at[:, :, cols], p.at(c=1))
    yield
    for i in (2, 1, 3, 0):
        cols = lanes((p.y + i) % 4, width)
        block = mine.at[:, :, cols]
        net.need((tag, "c", i))

        def near(k):
            add_rows(block.at[k], block.at[k], [rc.at[k, :, cols]], 96)

        each(8, near)
        if i:
            net.send((tag, "w", i), block, ry.at[i - 1], p.at(y=i))
    yield
    block = mine.at[:, :, lanes(p.y, width)]
    net.need(*[(tag, "w", i) for i in (1, 3, 2)])

    def whole(k):
        add_rows(block.at[k], block.at[k], [ry.at[i, k] for i in range(3)], 96)

    each(8, whole)
    yield from cross_sum(net, p, tag, block, rx, total)


def tp_scatter(net, p, tag, totals, pads, fins, to):
    t = p.t
    at = 0
    for total in totals:
        width = total.shape[1]
        for i in range(8):
            pads[i, pl.ds(0, 12), pl.ds(at, width)] = total[pl.ds(12 * i, 12), :].astype(BF)
            pads[i, pl.ds(12, 4), pl.ds(at, width)] = jnp.zeros((4, width), BF)
        at += width
    for i in range(1, 8):
        net.send((tag, "f", i), pads.at[(t + i) % 8], fins.at[t], to[i - 1])
    fins[t] = pads[t]


def norm_back_rows(grad, values, gain, base, out, grad_gain):
    grad_gain[...] = jnp.zeros_like(grad_gain)

    def body(i):
        at = pl.ds(pl.multiple_of(i * 16, 16), 16)
        v = values[at, :].astype(F32)
        g = grad[at, :]
        r = lax.rsqrt(jnp.mean(v * v, axis=-1, keepdims=True) + norm_eps)
        a = g * gain
        grad_gain[...] += jnp.sum(g * v * r, axis=0, keepdims=True)
        back = r * a - v * r * r * r * jnp.mean(a * v, axis=-1, keepdims=True)
        out[at, :] = base[at, :].astype(F32) + back

    each(grad.shape[0] // 16, body)


def backward_kernel(*refs):
    ga, gb, hp, w2t, w1, probs = refs[:6]
    near_in = refs[6:17]
    h_out, grad_in, o1, o2, oa, ob, small = refs[17:24]
    rest = list(refs[24:])

    def take(n):
        out = rest[:n]
        del rest[:n]
        return out

    near = take(11)
    gn, middle, cot, hidden_in, normed, attended, queries, kv, cos, sin, gains = near
    m_bufs = [take(6), take(6)]
    q_bufs, q_total = take(6), take(1)[0]
    o_bufs, o_total = take(6), take(1)[0]
    r_bufs, r_total = take(6), take(1)[0]
    v_bufs, v_total = take(3), take(1)[0]
    hp_bufs, hp_own = take(12), take(1)[0]
    kv_bufs, kv_part, kv_sum = take(12), take(1)[0], take(1)[0]
    rcs, rs1, rs2, rs3 = take(4)
    pad_q, fin_q, pad_v, fin_v = take(4)
    wide, deep, g1, g_mid, g_proj, g_att, g_qkv, stack_q, stack_a = take(9)
    gain_two, gain_one, part_small, gno = take(4)
    send_sems, recv_sems, local_sems, hp_sems, load_sems = take(5)

    p = Place()
    t = p.t
    tp_all = [{FS: p.f, CX: p.c, TP: (t + i) % 8} for i in range(1, 8)]
    loads = Loads(load_sems)
    for i in (0, 1, 2, 10):
        loads.start(i, near_in[i], near[i])
    loads.start("w", w2t, wide)
    loads.start("p", probs, deep)
    for i in (5, 7, 6, 8, 9, 4, 3):
        loads.start(i, near_in[i], near[i])
    greet(
        [p.at(c=1)] + [p.at(x=i) for i in (1, 2, 3)] + tp_all + [p.at(z=2)]
        + [p.mirror(i) for i in range(4)]
    )
    net = Net(send_sems, recv_sems)
    steps = Steps(BACKWARD_ORDER)
    steps.add("a", weight_flow(net, p, "a", ga, *m_bufs[0], oa, local_sems.at[0]))
    steps.add("b", weight_flow(net, p, "b", gb, *m_bufs[1], ob, local_sems.at[1]))
    flow_h = tp_sum_flow(
        net, p, "h", hp, h_out, hp_bufs, 2, loads=(hp_own, hp_sems), base=middle
    )
    steps.add("h", flow_h)
    steps.point()
    loads.need(0, 1, 2, 10)
    norm_back_rows(gn, middle, gains[pl.ds(1, 1), :], cot, g_mid, gain_two)
    g_proj[...] = g_mid[...].astype(BF)
    steps.point()
    loads.need("w")

    def grad_attended(j):
        at = pl.ds(pl.multiple_of(j * 512, 512), 512)
        g_att[:, at] = dots(g_proj[...], wide[:, at], 1, 0).astype(BF)

    each(3, grad_attended)
    steps.point()
    loads.need(5)

    def grad_out(j):
        at = pl.ds(pl.multiple_of(j * 384, 128), 384)
        wide[at, :] = dots(g_proj[:, at], attended[...], 0, 0).astype(BF)

    each(4, grad_out)
    steps.add("o", y_flow(net, p, 2, wide.reshape(8, 2, 96, 1536), o_bufs, o_total, 384, 0))
    steps.point()
    loads.need("p", 7, 6)
    size = HEAD_SIZE
    scale = size**-0.5

    def stack(h):
        at = pl.ds(pl.multiple_of(h * size, size), size)
        stack_q[at, :] = queries[:, at]
        stack_a[at, :] = g_att[:, at]

    each(QUERY_HEADS, stack)
    group_rows = [pl.ds(768 * group, 768) for group in range(KEY_VALUE_HEADS)]

    def sums(left, right, first, factor):
        def body(j):
            at = pl.ds(pl.multiple_of(j * 256, 256), 256)
            for group, rows in enumerate(group_rows):
                grad = dots(left[rows, at], right[rows, :], 0, 0) * factor
                to = pl.ds((first + group) * size, size)
                kv_part[pl.ds(j * 2, 2), :, to] = grad.astype(BF).reshape(2, 128, size)

        each(4, body)

    sums(deep, stack_a, KEY_VALUE_HEADS, 1.0)
    steps.point()
    for group in range(KEY_VALUE_HEADS):
        values = kv.at[:, pl.ds((KEY_VALUE_HEADS + group) * size, size)]

        def heads(j):
            at = pl.ds(pl.multiple_of(group * 768 + j * 256, 256), 256)
            grad = dots(stack_a[at, :], values[...], 1, 1)
            weight = deep[at, :].astype(F32)
            inner = jnp.sum(weight * grad, axis=-1, keepdims=True)
            deep[at, :] = (weight * (grad - inner)).astype(BF)

        each(3, heads)
        steps.point()
    sums(deep, stack_q, 0, scale)
    steps.add("k", tp_sum_flow(net, p, "k", kv_part, kv_sum, kv_bufs, 1))
    steps.point()
    loads.need(8, 9)

    def turned_back(grad):
        return (grad * cos[...] - pltpu.roll(grad, size // 2, 1) * sin[...]).astype(BF)

    for group in range(KEY_VALUE_HEADS):
        keys = kv.at[:, pl.ds(group * size, size)]

        def grad_query(j):
            at = pl.ds(pl.multiple_of(group * 768 + j * 256, 256), 256)
            grad = dots(deep[at, :], keys[...], 1, 0) * scale
            for i in range(2):
                to = pl.ds(pl.multiple_of((group * 6 + j * 2 + i) * size, size), size)
                g_qkv[:, to] = turned_back(grad[i * size : (i + 1) * size])

        each(3, grad_query)
        steps.point()
    loads.start("u", w1.at[:, pl.ds(0, 1024)], deep)
    loads.need(4)

    def grad_w(begin, count):
        at = pl.ds(begin, count)

        def body(j):
            d = pl.ds(pl.multiple_of(j * 384, 128), 384)
            total = dots(normed[:, d], g_qkv[:, at], 0, 0)
            g1[pl.ds(j * 2, 2), :, :, at] = total.astype(BF).reshape(2, 2, 96, count)

        each(4, body)

    grad_w(0, 1024)
    steps.add("q", z_flow(net, p, 1, g1, q_bufs, q_total, 512))
    steps.point()
    grad_w(1024, 512)
    steps.add("r", y_flow(net, p, 3, g1, r_bufs, r_total, 128, 1024))
    for _ in range(8):
        steps.point()
    steps.finish("k")
    for i in range(KEY_VALUE_HEADS):
        at, to = pl.ds(i * size, size), pl.ds((QUERY_HEADS + i) * size, size)
        g_qkv[:, to] = turned_back(kv_sum[:, at])
    at = pl.ds((QUERY_HEADS + KEY_VALUE_HEADS) * size, KEY_VALUE_HEADS * size)
    g_qkv[:, at] = kv_sum[:, pl.ds(KEY_VALUE_HEADS * size, KEY_VALUE_HEADS * size)].astype(BF)
    grad_w(1536, 512)
    steps.add("v", y_direct_flow(net, p, 4, g1, v_bufs, v_total, 128, 1536))
    for _ in range(4):
        steps.point()

    def normed_back(i):
        def body(j):
            at = pl.ds(pl.multiple_of(j * 512, 512), 512)
            total = dots(g_qkv[:, pl.ds(1024 * i, 1024)], deep[at, :], 1, 1)
            gno[:, at] = total if i == 0 else gno[:, at] + total

        each(3, body)

    loads.need("u")
    normed_back(0)
    loads.start("v", w1.at[:, pl.ds(1024, 1024)], deep)
    for _ in range(4):
        steps.point()
    loads.need("v")
    normed_back(1)
    loads.need(3)
    steps.point()
    norm_back_rows(gno, hidden_in, gains[pl.ds(0, 1), :], g_mid, grad_in, gain_one)
    bias = jnp.sum(g_qkv[...].astype(F32), axis=0, keepdims=True)
    for i in range(16):
        part_small[pl.ds(i, 1), :] = bias[:, i * 128 : i * 128 + 128]
    for i in range(12):
        part_small[pl.ds(16 + i, 1), :] = gain_one[:, pl.ds(i * 128, 128)]
        part_small[pl.ds(28 + i, 1), :] = gain_two[:, pl.ds(i * 128, 128)]
    steps.add("t", small_flow(net, p, part_small, small, rcs, (rs1, rs2, rs3)))
    for _ in range(14):
        steps.point()
    steps.finish("v")
    tp_scatter(net, p, 4, [v_total], pad_v, fin_v, tp_all)
    for _ in range(10):
        steps.point()
    steps.finish("q", "r", "o")
    tp_scatter(net, p, 2, [q_total, r_total, o_total], pad_q, fin_q, tp_all)
    for _ in range(8):
        steps.point()
    steps.finish("t", "a", "b", "h")
    net.need(*[(2, "f", i) for i in range(1, 8)])
    for k in range(2):
        at = pl.ds(0, 512)
        total = fin_q[k, :, at].astype(F32)
        for yy in range(1, 4):
            total += fin_q[2 * yy + k, :, at].astype(F32)
        o1[:, pl.ds(512 * k, 512)] = total
    for yy in range(4):
        at = pl.ds(512, 128)
        total = fin_q[2 * yy, :, at].astype(F32) + fin_q[2 * yy + 1, :, at].astype(F32)
        o1[:, pl.ds(1024 + 128 * yy, 128)] = total
        at = pl.ds(640, 384)
        total = fin_q[2 * yy, :, at].astype(F32) + fin_q[2 * yy + 1, :, at].astype(F32)
        o2[:, pl.ds(384 * yy, 384)] = total
    net.need(*[(4, "f", i) for i in range(1, 8)])
    for yy in range(4):
        total = fin_v[2 * yy].astype(F32) + fin_v[2 * yy + 1].astype(F32)
        o1[:, pl.ds(1536 + 128 * yy, 128)] = total
    net.finish()


def backward(far, near, cid=1, name="backward"):
    vm = pl.BlockSpec(memory_space=pltpu.VMEM)
    hbm = pl.BlockSpec(memory_space=pl.ANY)
    V = lambda *s: pltpu.VMEM(s, BF)
    W = lambda *s: pltpu.VMEM(s, F32)
    scratch = [pltpu.VMEM(a.shape, a.dtype) for a in near]
    for w in (far[0].shape[-1], far[1].shape[-1]):
        scratch += [
            V(8, 96, w), V(2, 48, w), V(2, 48, w), V(2, 96, w), V(2, 96, w), V(96, w),
        ]
    scratch += [
        V(8, 96, 1024), V(4, 48, 512), V(4, 48, 512), V(4, 96, 512), V(4, 96, 512), V(3, 96, 512),
        W(96, 512),
    ]
    for w in (384, 128):
        scratch += [
            V(8, 96, 4 * w), V(8, 48, w), V(8, 48, w), V(8, 96, w), V(8, 96, w), V(7, 96, w), W(96, w),
        ]
    scratch += [V(8, 96, 512), V(3, 8, 96, 128), V(7, 96, 128), W(96, 128)]
    whole, half = V(128, 1536), V(64, 1536)
    scratch += [whole] * 3 + [half] * 2 + [whole] * 7 + [whole]
    whole, half = V(128, 512), V(64, 512)
    scratch += [whole] * 3 + [half] * 2 + [whole] * 7 + [V(8, 128, 512), W(128, 512)]
    scratch += [W(40, 128)] + [W(4, 40, 128)] * 3
    scratch += [V(8, 16, 1024)] * 2 + [V(8, 16, 128)] * 2
    scratch += [
        V(1536, 1536), V(1536, 1024), V(8, 2, 96, 2048), W(128, 1536), V(128, 1536), V(128, 1536),
        V(128, 2048), V(1536, 128), V(1536, 128),
        W(1, 1536), W(1, 1536), W(40, 128), W(128, 1536),
    ]
    n = 140
    D = pltpu.SemaphoreType.DMA
    scratch += [D((n,)), D((n,)), D((2,)), D((5,)), D((16,))]
    S = lambda *s: jax.ShapeDtypeStruct(s, F32)
    return pl.pallas_call(
        backward_kernel,
        out_shape=(
            S(128, 1536), S(128, 1536), S(16, 2048), S(16, 1536),
            S(96, far[0].shape[-1]), S(96, far[1].shape[-1]), S(40, 128),
        ),
        in_specs=[hbm] * (len(far) + len(near)),
        out_specs=(vm,) * 7,
        scratch_shapes=scratch,
        name=name,
        compiler_params=pltpu.CompilerParams(
            collective_id=cid, has_side_effects=True, vmem_limit_bytes=62 << 20
        ),
    )(*far, *near)


def gather_rows_flow(net, p, tag, own, pad):
    t, tq = p.t, p.y * 2 + 1 - p.zl
    net.send((tag, "z"), own, pad.at[t], p.partner())
    for i in (1, 3, 2):
        net.send((tag, "y", i), own, pad.at[t], p.at(y=i))
    yield
    net.need((tag, "z"))
    for i in (1, 3, 2):
        net.send((tag, "p", i), pad.at[tq], pad.at[tq], p.at(y=i))
    yield
    net.need(*[(tag, k, i) for k in "yp" for i in (1, 2, 3)])


def close_up(pad, wide, blk):
    width = pad.shape[-1]
    for i in range(8):
        wide[pl.ds(12 * i, 12), pl.ds(0, width)] = pad[i, pl.ds(0, 12), :].astype(F32)
    blk[...] = wide[:, pl.ds(0, width)].astype(BF)


def cross_sends(net, p, tag, src, place):
    for i in (1, 3, 2):
        net.send((tag, "x", i), src, place, p.at(x=i))
    for i in (0, 1, 3, 2):
        net.send((tag, "m", i), src, place, p.mirror(i))


def cross_names(tag):
    return [(tag, "x", i) for i in (1, 2, 3)] + [(tag, "m", i) for i in range(4)]


def ring_gather_flow(net, p, tag, w, ring, block, count):
    c = p.c
    top, low = pl.ds(0, 48), pl.ds(48, 48)

    def part(i, rows=None):
        first, cols = block(i)
        if rows is None:
            return w.at[pl.ds(first, count), c, :, cols]
        return w.at[pl.ds(first, count), c, rows, cols]

    sib = p.at(c=1)
    net.send((tag, "r", 1), part(0), part(0), ring(1))
    net.send((tag, "r", 3), part(0), part(0), ring(3))
    net.send((tag, "c", 0), part(0), part(0), sib)
    yield
    net.need((tag, "r", 1), (tag, "r", 3))
    net.send((tag, "f", 1), part(3, top), part(3, top), ring(1))
    net.send((tag, "f", 3), part(1, low), part(1, low), ring(3))
    net.send((tag, "c", 3), part(3), part(3), sib)
    net.send((tag, "c", 1), part(1), part(1), sib)
    yield
    net.need((tag, "f", 1), (tag, "f", 3))
    net.send((tag, "c", 2), part(2), part(2), sib)
    yield
    net.need(*[(tag, "c", i) for i in range(4)])


def weights_flow(net, p, m_in, mw):
    f, c, x, zh = p.f, p.c, p.x, p.zh
    top, low = pl.ds(0, 48), pl.ds(48, 48)
    sib = p.at(c=1)
    far = (1 - zh) * 4 + x

    def across(k, ff):
        net.send(("m", "c", k), mw.at[ff, c], mw.at[ff, c], sib)

    def ring(tag, src, ff):
        net.send((tag, "r", 0), src.at[top], mw.at[ff, c, top], p.at(x=1))
        net.send((tag, "l", 1), src.at[low], mw.at[ff, c, low], p.at(x=3))
        yield
        net.send((tag, "r", 1), src.at[low], mw.at[ff, c, low], p.at(x=1))
        net.send((tag, "l", 0), src.at[top], mw.at[ff, c, top], p.at(x=3))
        yield

    def onward(tag, side, k):
        after, before = side * 4 + (x + 1) % 4, side * 4 + (x + 3) % 4
        net.need((tag, "r", 0), (tag, "l", 1))
        ref = mw.at[before, c, top]
        net.send((tag, "f", 1), ref, ref, p.at(x=1))
        ref = mw.at[after, c, low]
        net.send((tag, "f", 3), ref, ref, p.at(x=3))
        yield
        net.need((tag, "r", 1), (tag, "l", 0))
        across(k, before)
        across(k + 1, after)
        yield
        net.need((tag, "f", 1), (tag, "f", 3))
        across(k + 2, side * 4 + (x + 2) % 4)
        yield

    net.send(("m", "z"), m_in, mw.at[f, c], p.at(z=2))
    yield
    yield from ring("m", m_in, f)
    net.send(("m", "c", 0), m_in, mw.at[f, c], sib)
    net.need(("m", "z"))
    yield from ring("n", mw.at[far, c], far)
    yield from onward("m", zh, 1)
    across(4, far)
    yield from onward("n", 1 - zh, 5)
    net.need(*[("m", "c", k) for k in range(8)])


def cotangent_flow(net, p, own, out):
    y, zl, t = p.y, p.zl, p.t
    tq = y * 2 + 1 - zl
    zp = p.partner()
    top, low = pl.ds(0, 64), pl.ds(64, 64)
    net.send(("g", "r", 0), own.at[top], out.at[t, top], p.at(y=1))
    net.send(("g", "l", 1), own.at[low], out.at[t, low], p.at(y=3))
    yield
    net.send(("g", "r", 1), own.at[low], out.at[t, low], p.at(y=1))
    net.send(("g", "l", 0), own.at[top], out.at[t, top], p.at(y=3))
    yield
    net.send(("g", "z"), own, out.at[t], zp)
    yield
    net.need(("g", "r", 0), ("g", "l", 1))
    ref = out.at[((y + 3) % 4) * 2 + zl, top]
    net.send(("g", "f", 1), ref, ref, p.at(y=1))
    ref = out.at[((y + 1) % 4) * 2 + zl, low]
    net.send(("g", "f", 3), ref, ref, p.at(y=3))
    yield
    net.need(("g", "z"))
    net.send(("g", "p", 1), out.at[tq], out.at[tq], p.at(y=1))
    net.send(("g", "p", 3), out.at[tq], out.at[tq], p.at(y=3))
    yield
    net.need(("g", "f", 1), ("g", "f", 3))
    ref = out.at[((y + 2) % 4) * 2 + zl]
    net.send(("g", "o"), ref, ref, zp)
    yield
    net.need(("g", "r", 1), ("g", "l", 0), ("g", "p", 1), ("g", "p", 3), ("g", "o"))


def forward_kernel(*refs):
    a1_in, a2_in, m_in, c_in, hidden_in, bias_in, cos_in, sin_in, mask_in = refs[:9]
    w1, w2, mw, cg, probs, normed, queries, keys_values, attended, middle, normed_two, gains = refs[
        9:21
    ]
    (
        a1, a2, hid, bias, cos, sin, mask, pad1, pad2, wide, wide2, blk1, blk2,
        w1v, w2v, gn, kv, kv_own, prob, stack, nrm, send_sems, recv_sems, load_sems, store_sems,
    ) = refs[21:]
    p = Place()
    f, c, t, y, zl, zh = p.f, p.c, p.t, p.y, p.zl, p.zh
    loads, stores = Loads(load_sems), Loads(store_sems)
    loads.start("a", a1_in, a1)
    loads.start("o", a2_in, a2)
    loads.start("m", m_in, mw.at[f, c])
    loads.start("g", c_in, cg.at[t])
    for name, src, dst in (
        ("h", hidden_in, hid), ("b", bias_in, bias), ("c", cos_in, cos), ("s", sin_in, sin),
        ("k", mask_in, mask),
    ):
        loads.start(name, src, dst)
    greet(
        [p.at(c=1)]
        + [p.at(x=i) for i in (1, 2, 3)]
        + [p.at(y=i) for i in (1, 2, 3)]
        + [p.at(z=i) for i in (1, 2, 3)]
        + [p.mirror(i) for i in (1, 2, 3)]
    )
    net = Net(send_sems, recv_sems)
    steps = Steps(FORWARD_ORDER)
    loads.need("a")
    rows_1 = gather_rows_flow(net, p, "a", a1, pad1)
    next(rows_1)
    pad1[t] = a1[...]
    z_cols, y_cols = lanes(zl, 512), pl.ds(pl.multiple_of(1024 + y * 256, 128), 256)
    o_cols = lanes(zl, 768)
    x_three = (1, 3, 2)

    def z_block(width):
        def block(i):
            zz = (p.z + i) % 4
            return (zz // 2) * 4, lanes(zz % 2, width)

        return block

    def y_block(i):
        return 0, pl.ds(pl.multiple_of(1024 + ((y + i) % 4) * 256, 128), 256)

    def second_half():
        cross_sends(net, p, 2, blk1.at[:, y_cols], w1v.at[f, c, :, y_cols])
        w1v[f, c, :, y_cols] = blk1[:, y_cols]
        yield
        net.need(*cross_names(2))
        yield from ring_gather_flow(net, p, 5, w1v, lambda i: p.at(y=i), y_block, 8)

    def gains_flow():
        for i in x_three:
            net.send((3, "x", i), blk1.at[:, pl.ds(2048, 128)], gn.at[f, c], p.at(x=i))
        gn[f, c] = blk1[:, pl.ds(2048, 128)]
        yield
        net.need(*[(3, "x", i) for i in x_three])
        own_zh = pl.ds(zh * 4, 4)
        net.send((3, "m"), gn.at[own_zh, c], gn.at[own_zh, c], p.mirror())
        yield
        net.need((3, "m"))
        net.send((3, "c"), gn.at[:, c], gn.at[:, c], p.at(c=1))
        yield
        net.need((3, "c"))
        gains[...] = gn[...].reshape(1536, 128).astype(F32).T[:2]

    def out_flow():
        loads.need("o")
        rows = gather_rows_flow(net, p, "b", a2, pad2)
        next(rows)
        pad2[t] = a2[...]
        yield
        yield from rows
        close_up(pad2, wide2, blk2)
        for i in x_three:
            net.send((6, "x", i), blk2.at[:, o_cols], w2v.at[f, c, :, o_cols], p.at(x=i))
        w2v[f, c, :, o_cols] = blk2[:, o_cols]
        yield
        net.need(*[(6, "x", i) for i in x_three])
        yield from ring_gather_flow(net, p, 7, w2v, lambda i: p.at(z=i), z_block(768), 4)

    steps.add("m", weights_flow(net, p, m_in, mw))
    steps.add("c", cotangent_flow(net, p, c_in, cg))
    steps.add("o", out_flow())
    steps.point()
    next(rows_1)
    steps.point()
    next(rows_1, None)
    close_up(pad1, wide, blk1)
    for i in x_three:
        net.send((1, "x", i), blk1.at[:, z_cols], w1v.at[f, c, :, z_cols], p.at(x=i))
    w1v[f, c, :, z_cols] = blk1[:, z_cols]
    steps.add("2", second_half())
    steps.add("g", gains_flow())
    steps.point()
    net.need(*[(1, "x", i) for i in x_three])
    steps.add("1", ring_gather_flow(net, p, 4, w1v, lambda i: p.at(z=i), z_block(512), 4))
    for _ in range(8):
        steps.point()
    steps.finish("g")
    loads.need("h")

    def norm_one(i):
        at = pl.ds(pl.multiple_of(i * 16, 16), 16)
        v = hid[at, :].astype(F32)
        r = lax.rsqrt(jnp.mean(v * v, axis=-1, keepdims=True) + norm_eps)
        nrm[at, :] = (v * r * gains[pl.ds(0, 1), :]).astype(BF)

    each(8, norm_one)
    stores.start("n", nrm, normed)
    for _ in range(8):
        steps.point()
    steps.finish("1", "2")
    stores.start(1, w1v, w1)
    steps.point()
    loads.need("b", "c", "s")
    size = HEAD_SIZE
    weights = w1v.reshape(1536, 2048)

    def project(at):
        total = dots(nrm[...], weights[:, at], 1, 0)
        return total + bias[:, at]

    def turn(value):
        return (value * cos[...] + pltpu.roll(value, size // 2, 1) * sin[...]).astype(BF)

    total = project(pl.ds(1536, 512))
    for i in range(KEY_VALUE_HEADS):
        at = pl.ds(i * size, size)
        kv_own[:, at] = turn(total[:, i * size : (i + 1) * size])
    kv_own[:, pl.ds(256, 256)] = total[:, 256:].astype(BF)
    kv[t] = kv_own[...]

    def keys_flow():
        yield from tp_gather_flow(net, p, "k", kv_own, kv, 128)
        yield
        net.need(("k", "r", 1), ("k", "l", 0), ("k", "p", 1), ("k", "p", 3), ("k", "o"))

    steps.add("k", keys_flow())
    steps.point()
    for j in range(3):
        total = project(pl.ds(512 * j, 512))
        for i in range(4):
            rows = pl.ds((j * 4 + i) * size, size)
            stack[rows, :] = turn(total[:, i * size : (i + 1) * size])
        steps.point()
    for _ in range(8):
        steps.point()
    steps.finish("k")
    loads.need("k")
    stores.start("k", kv, keys_values)
    scale = size**-0.5
    for group in range(KEY_VALUE_HEADS):
        at_k, at_v = pl.ds(group * size, size), pl.ds((KEY_VALUE_HEADS + group) * size, size)

        def heads(j):
            rows = pl.ds(pl.multiple_of(group * 768 + j * 256, 256), 256)
            keys = kv[:, :, at_k].reshape(1024, size)
            values = kv[:, :, at_v].reshape(1024, size)
            score = dots(stack[rows, :], keys, 1, 1).reshape(2, 128, 1024) * scale
            score = jnp.where(mask[...][None] > 0.0, score, -1e30)
            top = jnp.max(score, axis=-1, keepdims=True)
            power = jnp.exp(score - top)
            share = power / jnp.sum(power, axis=-1, keepdims=True)
            share = share.astype(BF).reshape(256, 1024)
            prob[rows, :] = share
            total = dots(share, values, 1, 0).astype(BF)
            for i in range(2):
                head = group * 6 + j * 2 + i
                to = pl.ds(pl.multiple_of(head * size, size), size)
                attended[:, to] = total[i * size : (i + 1) * size]
                queries[:, to] = stack[pl.ds(pl.multiple_of(head * size, size), size), :]

        each(3, heads)
        steps.point()
    stores.start("p", prob, probs)
    for _ in range(6):
        steps.point()
    steps.finish("o")
    stores.start(2, w2v, w2)
    out_weights = w2v.reshape(1536, 1536)

    def project_out(j):
        at = pl.ds(pl.multiple_of(j * 512, 512), 512)
        middle[:, at] = hid[:, at].astype(F32) + dots(attended[...], out_weights[at, :], 1, 1)

    each(3, project_out)
    steps.point()

    def norm_two(i):
        at = pl.ds(pl.multiple_of(i * 16, 16), 16)
        v = middle[at, :]
        r = lax.rsqrt(jnp.mean(v * v, axis=-1, keepdims=True) + norm_eps)
        normed_two[at, :] = (v * r * gains[pl.ds(1, 1), :]).astype(BF)

    each(8, norm_two)
    for _ in range(6):
        steps.point()
    steps.finish("c", "m")
    net.finish()
    loads.need("m", "g")
    stores.need("n", 1, "k", "p", 2)


def forward(*args, cid=0, name="forward"):
    vm = pl.BlockSpec(memory_space=pltpu.VMEM)
    hbm = pl.BlockSpec(memory_space=pl.ANY)
    V = lambda *s: pltpu.VMEM(s, BF)
    W = lambda *s: pltpu.VMEM(s, F32)
    B = lambda *s: jax.ShapeDtypeStruct(s, BF)
    S = lambda *s: jax.ShapeDtypeStruct(s, F32)
    D = pltpu.SemaphoreType.DMA
    n = 110
    return pl.pallas_call(
        forward_kernel,
        out_shape=(
            B(8, 2, 96, 2048), B(8, 2, 96, 1536), B(8, 2, 96, 3 * FF_PAD), B(8, 128, 1536),
            B(1536, 1024), B(128, 1536), B(128, 1536), B(8, 128, 512), B(128, 1536),
            S(128, 1536), B(128, 1536), S(2, 1536),
        ),
        in_specs=[hbm] * len(args),
        out_specs=(hbm,) * 6 + (vm, hbm) + (vm,) * 4,
        scratch_shapes=[pltpu.VMEM(args[i].shape, args[i].dtype) for i in (0, 1, 4, 5, 6, 7, 8)]
        + [
            V(8, 16, 2176), V(8, 16, 1536), W(96, 2176), W(96, 1536), V(96, 2176), V(96, 1536),
            V(8, 2, 96, 2048), V(8, 2, 96, 1536), V(8, 2, 96, 128), V(8, 128, 512), V(128, 512),
            V(1536, 1024), V(1536, 128), V(128, 1536),
            D((n,)), D((n,)), D((9,)), D((5,)),
        ],
        name=name,
        compiler_params=pltpu.CompilerParams(
            collective_id=cid, has_side_effects=True, vmem_limit_bytes=60 << 20
        ),
    )(*args)


def doc_layout(lengths, places):
    ends = jnp.cumsum(lengths)
    starts = ends - lengths
    doc_ids = jnp.sum((ends[None, :] <= places[:, None]).astype(jnp.int32), axis=1)
    doc_start = jnp.max(jnp.where(starts[None, :] <= places[:, None], starts[None, :], 0), axis=1)
    return (doc_ids, places - doc_start)


def angles(position, size):
    half = size // 2
    freq = jnp.exp(jnp.arange(half, dtype=jnp.float32) * (-2.0 * math.log(rope_base) / size))
    angle = position.astype(jnp.float32)[:, None] * freq[None, :]
    return (jnp.cos(angle), jnp.sin(angle))


def adam_step(weight, moment, second, grad, rate, decay):
    moment = beta_one * moment + (1.0 - beta_one) * grad
    second = beta_two * second + (1.0 - beta_two) * grad * grad
    fix_one = 1.0 - beta_one**STEP
    fix_two = 1.0 - beta_two**STEP
    direction = moment / fix_one / (jnp.sqrt(second / fix_two) + adam_eps)
    return (weight - rate * (direction + decay * weight), moment, second)


def on_device(
    hidden_in,
    cotangent,
    seq_lengths,
    w_qkv,
    m_qkv,
    v_qkv,
    b_qkv,
    m_bias,
    v_bias,
    w_out,
    m_out,
    v_out,
    w_gate_up,
    m_gate_up,
    v_gate_up,
    w_down,
    m_down,
    v_down,
    gains,
    m_gains,
    v_gains,
):
    token_rows = hidden_in.shape[0]
    model_width = hidden_in.shape[1]
    tp_count = lax.axis_size(TP)
    packed_length = token_rows * tp_count
    ff_dev = w_gate_up.shape[2]
    own_places = lax.axis_index(TP) * token_rows + jnp.arange(token_rows, dtype=jnp.int32)
    key_places = jnp.arange(packed_length, dtype=jnp.int32)
    own_docs, own_pos = doc_layout(seq_lengths[0], own_places)
    key_docs = doc_layout(seq_lengths[0], key_places)[0]
    allowed = (own_docs[:, None] == key_docs[None, :]) & (
        key_places[None, :] <= own_places[:, None]
    )
    cosine_table, sine_table = angles(own_pos, HEAD_SIZE)
    cos_row = jnp.concatenate([cosine_table, cosine_table], axis=1)
    sin_row = jnp.concatenate([-sine_table, sine_table], axis=1)
    qkv_shard = jnp.concatenate([w_qkv.astype(BF), gains.astype(BF).T], axis=1)
    qkv_shard = jnp.pad(qkv_shard, ((0, 4), (0, 126)))
    out_shard = jnp.pad(w_out.astype(BF).T, ((0, 4), (0, 0)))
    side = ((0, 0), (0, FF_PAD - ff_dev))
    mlp_shard = jnp.concatenate(
        [
            jnp.pad(w_gate_up[:, 0].astype(BF), side),
            jnp.pad(w_gate_up[:, 1].astype(BF), side),
            jnp.pad(w_down.astype(BF).T, side),
        ],
        axis=1,
    )
    (
        qkv_full, out_turned, mlp_full, grad_group,
        probs, normed_one, queries, keys_values, attended, middle, normed_two, gains_full,
    ) = forward(
        qkv_shard,
        out_shard,
        mlp_shard,
        cotangent,
        hidden_in,
        b_qkv.astype(BF).astype(F32).reshape(1, -1),
        cos_row,
        sin_row,
        allowed.astype(F32),
    )
    grad_normed_two, down_parts, grad_w_gate_up, grad_w_down = feed_forward(
        normed_two, grad_group, mlp_full.reshape(model_width, -1)
    )
    hidden_out, grad_in, owned_qkv, owned_out, owned_gate_up, owned_down, small = backward(
        [
            grad_w_gate_up,
            grad_w_down,
            down_parts,
            out_turned.reshape(model_width, -1),
            qkv_full.reshape(model_width, -1),
            probs,
        ],
        [
            grad_normed_two,
            middle,
            cotangent,
            hidden_in,
            normed_one,
            attended,
            queries,
            keys_values.reshape(packed_length, -1),
            cos_row,
            sin_row,
            gains_full,
        ],
    )
    small = small.reshape(-1)
    summed_bias = small[: b_qkv.shape[0]]
    summed_gains = small[b_qkv.shape[0] :].reshape(2, model_width)
    own_gains = gains.shape[1]
    owned_gains = lax.dynamic_slice_in_dim(
        summed_gains, lax.axis_index(ALL) * own_gains, own_gains, axis=1
    )
    own_rows = w_qkv.shape[0]
    owned_qkv = owned_qkv[:own_rows]
    owned_out = owned_out[:own_rows].T
    owned_gate_up = jnp.stack(
        [owned_gate_up[:, :ff_dev], owned_gate_up[:, FF_PAD : FF_PAD + ff_dev]], axis=1
    )
    owned_down = owned_down[:, :ff_dev].T
    qkv_new, qkv_moment, qkv_second = adam_step(
        w_qkv, m_qkv, v_qkv, owned_qkv, rate_qkv, weight_decay
    )
    bias_new, bias_moment, bias_second = adam_step(
        b_qkv, m_bias, v_bias, summed_bias, rate_small, 0.0
    )
    out_new, out_moment, out_second = adam_step(
        w_out, m_out, v_out, owned_out, rate_out, weight_decay
    )
    gate_up_new, gate_up_moment, gate_up_second = adam_step(
        w_gate_up, m_gate_up, v_gate_up, owned_gate_up, rate_gate_up, weight_decay
    )
    down_new, down_moment, down_second = adam_step(
        w_down, m_down, v_down, owned_down, rate_down, weight_decay
    )
    gains_new, gains_moment, gains_second = adam_step(
        gains, m_gains, v_gains, owned_gains, rate_small, 0.0
    )
    return (
        hidden_out,
        grad_in,
        qkv_new,
        qkv_moment,
        qkv_second,
        bias_new,
        bias_moment,
        bias_second,
        out_new,
        out_moment,
        out_second,
        gate_up_new,
        gate_up_moment,
        gate_up_second,
        down_new,
        down_moment,
        down_second,
        gains_new,
        gains_moment,
        gains_second,
    )


def solution(mesh):
    placed = (
        P((FS, CX, TP), None),
        P((FS, CX, TP), None),
        P((FS, CX), None),
        P((FS, CX, TP), None),
        P((FS, CX, TP), None),
        P((FS, CX, TP), None),
        P(),
        P(),
        P(),
        P(None, (FS, CX, TP)),
        P(None, (FS, CX, TP)),
        P(None, (FS, CX, TP)),
        P((FS, CX), None, TP),
        P((FS, CX), None, TP),
        P((FS, CX), None, TP),
        P(TP, (FS, CX)),
        P(TP, (FS, CX)),
        P(TP, (FS, CX)),
        P(None, (FS, CX, TP)),
        P(None, (FS, CX, TP)),
        P(None, (FS, CX, TP)),
    )
    return jax.shard_map(
        on_device,
        mesh=mesh,
        in_specs=placed,
        out_specs=(
            P((FS, CX, TP), None),
            P((FS, CX, TP), None),
            P((FS, CX, TP), None),
            P((FS, CX, TP), None),
            P((FS, CX, TP), None),
            P(),
            P(),
            P(),
            P(None, (FS, CX, TP)),
            P(None, (FS, CX, TP)),
            P(None, (FS, CX, TP)),
            P((FS, CX), None, TP),
            P((FS, CX), None, TP),
            P((FS, CX), None, TP),
            P(TP, (FS, CX)),
            P(TP, (FS, CX)),
            P(TP, (FS, CX)),
            P(None, (FS, CX, TP)),
            P(None, (FS, CX, TP)),
            P(None, (FS, CX, TP)),
        ),
        check_vma=False,
    )
```

```python
import functools
import math

import jax
import jax.numpy as jnp
from jax import lax
from jax.experimental import pallas as pl
from jax.experimental.layout import Layout, with_layout_constraint
from jax.experimental.pallas import tpu as pltpu
from jax.sharding import PartitionSpec as P

QUERY_HEADS = 12
KEY_VALUE_HEADS = 2
HEAD_SIZE = 128
STEP = 10


norm_eps = 1e-06
rope_base = 1000000.0
beta_one = 0.9
beta_two = 0.95
adam_eps = 1e-08
weight_decay = 0.1
rate_qkv = 0.05
rate_out = 0.3
rate_gate_up = 0.05
rate_down = 0.02
rate_small = 0.5

BF = jnp.bfloat16
F32 = jnp.float32
FS, CX, TP = ALL = ("fsdp", "ctx", "tp")
FF_PAD = 1152
FORWARD_ORDER = (
    "21mmc", "1", "gc", "", "oc", "v1", "mog", "v", "", "1g", "c", "", "2ov", "2", "", "", "",
    "", "m", "", "", "", "", "mvk", "", "m", "1", "", "k2", "cmo", "g", "", "o2", "mm", "",
    "m1", "", "", "", "1ov", "", "m", "", "k", "", "", "c", "m", "", "", "", "o", "",
)
BACKWARD_ORDER = (
    "babh", "", "", "oa", "h", "bo", "", "kb", "b", "", "qo", "k", "", "", "q", "k", "", "oa",
    "", "", "vq", "", "qa", "", "vkr", "", "", "ra", "tt", "", "oh", "", "", "", "r", "",
    "rvtqt", "h", "", "", "", "r", "v", "", "", "", "", "b", "r", "", "", "", "", "", "", "",
    "", "q", "", "taho",
)


class Place:
    def __init__(self):
        self.f = lax.axis_index(FS)
        self.c = lax.axis_index(CX)
        self.t = lax.axis_index(TP)
        self.zh, self.x = self.f // 4, self.f % 4
        self.y, self.zl = self.t // 2, self.t % 2
        self.z = self.zh * 2 + self.zl

    def at(self, x=0, y=0, z=0, c=0):
        zz = (self.z + z) % 4
        return {
            FS: (zz // 2) * 4 + (self.x + x) % 4,
            CX: (self.c + c) % 2,
            TP: ((self.y + y) % 4) * 2 + zz % 2,
        }

    def partner(self):
        return {FS: self.f, CX: self.c, TP: self.y * 2 + 1 - self.zl}

    def mirror(self, x=0):
        return {
            FS: (1 - self.zh) * 4 + (self.x + x) % 4,
            CX: self.c,
            TP: self.y * 2 + 1 - self.zl,
        }


def greet(devices):
    barrier = pltpu.get_barrier_semaphore()
    for device in devices:
        pl.semaphore_signal(barrier, inc=1, device_id=device, device_id_type=pl.DeviceIdType.MESH)
    pl.semaphore_wait(barrier, len(devices))


class Steps:
    def __init__(self, order):
        self.flows, self.order, self.at = {}, order, 0

    def add(self, name, flow):
        self.flows[name] = flow

    def point(self):
        for name in self.order[self.at]:
            if name in self.flows:
                next(self.flows[name], None)
        self.at += 1

    def finish(self, *names):
        for name in names:
            for _ in self.flows[name]:
                pass


class Loads:
    def __init__(self, sems):
        self.sems, self.used, self.copies = sems, 0, {}

    def start(self, name, src, dst):
        copy = pltpu.make_async_copy(src, dst, self.sems.at[self.used])
        self.used += 1
        copy.start()
        self.copies[name] = copy

    def need(self, *names):
        for name in names:
            self.copies.pop(name).wait()


class Net:
    def __init__(self, send_sems, recv_sems):
        self.send_sems, self.recv_sems = send_sems, recv_sems
        self.copies, self.arrived = {}, set()

    def send(self, name, src, dst, device, after=()):
        self.need(*after)
        at = len(self.copies)
        copy = pltpu.make_async_remote_copy(
            src_ref=src,
            dst_ref=dst,
            send_sem=self.send_sems.at[at],
            recv_sem=self.recv_sems.at[at],
            device_id=device,
            device_id_type=pl.DeviceIdType.MESH,
        )
        copy.start()
        self.copies[name] = copy

    def need(self, *names):
        for name in names:
            if name not in self.arrived:
                self.arrived.add(name)
                self.copies[name].wait_recv()

    def finish(self):
        self.need(*self.copies)
        for copy in self.copies.values():
            copy.wait_send()


def lanes(at, size):
    return pl.ds(pl.multiple_of(at * size, 128), size)


def each(n, body):
    def step(i, carry):
        body(i)
        return carry

    lax.fori_loop(0, n, step, 0)


def add_rows(dst, first, others, rows):
    width = dst.shape[-1]
    step = max(k for k in range(16, rows + 1, 16) if rows % k == 0 and (k * width <= 49152 or k == 16))

    def body(i):
        at = pl.ds(pl.multiple_of(i * step, 16), step)
        if len(others) == 1 and dst.dtype == BF:
            dst[at, :] = first[at, :] + others[0][at, :]
        else:
            total = first[at, :].astype(F32)
            for other in others:
                total += other[at, :].astype(F32)
            dst[at, :] = total.astype(dst.dtype)

    if step == rows:
        body(0)
    else:
        each(rows // step, body)


def advance(*flows):
    for flow in flows:
        next(flow, None)


def tp_gather_flow(net, p, tag, own, out, rows):
    y, zl, t = p.y, p.zl, p.t
    tq = y * 2 + 1 - zl
    zp = p.partner()
    top, low = pl.ds(0, rows // 2), pl.ds(rows // 2, rows // 2)
    net.send((tag, "z"), own, out.at[t], zp)
    net.send((tag, "r", 0), own.at[top], out.at[t, top], p.at(y=1))
    net.send((tag, "l", 1), own.at[low], out.at[t, low], p.at(y=3))
    net.send((tag, "r", 1), own.at[low], out.at[t, low], p.at(y=1))
    net.send((tag, "l", 0), own.at[top], out.at[t, top], p.at(y=3))
    yield
    net.need((tag, "z"))
    net.send((tag, "p", 1), out.at[tq], out.at[tq], p.at(y=1))
    net.send((tag, "p", 3), out.at[tq], out.at[tq], p.at(y=3))
    yield
    ref = out.at[((y + 3) % 4) * 2 + zl, top]
    net.send((tag, "f", 1), ref, ref, p.at(y=1), after=[(tag, "r", 0)])
    ref = out.at[((y + 1) % 4) * 2 + zl, low]
    net.send((tag, "f", 3), ref, ref, p.at(y=3), after=[(tag, "l", 1)])
    yield
    ref = out.at[((y + 2) % 4) * 2 + zl]
    net.send((tag, "o"), ref, ref, zp, after=[(tag, "f", 1), (tag, "f", 3)])


def sum_side(net, p, tag, part, bufs, cols, i):
    src = part.at[((p.y + i) % 4) * 2 + 1 - p.zl]
    dst = bufs[1 if i == 1 else 2]
    for k, at in cols:
        net.send((tag, "p", i, k), src.at[:, at], dst.at[:, at], p.at(y=i))


def split_cols(width, chunks):
    w = width // chunks
    return [(k, pl.ds(k * w, w)) for k in range(chunks)]


def tp_sum_flow(net, p, tag, part, out, bufs, chunks, sent=False, loads=None, base=None):
    ro, rp1, rp3, rh1, rh3, rw1, rw3, rq, sb, sq, s1, s3 = bufs
    y, zl, t = p.y, p.zl, p.t
    zp = p.partner()
    rows, width = out.shape
    half = rows // 2
    top, low = pl.ds(0, half), pl.ds(half, half)
    cols = split_cols(width, chunks)

    def mine(i):
        return part.at[((y + i) % 4) * 2 + zl]

    def theirs(i):
        return part.at[((y + i) % 4) * 2 + 1 - zl]

    far, cross, right, left, own = mine(2), theirs(0), mine(1), mine(3), mine(0)
    copies = []
    if loads is not None:
        wanted = zip((far, cross, right, left, own), (sb, sq, s1, s3, loads[0]))
        copies = [
            pltpu.make_async_copy(src, dst, loads[1].at[i]) for i, (src, dst) in enumerate(wanted)
        ]
        far, cross, right, left, own = sb, sq, s1, s3, loads[0]
    for copy in copies:
        copy.start()
    for k, at in cols:
        net.send((tag, "o", k), theirs(2).at[:, at], ro.at[:, at], zp)
    if not sent:
        for i in (1, 3):
            sum_side(net, p, tag, part, bufs, cols, i)
    yield
    for copy in copies:
        copy.wait()
    for k, at in cols:
        net.need((tag, "o", k))
        add_rows(sb.at[:, at], far.at[:, at], [ro.at[:, at]], rows)
        net.send((tag, "h", 1, k), sb.at[low, at], rh1.at[:, at], p.at(y=1))
        net.send((tag, "h", 3, k), sb.at[top, at], rh3.at[:, at], p.at(y=3))
    yield
    for k, at in cols:
        net.need((tag, "p", 1, k), (tag, "p", 3, k))
        add_rows(sq.at[:, at], cross.at[:, at], [rp1.at[:, at], rp3.at[:, at]], rows)
        net.send((tag, "q", k), sq.at[:, at], rq.at[:, at], zp)
    yield
    for k, at in cols:
        net.need((tag, "h", 1, k))
        if loads is None:
            s1[top, at] = right[top, at]
            s3[low, at] = left[low, at]
        add_rows(s1.at[low, at], right.at[low, at], [rh1.at[:, at]], half)
        net.send((tag, "w", 1, k), s1.at[:, at], rw1.at[:, at], p.at(y=1))
        net.need((tag, "h", 3, k))
        add_rows(s3.at[top, at], left.at[top, at], [rh3.at[:, at]], half)
        net.send((tag, "w", 3, k), s3.at[:, at], rw3.at[:, at], p.at(y=3))
    yield
    for k, at in cols:
        net.need((tag, "q", k), (tag, "w", 1, k), (tag, "w", 3, k))
        others = [rq.at[:, at], rw1.at[:, at], rw3.at[:, at]]
        if base is not None:
            others.append(base.at[:, at])
        add_rows(out.at[:, at], own.at[:, at], others, rows)


def short_sum_flow(net, p, tag, part, out, bufs, chunks, sent=False):
    ro, rp1, rp3, rw1, rw3, rf, rq, sb, sq = bufs
    y, zl = p.y, p.zl
    zp = p.partner()
    rows, width = out.shape
    cols = split_cols(width, chunks)

    def mine(i):
        return part.at[((y + i) % 4) * 2 + zl]

    def theirs(i):
        return part.at[((y + i) % 4) * 2 + 1 - zl]

    for k, at in cols:
        net.send((tag, "o", k), theirs(2).at[:, at], ro.at[:, at], zp)
    if not sent:
        short_sides(net, p, tag, part, bufs, cols, True)
        short_sides(net, p, tag, part, bufs, cols, False)
    yield
    for k, at in cols:
        net.need((tag, "o", k))
        add_rows(sb.at[:, at], mine(2).at[:, at], [ro.at[:, at]], rows)
        net.send((tag, "f", k), sb.at[:, at], rf.at[:, at], p.at(y=2))
    yield
    for k, at in cols:
        net.need((tag, "p", 1, k), (tag, "p", 3, k))
        add_rows(sq.at[:, at], theirs(0).at[:, at], [rp1.at[:, at], rp3.at[:, at]], rows)
        net.send((tag, "q", k), sq.at[:, at], rq.at[:, at], zp)
    yield
    for k, at in cols:
        net.need((tag, "w", 1, k), (tag, "w", 3, k), (tag, "q", k), (tag, "f", k))
        others = [ref.at[:, at] for ref in (rq, rw1, rw3, rf)]
        add_rows(out.at[:, at], mine(0).at[:, at], others, rows)


def short_sides(net, p, tag, part, bufs, cols, theirs):
    for i in (1, 3):
        src = part.at[((p.y + i) % 4) * 2 + (1 - p.zl if theirs else p.zl)]
        dst = bufs[(1 if theirs else 3) + i // 2]
        for k, at in cols:
            name = (tag, "p" if theirs else "w", i, k)
            net.send(name, src.at[:, at], dst.at[:, at], p.at(y=i))


def dots(left, right, left_dim, right_dim):
    return lax.dot_general(
        left, right, (((left_dim,), (right_dim,)), ((), ())), preferred_element_type=F32
    )


def feed_forward_kernel(
    own, cot_in, weights_in, gn, hp_out, gu_out, dn_out,
    cot, weights, xs, gu, gh, hid, ggu, part, hp, dgu, dd, rgu, rdd, *rest,
):
    bufs, (send_sems, recv_sems, load_sems, store_sems) = rest[:9], rest[9:]
    p = Place()
    y, zl, c = p.y, p.zl, p.c
    sib = p.at(c=1)
    loads, stores = Loads(load_sems), Loads(store_sems)
    loads.start("x", own, xs.at[p.t])
    loads.start("c", cot_in, cot)
    loads.start("w", weights_in, weights)
    greet([sib, p.partner()] + [p.at(y=i) for i in (1, 2, 3)])
    net = Net(send_sems, recv_sems)
    t, tq, zp = p.t, y * 2 + 1 - zl, p.partner()
    top, low = pl.ds(0, 64), pl.ds(64, 64)
    net.send(("g", "z"), own, xs.at[t], zp)
    net.send(("g", "r", 0), own.at[top], xs.at[t, top], p.at(y=1))
    net.send(("g", "l", 1), own.at[low], xs.at[t, low], p.at(y=3))
    gate_up_at, down_at = pl.ds(0, 2 * FF_PAD), pl.ds(2 * FF_PAD, FF_PAD)
    loads.need("c", "w")

    def grad_hidden(i):
        at = pl.ds(i * 4, 4)
        gh[pl.ds(pl.multiple_of(i * 512, 512), 512), :] = dots(
            cot[at].reshape(512, -1), weights[:, down_at], 1, 0
        )

    grad_hidden(0)
    net.send(("g", "r", 1), own.at[low], xs.at[t, low], p.at(y=1))
    net.send(("g", "l", 0), own.at[top], xs.at[t, top], p.at(y=3))
    grad_hidden(1)

    def mine(i):
        return ((y + i) % 4) * 2 + zl

    def theirs(i):
        return ((y + i) % 4) * 2 + 1 - zl

    net.need(("g", "r", 0), ("g", "l", 1))
    net.send(("g", "f", 1), xs.at[mine(3), top], xs.at[mine(3), top], p.at(y=1))
    net.send(("g", "f", 3), xs.at[mine(1), low], xs.at[mine(1), low], p.at(y=3))
    net.need(("g", "z"))
    for i in (1, 3):
        net.send(("g", "p", i), xs.at[tq], xs.at[tq], p.at(y=i))
    loads.need("x")

    def pair(one, two, sends=()):
        def both(ref):
            return jnp.concatenate([ref[one], ref[two]], axis=0)

        gu[...] = dots(both(xs), weights[:, gate_up_at], 1, 0)
        for k, block in enumerate((one, two)):

            def gates(j):
                at = pl.ds(pl.multiple_of(k * 128 + j * 16, 16), 16)
                to = pl.ds(pl.multiple_of(j * 16, 16), 16)
                row = pl.ds(pl.multiple_of(block * 128 + j * 16, 16), 16)
                gate, up = gu[at, pl.ds(0, FF_PAD)], gu[at, pl.ds(FF_PAD, FF_PAD)]
                grad = gh[row, :]
                sigma = jax.nn.sigmoid(gate)
                activated = gate * sigma
                hid[block, to, :] = (activated * up).astype(BF)
                ggu[block, to, pl.ds(0, FF_PAD)] = (
                    grad * up * sigma * (1.0 + gate * (1.0 - sigma))
                ).astype(BF)
                ggu[block, to, pl.ds(FF_PAD, FF_PAD)] = (grad * activated).astype(BF)

            each(8, gates)
        for j in range(2):
            at = pl.ds(j * 768, 768)
            total = dots(both(ggu), weights[at, gate_up_at], 1, 1).astype(BF)
            part[one, :, at] = total[:128]
            part[two, :, at] = total[128:]
            for send in sends:
                send(j, at)

    def hidden_out(blocks):
        for j in range(2):
            at = pl.ds(j * 768, 768)
            rows = jnp.concatenate([hid[block] for block in blocks], axis=0)
            total = dots(rows, weights[at, down_at], 1, 1).astype(BF)
            for k, block in enumerate(blocks):
                hp[block, :, at] = total[k * 128 : k * 128 + 128]

    ro, rp1, rp3, rw1, rw3, rf, rq, sb, sq = bufs

    def side(name, i, src, dst):
        def send(j, at):
            net.send(("s", name, i, j), src.at[:, at], dst.at[:, at], p.at(y=i))

        return send

    def across(j, at):
        net.send(("s", "o", j), part.at[theirs(2), :, at], ro.at[:, at], zp)

    pair(mine(0), theirs(0))
    net.need(("g", "f", 1), ("g", "f", 3))
    net.send(("g", "o"), xs.at[mine(2)], xs.at[mine(2)], zp)
    net.need(("g", "r", 1), ("g", "l", 0))
    pair(mine(1), mine(3))
    hidden_out([mine(0), theirs(0), mine(1), mine(3)])
    net.need(("g", "p", 1), ("g", "p", 3))
    sides = [(1, rp1, rw1), (3, rp3, rw3)]
    pair(
        theirs(1), theirs(3), [side("p", i, part.at[theirs(i)], dst) for i, dst, _ in sides]
    )
    net.need(("g", "o"))
    pair(mine(2), theirs(2), [across])
    cols = split_cols(gn.shape[1], 2)
    for i, _, dst in sides:
        for j, at in cols:
            side("w", i, part.at[mine(i)], dst)(j, at)
    hidden_out([theirs(1), theirs(3), mine(2), theirs(2)])
    stores.start("h", hp, hp_out)
    rows = own.shape[0]
    def halves(ref, came, k):
        for f in (2 * k, 2 * k + 1):
            add_rows(ref.at[f, c], ref.at[f, c], [came.at[f]], 96)

    for k in range(4):
        two = pl.ds(k * 2, 2)

        def columns(j):
            at, to = pl.ds(k * 384, 384), pl.ds(pl.multiple_of(j * 768, 128), 768)
            left, right = xs[:, :, at].reshape(1024, 384), ggu[:, :, to].reshape(1024, 768)
            dgu[two, :, :, to] = dots(left, right, 0, 0).astype(BF).reshape(2, 2, 96, 768)

        each(3, columns)
        net.send(("e", k), dgu.at[two, 1 - c], rgu.at[two], sib)
        if k == 0:
            for j, at in cols:
                net.need(("s", "o", j))
                add_rows(sb.at[:, at], part.at[mine(2), :, at], [ro.at[:, at]], rows)
                net.send(("s", "f", j), sb.at[:, at], rf.at[:, at], p.at(y=2))
            for j, at in cols:
                net.need(("s", "p", 1, j), ("s", "p", 3, j))
                others = [rp1.at[:, at], rp3.at[:, at]]
                add_rows(sq.at[:, at], part.at[theirs(0), :, at], others, rows)
                net.send(("s", "q", j), sq.at[:, at], rq.at[:, at], zp)
        else:
            net.need(("e", k - 1))
            halves(dgu, rgu, k - 1)
    for k in range(4):
        two, at = pl.ds(k * 2, 2), pl.ds(k * 384, 384)
        total = dots(cot[:, :, at].reshape(1024, 384), hid[...].reshape(1024, -1), 0, 0)
        dd[two] = total.astype(BF).reshape(2, 2, 96, FF_PAD)
        net.send(("d", k), dd.at[two, 1 - c], rdd.at[two], sib)
        if k == 0:
            net.need(("e", 3))
            halves(dgu, rgu, 3)
            stores.start("g", dgu.at[:, c], gu_out)
        else:
            net.need(("d", k - 1))
            halves(dd, rdd, k - 1)
    for j, at in cols:
        net.need(("s", "w", 1, j), ("s", "w", 3, j), ("s", "q", j), ("s", "f", j))
        others = [ref.at[:, at] for ref in (rq, rw1, rw3, rf)]
        add_rows(gn.at[:, at], part.at[t, :, at], others, rows)
    net.need(("d", 3))
    halves(dd, rdd, 3)
    stores.start("d", dd.at[:, c], dn_out)
    stores.need("h", "d", "g")
    net.finish()


def feed_forward(own, cot, weights, cid=3, name="feed_forward"):
    vm = pl.BlockSpec(memory_space=pltpu.VMEM)
    hbm = pl.BlockSpec(memory_space=pl.ANY)
    rows, width = own.shape
    V = lambda *s: pltpu.VMEM(s, BF)
    whole = V(rows, width)
    B = lambda *s: jax.ShapeDtypeStruct(s, BF)
    D = pltpu.SemaphoreType.DMA
    n = 36
    return pl.pallas_call(
        feed_forward_kernel,
        out_shape=(
            jax.ShapeDtypeStruct((rows, width), F32),
            B(8, rows, width),
            B(8, 96, 2 * FF_PAD),
            B(8, 96, FF_PAD),
        ),
        in_specs=[hbm] * 3,
        out_specs=(vm, hbm, hbm, hbm),
        scratch_shapes=[
            V(8, rows, width),
            V(width, 3 * FF_PAD),
            V(8, rows, width),
            pltpu.VMEM((256, 2 * FF_PAD), F32),
            pltpu.VMEM((1024, FF_PAD), F32),
            V(8, 128, FF_PAD),
            V(8, 128, 2 * FF_PAD),
            V(8, rows, width),
            V(8, rows, width),
            V(8, 2, 96, 2 * FF_PAD),
            V(8, 2, 96, FF_PAD),
            V(8, 96, 2 * FF_PAD),
            V(8, 96, FF_PAD),
        ]
        + [whole] * 9
        + [D((n,)), D((n,)), D((3,)), D((3,))],
        name=name,
        compiler_params=pltpu.CompilerParams(
            collective_id=cid, has_side_effects=True, vmem_limit_bytes=63 << 20
        ),
    )(own, cot, weights)


def weight_flow(net, p, tag, g, acc, rh1, rh3, rw1, rw3, rz, out, local):
    x, zh = p.x, p.zh
    top, low = pl.ds(0, 48), pl.ds(48, 48)
    sides = (("o", 1 - zh), ("s", zh))
    own = pltpu.make_async_copy(g, acc, local)
    own.start()

    def at(i, side):
        return side * 4 + (x + i) % 4

    for k, (s, side) in enumerate(sides):
        b = at(2, side)
        net.send((tag, "h", 1, s), g.at[b, low], rh1.at[k], p.at(x=1))
        net.send((tag, "h", 3, s), g.at[b, top], rh3.at[k], p.at(x=3))
        yield
    own.wait()
    for k, (s, side) in enumerate(sides):
        b = at(1, side)
        net.need((tag, "h", 1, s))
        add_rows(acc.at[b, low], acc.at[b, low], [rh1.at[k]], 48)
        net.send((tag, "w", 1, s), acc.at[b], rw1.at[k], p.at(x=1))
        b = at(3, side)
        net.need((tag, "h", 3, s))
        add_rows(acc.at[b, top], acc.at[b, top], [rh3.at[k]], 48)
        net.send((tag, "w", 3, s), acc.at[b], rw3.at[k], p.at(x=3))
        yield
    b = at(0, 1 - zh)
    net.need((tag, "w", 1, "o"), (tag, "w", 3, "o"))
    add_rows(acc.at[b], acc.at[b], [rw1.at[0], rw3.at[0]], 96)
    net.send((tag, "z"), acc.at[b], rz, p.at(z=2))
    yield
    b = at(0, zh)
    net.need((tag, "w", 1, "s"), (tag, "w", 3, "s"), (tag, "z"))
    add_rows(out, acc.at[b], [rw1.at[1], rw3.at[1], rz], 96)


def small_flow(net, p, src, out, rc, rings):
    net.send(("t", "c"), src, rc, p.at(c=1))
    yield
    net.need(("t", "c"))
    out[...] = src[...] + rc[...]
    for k, (ring, place) in enumerate(zip(rings, (p.x, p.y, p.z))):
        ring[place] = out[...]
        for i in (1, 3, 2):
            step = {"xyz"[k]: i}
            net.send(("t", k, i), ring.at[place], ring.at[place], p.at(**step))
        yield
        net.need(("t", k, 1), ("t", k, 2), ("t", k, 3))
        out[...] = ring[0] + ring[1] + ring[2] + ring[3]


def ring_sum_flow(net, p, tag, g, rc, rh1, rh3, rw1, rw3, ring, block, count):
    c = p.c
    sib = p.at(c=1)
    top, low = pl.ds(0, 48), pl.ds(48, 48)

    def mine(i):
        first, cols = block(i)
        return g.at[pl.ds(first, count), c, :, cols]

    def theirs(i):
        first, cols = block(i)
        return g.at[pl.ds(first, count), 1 - c, :, cols]

    def landed(i):
        first, cols = block(i)
        return rc.at[pl.ds(first, count), :, cols]

    def add(dst, others, rows, skip=0):
        def body(i):
            to = dst.at[i, pl.ds(skip, rows)]
            add_rows(to, to, [other.at[i] for other in others], rows)

        each(count, body)

    for i in (2, 3, 1, 0):
        net.send((tag, "c", i), theirs(i), landed(i), sib)
    yield
    b = mine(2)
    net.need((tag, "c", 2))
    add(b, [landed(2)], 96)
    net.send((tag, "h", 1), b.at[:, low], rh1, ring(1))
    net.send((tag, "h", 3), b.at[:, top], rh3, ring(3))
    yield
    for i in (1, 3):
        net.need((tag, "c", i))
        add(mine(i), [landed(i)], 96)
    yield
    for i, came, skip in ((1, rh1, 48), (3, rh3, 0)):
        net.need((tag, "h", i))
        add(mine(i), [came], 48, skip)
        net.send((tag, "w", i), mine(i), rw1 if i == 1 else rw3, ring(i))
    yield
    net.need((tag, "c", 0), (tag, "w", 1), (tag, "w", 3))
    add(mine(0), [landed(0), rw1, rw3], 96)


def along_x(net, p, tag, src, rx, total):
    x = p.x
    for i in (1, 3, 2):
        net.send((tag, "x", i), src.at[(x + i) % 4], rx.at[i - 1], p.at(x=i))
    yield
    net.need((tag, "x", 1), (tag, "x", 2), (tag, "x", 3))
    add_rows(total, src.at[x], [rx.at[0], rx.at[1], rx.at[2]], 96)


def z_flow(net, p, tag, g, bufs, total, width):
    rc, rh1, rh3, rw1, rw3, rx = bufs

    def block(i):
        zz = (p.z + i) % 4
        return (zz // 2) * 4, lanes(zz % 2, width)

    yield from ring_sum_flow(
        net, p, tag, g, rc, rh1, rh3, rw1, rw3, lambda i: p.at(z=i), block, 4
    )
    src = g.at[pl.ds(p.zh * 4, 4), p.c, :, lanes(p.zl, width)]
    yield from along_x(net, p, tag, src, rx, total)


def cross_sum(net, p, tag, src, rx, total):
    x, zh = p.x, p.zh
    for i in (0, 1, 3, 2):
        ref = src.at[(1 - zh) * 4 + (x + i) % 4]
        net.send((tag, "m", i), ref, rx.at[3 + i], p.mirror(i))
    for i in (1, 3, 2):
        net.send((tag, "x", i), src.at[zh * 4 + (x + i) % 4], rx.at[i - 1], p.at(x=i))
    yield
    net.need(*[(tag, "m", i) for i in range(4)], *[(tag, "x", i) for i in range(1, 4)])
    add_rows(total, src.at[p.f], [rx.at[i] for i in range(7)], 96)


def y_flow(net, p, tag, g, bufs, total, width, begin):
    rc, rh1, rh3, rw1, rw3, rx = bufs
    part = g.at[:, :, :, pl.ds(begin, 4 * width)] if begin else g
    yield from ring_sum_flow(
        net,
        p,
        tag,
        part,
        rc,
        rh1,
        rh3,
        rw1,
        rw3,
        lambda i: p.at(y=i),
        lambda i: (0, lanes((p.y + i) % 4, width)),
        8,
    )
    yield from cross_sum(net, p, tag, part.at[:, p.c, :, lanes(p.y, width)], rx, total)


def y_direct_flow(net, p, tag, g, bufs, total, width, begin):
    rc, ry, rx = bufs
    part = g.at[:, :, :, pl.ds(begin, 4 * width)]
    mine, theirs = part.at[:, p.c], part.at[:, 1 - p.c]
    for i in (2, 1, 3, 0):
        cols = lanes((p.y + i) % 4, width)
        net.send((tag, "c", i), theirs.at[:, :, cols], rc.at[:, :, cols], p.at(c=1))
    yield
    for i in (2, 1, 3, 0):
        cols = lanes((p.y + i) % 4, width)
        block = mine.at[:, :, cols]
        net.need((tag, "c", i))

        def near(k):
            add_rows(block.at[k], block.at[k], [rc.at[k, :, cols]], 96)

        each(8, near)
        if i:
            net.send((tag, "w", i), block, ry.at[i - 1], p.at(y=i))
    yield
    block = mine.at[:, :, lanes(p.y, width)]
    net.need(*[(tag, "w", i) for i in (1, 3, 2)])

    def whole(k):
        add_rows(block.at[k], block.at[k], [ry.at[i, k] for i in range(3)], 96)

    each(8, whole)
    yield from cross_sum(net, p, tag, block, rx, total)


def tp_scatter(net, p, tag, totals, pads, fins, to):
    t = p.t
    at = 0
    for total in totals:
        width = total.shape[1]
        for i in range(8):
            pads[i, pl.ds(0, 12), pl.ds(at, width)] = total[pl.ds(12 * i, 12), :].astype(BF)
            pads[i, pl.ds(12, 4), pl.ds(at, width)] = jnp.zeros((4, width), BF)
        at += width
    for i in range(1, 8):
        net.send((tag, "f", i), pads.at[(t + i) % 8], fins.at[t], to[i - 1])
    fins[t] = pads[t]


def norm_back_rows(grad, values, gain, base, out, grad_gain):
    grad_gain[...] = jnp.zeros_like(grad_gain)

    def body(i):
        at = pl.ds(pl.multiple_of(i * 16, 16), 16)
        v = values[at, :].astype(F32)
        g = grad[at, :]
        r = lax.rsqrt(jnp.mean(v * v, axis=-1, keepdims=True) + norm_eps)
        a = g * gain
        grad_gain[...] += jnp.sum(g * v * r, axis=0, keepdims=True)
        back = r * a - v * r * r * r * jnp.mean(a * v, axis=-1, keepdims=True)
        out[at, :] = base[at, :].astype(F32) + back

    each(grad.shape[0] // 16, body)


def backward_kernel(*refs):
    ga, gb, hp, w2t, w1, probs = refs[:6]
    near_in = refs[6:17]
    h_out, grad_in, o1, o2, oa, ob, small = refs[17:24]
    rest = list(refs[24:])

    def take(n):
        out = rest[:n]
        del rest[:n]
        return out

    near = take(11)
    gn, middle, cot, hidden_in, normed, attended, queries, kv, cos, sin, gains = near
    m_bufs = [take(6), take(6)]
    q_bufs, q_total = take(6), take(1)[0]
    o_bufs, o_total = take(6), take(1)[0]
    r_bufs, r_total = take(6), take(1)[0]
    v_bufs, v_total = take(3), take(1)[0]
    hp_bufs, hp_own = take(12), take(1)[0]
    kv_bufs, kv_part, kv_sum = take(9), take(1)[0], take(1)[0]
    rcs, rs1, rs2, rs3 = take(4)
    pad_q, fin_q, pad_v, fin_v = take(4)
    wide, deep, g1, g_mid, g_proj, g_att, g_qkv, stack_q, stack_a = take(9)
    gain_two, gain_one, part_small, gno = take(4)
    send_sems, recv_sems, local_sems, hp_sems, load_sems = take(5)

    p = Place()
    t = p.t
    tp_all = [{FS: p.f, CX: p.c, TP: (t + i) % 8} for i in range(1, 8)]
    loads = Loads(load_sems)
    for i in (0, 1, 2, 10):
        loads.start(i, near_in[i], near[i])
    loads.start("w", w2t, wide)
    loads.start("p", probs, deep)
    for i in (5, 7, 6, 8, 9, 4, 3):
        loads.start(i, near_in[i], near[i])
    greet(
        [p.at(c=1)] + [p.at(x=i) for i in (1, 2, 3)] + tp_all + [p.at(z=2)]
        + [p.mirror(i) for i in range(4)]
    )
    net = Net(send_sems, recv_sems)
    steps = Steps(BACKWARD_ORDER)
    steps.add("a", weight_flow(net, p, "a", ga, *m_bufs[0], oa, local_sems.at[0]))
    steps.add("b", weight_flow(net, p, "b", gb, *m_bufs[1], ob, local_sems.at[1]))
    flow_h = tp_sum_flow(
        net, p, "h", hp, h_out, hp_bufs, 2, loads=(hp_own, hp_sems), base=middle
    )
    steps.add("h", flow_h)
    steps.point()
    loads.need(0, 1, 2, 10)
    norm_back_rows(gn, middle, gains[pl.ds(1, 1), :], cot, g_mid, gain_two)
    g_proj[...] = g_mid[...].astype(BF)
    steps.point()
    loads.need("w")

    def grad_attended(j):
        at = pl.ds(pl.multiple_of(j * 512, 512), 512)
        g_att[:, at] = dots(g_proj[...], wide[:, at], 1, 0).astype(BF)

    each(3, grad_attended)
    steps.point()
    loads.need(5)

    def grad_out(j):
        at = pl.ds(pl.multiple_of(j * 384, 128), 384)
        wide[at, :] = dots(g_proj[:, at], attended[...], 0, 0).astype(BF)

    each(4, grad_out)
    steps.add("o", y_flow(net, p, 2, wide.reshape(8, 2, 96, 1536), o_bufs, o_total, 384, 0))
    steps.point()
    loads.need("p", 7, 6)
    size = HEAD_SIZE
    scale = size**-0.5

    def stack(h):
        at = pl.ds(pl.multiple_of(h * size, size), size)
        stack_q[at, :] = queries[:, at]
        stack_a[at, :] = g_att[:, at]

    each(QUERY_HEADS, stack)
    group_rows = [pl.ds(768 * group, 768) for group in range(KEY_VALUE_HEADS)]

    def sums(left, right, first, factor):
        def body(j):
            at = pl.ds(pl.multiple_of(j * 256, 256), 256)
            for group, rows in enumerate(group_rows):
                grad = dots(left[rows, at], right[rows, :], 0, 0) * factor
                to = pl.ds((first + group) * size, size)
                kv_part[pl.ds(j * 2, 2), :, to] = grad.astype(BF).reshape(2, 128, size)

        each(4, body)

    sums(deep, stack_a, KEY_VALUE_HEADS, 1.0)
    steps.point()
    for group in range(KEY_VALUE_HEADS):
        values = kv.at[:, pl.ds((KEY_VALUE_HEADS + group) * size, size)]

        def heads(j):
            at = pl.ds(pl.multiple_of(group * 768 + j * 256, 256), 256)
            grad = dots(stack_a[at, :], values[...], 1, 1)
            weight = deep[at, :].astype(F32)
            inner = jnp.sum(weight * grad, axis=-1, keepdims=True)
            deep[at, :] = (weight * (grad - inner)).astype(BF)

        each(3, heads)
        steps.point()
    sums(deep, stack_q, 0, scale)
    steps.add("k", short_sum_flow(net, p, "k", kv_part, kv_sum, kv_bufs, 1))
    steps.point()
    loads.need(8, 9)

    def turned_back(grad):
        return (grad * cos[...] - pltpu.roll(grad, size // 2, 1) * sin[...]).astype(BF)

    for group in range(KEY_VALUE_HEADS):
        keys = kv.at[:, pl.ds(group * size, size)]

        def grad_query(j):
            at = pl.ds(pl.multiple_of(group * 768 + j * 256, 256), 256)
            grad = dots(deep[at, :], keys[...], 1, 0) * scale
            for i in range(2):
                to = pl.ds(pl.multiple_of((group * 6 + j * 2 + i) * size, size), size)
                g_qkv[:, to] = turned_back(grad[i * size : (i + 1) * size])

        each(3, grad_query)
        steps.point()
    loads.start("u", w1.at[:, pl.ds(0, 1024)], deep)
    loads.need(4)

    def grad_w(begin, count):
        at = pl.ds(begin, count)

        def body(j):
            d = pl.ds(pl.multiple_of(j * 384, 128), 384)
            total = dots(normed[:, d], g_qkv[:, at], 0, 0)
            g1[pl.ds(j * 2, 2), :, :, at] = total.astype(BF).reshape(2, 2, 96, count)

        each(4, body)

    grad_w(0, 1024)
    steps.add("q", z_flow(net, p, 1, g1, q_bufs, q_total, 512))
    steps.point()
    grad_w(1024, 512)
    steps.add("r", y_flow(net, p, 3, g1, r_bufs, r_total, 128, 1024))
    for _ in range(8):
        steps.point()
    steps.finish("k")
    for i in range(KEY_VALUE_HEADS):
        at, to = pl.ds(i * size, size), pl.ds((QUERY_HEADS + i) * size, size)
        g_qkv[:, to] = turned_back(kv_sum[:, at])
    at = pl.ds((QUERY_HEADS + KEY_VALUE_HEADS) * size, KEY_VALUE_HEADS * size)
    g_qkv[:, at] = kv_sum[:, pl.ds(KEY_VALUE_HEADS * size, KEY_VALUE_HEADS * size)].astype(BF)
    grad_w(1536, 512)
    steps.add("v", y_direct_flow(net, p, 4, g1, v_bufs, v_total, 128, 1536))
    for _ in range(4):
        steps.point()

    def normed_back(i):
        def body(j):
            at = pl.ds(pl.multiple_of(j * 512, 512), 512)
            total = dots(g_qkv[:, pl.ds(1024 * i, 1024)], deep[at, :], 1, 1)
            gno[:, at] = total if i == 0 else gno[:, at] + total

        each(3, body)

    loads.need("u")
    normed_back(0)
    loads.start("v", w1.at[:, pl.ds(1024, 1024)], deep)
    for _ in range(4):
        steps.point()
    loads.need("v")
    normed_back(1)
    loads.need(3)
    steps.point()
    norm_back_rows(gno, hidden_in, gains[pl.ds(0, 1), :], g_mid, grad_in, gain_one)
    bias = jnp.sum(g_qkv[...].astype(F32), axis=0, keepdims=True)
    for i in range(16):
        part_small[pl.ds(i, 1), :] = bias[:, i * 128 : i * 128 + 128]
    for i in range(12):
        part_small[pl.ds(16 + i, 1), :] = gain_one[:, pl.ds(i * 128, 128)]
        part_small[pl.ds(28 + i, 1), :] = gain_two[:, pl.ds(i * 128, 128)]
    steps.add("t", small_flow(net, p, part_small, small, rcs, (rs1, rs2, rs3)))
    for _ in range(14):
        steps.point()
    steps.finish("v")
    tp_scatter(net, p, 4, [v_total], pad_v, fin_v, tp_all)
    for _ in range(10):
        steps.point()
    steps.finish("q", "r", "o")
    tp_scatter(net, p, 2, [q_total, r_total, o_total], pad_q, fin_q, tp_all)
    for _ in range(8):
        steps.point()
    steps.finish("t", "a", "b", "h")
    net.need(*[(2, "f", i) for i in range(1, 8)])
    for k in range(2):
        at = pl.ds(0, 512)
        total = fin_q[k, :, at].astype(F32)
        for yy in range(1, 4):
            total += fin_q[2 * yy + k, :, at].astype(F32)
        o1[:, pl.ds(512 * k, 512)] = total
    for yy in range(4):
        at = pl.ds(512, 128)
        total = fin_q[2 * yy, :, at].astype(F32) + fin_q[2 * yy + 1, :, at].astype(F32)
        o1[:, pl.ds(1024 + 128 * yy, 128)] = total
        at = pl.ds(640, 384)
        total = fin_q[2 * yy, :, at].astype(F32) + fin_q[2 * yy + 1, :, at].astype(F32)
        o2[:, pl.ds(384 * yy, 384)] = total
    net.need(*[(4, "f", i) for i in range(1, 8)])
    for yy in range(4):
        total = fin_v[2 * yy].astype(F32) + fin_v[2 * yy + 1].astype(F32)
        o1[:, pl.ds(1536 + 128 * yy, 128)] = total
    net.finish()


def backward(far, near, cid=1, name="backward"):
    vm = pl.BlockSpec(memory_space=pltpu.VMEM)
    hbm = pl.BlockSpec(memory_space=pl.ANY)
    V = lambda *s: pltpu.VMEM(s, BF)
    W = lambda *s: pltpu.VMEM(s, F32)
    scratch = [pltpu.VMEM(a.shape, a.dtype) for a in near]
    for w in (far[0].shape[-1], far[1].shape[-1]):
        scratch += [
            V(8, 96, w), V(2, 48, w), V(2, 48, w), V(2, 96, w), V(2, 96, w), V(96, w),
        ]
    scratch += [
        V(8, 96, 1024), V(4, 48, 512), V(4, 48, 512), V(4, 96, 512), V(4, 96, 512), V(3, 96, 512),
        W(96, 512),
    ]
    for w in (384, 128):
        scratch += [
            V(8, 96, 4 * w), V(8, 48, w), V(8, 48, w), V(8, 96, w), V(8, 96, w), V(7, 96, w), W(96, w),
        ]
    scratch += [V(8, 96, 512), V(3, 8, 96, 128), V(7, 96, 128), W(96, 128)]
    whole, half = V(128, 1536), V(64, 1536)
    scratch += [whole] * 3 + [half] * 2 + [whole] * 7 + [whole]
    scratch += [V(128, 512)] * 9 + [V(8, 128, 512), W(128, 512)]
    scratch += [W(40, 128)] + [W(4, 40, 128)] * 3
    scratch += [V(8, 16, 1024)] * 2 + [V(8, 16, 128)] * 2
    scratch += [
        V(1536, 1536), V(1536, 1024), V(8, 2, 96, 2048), W(128, 1536), V(128, 1536), V(128, 1536),
        V(128, 2048), V(1536, 128), V(1536, 128),
        W(1, 1536), W(1, 1536), W(40, 128), W(128, 1536),
    ]
    n = 140
    D = pltpu.SemaphoreType.DMA
    scratch += [D((n,)), D((n,)), D((2,)), D((5,)), D((16,))]
    S = lambda *s: jax.ShapeDtypeStruct(s, F32)
    return pl.pallas_call(
        backward_kernel,
        out_shape=(
            S(128, 1536), S(128, 1536), S(16, 2048), S(16, 1536),
            S(96, far[0].shape[-1]), S(96, far[1].shape[-1]), S(40, 128),
        ),
        in_specs=[hbm] * (len(far) + len(near)),
        out_specs=(vm,) * 7,
        scratch_shapes=scratch,
        name=name,
        compiler_params=pltpu.CompilerParams(
            collective_id=cid, has_side_effects=True, vmem_limit_bytes=62 << 20
        ),
    )(*far, *near)


def gather_rows_flow(net, p, tag, own, pad):
    t, tq = p.t, p.y * 2 + 1 - p.zl
    net.send((tag, "z"), own, pad.at[t], p.partner())
    for i in (1, 3, 2):
        net.send((tag, "y", i), own, pad.at[t], p.at(y=i))
    yield
    net.need((tag, "z"))
    for i in (1, 3, 2):
        net.send((tag, "p", i), pad.at[tq], pad.at[tq], p.at(y=i))
    yield
    net.need(*[(tag, k, i) for k in "yp" for i in (1, 2, 3)])


def close_up(pad, wide, blk):
    width = pad.shape[-1]
    for i in range(8):
        wide[pl.ds(12 * i, 12), pl.ds(0, width)] = pad[i, pl.ds(0, 12), :].astype(F32)
    blk[...] = wide[:, pl.ds(0, width)].astype(BF)


def cross_sends(net, p, tag, src, place):
    for i in (1, 3, 2):
        net.send((tag, "x", i), src, place, p.at(x=i))
    for i in (0, 1, 3, 2):
        net.send((tag, "m", i), src, place, p.mirror(i))


def cross_names(tag):
    return [(tag, "x", i) for i in (1, 2, 3)] + [(tag, "m", i) for i in range(4)]


def ring_gather_flow(net, p, tag, w, ring, block, count):
    c = p.c
    top, low = pl.ds(0, 48), pl.ds(48, 48)

    def part(i, rows=None):
        first, cols = block(i)
        if rows is None:
            return w.at[pl.ds(first, count), c, :, cols]
        return w.at[pl.ds(first, count), c, rows, cols]

    sib = p.at(c=1)
    net.send((tag, "r", 1), part(0), part(0), ring(1))
    net.send((tag, "r", 3), part(0), part(0), ring(3))
    net.send((tag, "c", 0), part(0), part(0), sib)
    yield
    net.need((tag, "r", 1), (tag, "r", 3))
    net.send((tag, "f", 1), part(3, top), part(3, top), ring(1))
    net.send((tag, "f", 3), part(1, low), part(1, low), ring(3))
    net.send((tag, "c", 3), part(3), part(3), sib)
    net.send((tag, "c", 1), part(1), part(1), sib)
    yield
    net.need((tag, "f", 1), (tag, "f", 3))
    net.send((tag, "c", 2), part(2), part(2), sib)
    yield
    net.need(*[(tag, "c", i) for i in range(4)])


def weights_flow(net, p, m_in, mw):
    f, c, x, zh = p.f, p.c, p.x, p.zh
    top, low = pl.ds(0, 48), pl.ds(48, 48)
    sib = p.at(c=1)
    far = (1 - zh) * 4 + x

    def across(k, ff):
        net.send(("m", "c", k), mw.at[ff, c], mw.at[ff, c], sib)

    def ring(tag, src, ff):
        net.send((tag, "r", 0), src.at[top], mw.at[ff, c, top], p.at(x=1))
        net.send((tag, "l", 1), src.at[low], mw.at[ff, c, low], p.at(x=3))
        yield
        net.send((tag, "r", 1), src.at[low], mw.at[ff, c, low], p.at(x=1))
        net.send((tag, "l", 0), src.at[top], mw.at[ff, c, top], p.at(x=3))
        yield

    def onward(tag, side, k):
        after, before = side * 4 + (x + 1) % 4, side * 4 + (x + 3) % 4
        net.need((tag, "r", 0), (tag, "l", 1))
        ref = mw.at[before, c, top]
        net.send((tag, "f", 1), ref, ref, p.at(x=1))
        ref = mw.at[after, c, low]
        net.send((tag, "f", 3), ref, ref, p.at(x=3))
        yield
        net.need((tag, "r", 1), (tag, "l", 0))
        across(k, before)
        across(k + 1, after)
        yield
        net.need((tag, "f", 1), (tag, "f", 3))
        across(k + 2, side * 4 + (x + 2) % 4)
        yield

    net.send(("m", "z"), m_in, mw.at[f, c], p.at(z=2))
    yield
    yield from ring("m", m_in, f)
    net.send(("m", "c", 0), m_in, mw.at[f, c], sib)
    net.need(("m", "z"))
    yield from ring("n", mw.at[far, c], far)
    yield from onward("m", zh, 1)
    across(4, far)
    yield from onward("n", 1 - zh, 5)
    net.need(*[("m", "c", k) for k in range(8)])


def cotangent_flow(net, p, own, out):
    y, zl, t = p.y, p.zl, p.t
    tq = y * 2 + 1 - zl
    zp = p.partner()
    top, low = pl.ds(0, 64), pl.ds(64, 64)
    net.send(("g", "r", 0), own.at[top], out.at[t, top], p.at(y=1))
    net.send(("g", "l", 1), own.at[low], out.at[t, low], p.at(y=3))
    yield
    net.send(("g", "r", 1), own.at[low], out.at[t, low], p.at(y=1))
    net.send(("g", "l", 0), own.at[top], out.at[t, top], p.at(y=3))
    yield
    net.send(("g", "z"), own, out.at[t], zp)
    yield
    net.need(("g", "r", 0), ("g", "l", 1))
    ref = out.at[((y + 3) % 4) * 2 + zl, top]
    net.send(("g", "f", 1), ref, ref, p.at(y=1))
    ref = out.at[((y + 1) % 4) * 2 + zl, low]
    net.send(("g", "f", 3), ref, ref, p.at(y=3))
    yield
    net.need(("g", "z"))
    for i in (2, 1, 3):
        net.send(("g", "p", i), out.at[tq], out.at[tq], p.at(y=i))
    yield
    net.need(*[("g", k, i) for k, i in (("r", 1), ("l", 0), ("f", 1), ("f", 3))])
    net.need(*[("g", "p", i) for i in (1, 2, 3)])


def forward_kernel(*refs):
    q_in, o_in, g_in, m_in, c_in, hidden_in, bias_in, cos_in, sin_in, mask_in = refs[:10]
    w1, w2, mw, cg, probs, normed, queries, keys_values, attended, middle, normed_two, gains = refs[
        10:22
    ]
    (
        w_q, w_o, w_g, hid, bias, cos, sin, mask, pad1, pad2, wide, wide2, blk1, blk2,
        w1v, w2v, gn, kv, kv_own, prob, stack, nrm, m_own, c_own,
        a1, a2, tile, send_sems, recv_sems, load_sems, store_sems,
    ) = refs[22:]
    p = Place()
    f, c, t, y, zl, zh = p.f, p.c, p.t, p.y, p.zl, p.zh
    loads, stores = Loads(load_sems), Loads(store_sems)
    loads.start("a", q_in, w_q)
    loads.start("n", g_in, w_g)
    loads.start("o", o_in, w_o)
    loads.start("m", m_in, m_own)
    loads.start("g", c_in, c_own)
    for name, src, dst in (
        ("h", hidden_in, hid), ("b", bias_in, bias), ("c", cos_in, cos), ("s", sin_in, sin),
        ("k", mask_in, mask),
    ):
        loads.start(name, src, dst)
    greet(
        [p.at(c=1)]
        + [p.at(x=i) for i in (1, 2, 3)]
        + [p.at(y=i) for i in (1, 2, 3)]
        + [p.at(z=i) for i in (1, 2, 3)]
        + [p.mirror(i) for i in (1, 2, 3)]
    )
    net = Net(send_sems, recv_sems)
    steps = Steps(FORWARD_ORDER)
    tile[...] = jnp.zeros_like(tile)
    loads.need("a", "n")
    tile[pl.ds(0, 2), pl.ds(0, 12)] = w_g[...]
    wide[pl.ds(0, 16), pl.ds(2048, 128)] = tile[...].T[:16]
    wide[pl.ds(0, 12), pl.ds(0, 2048)] = w_q[...]
    wide[pl.ds(12, 4), pl.ds(0, 2048)] = jnp.zeros((4, 2048), F32)
    a1[...] = wide[pl.ds(0, 16), :].astype(BF)
    z_cols, o_cols = lanes(zl, 512), lanes(zl, 768)
    q_part, kv_part = pl.ds(0, 1536), pl.ds(1536, 640)
    x_three = (1, 3, 2)
    rows_1 = gather_rows_flow(net, p, "e", a1.at[:, kv_part], pad1.at[:, :, kv_part])
    next(rows_1)
    pad1[t] = a1[...]
    loads.need("m", "g")
    stores.start("m", m_own, mw.at[f, c])
    stores.start("g", c_own, cg.at[t])

    def z_block(width):
        def block(i):
            zz = (p.z + i) % 4
            return (zz // 2) * 4, lanes(zz % 2, width)

        return block

    def y_flow_of(tag, begin):
        def cols(i):
            return pl.ds(pl.multiple_of(begin + ((y + i) % 4) * 128, 128), 128)

        cross_sends(net, p, tag, blk1.at[:, cols(0)], w1v.at[f, c, :, cols(0)])
        w1v[f, c, :, cols(0)] = blk1[:, cols(0)]
        yield
        net.need(*cross_names(tag))
        yield from ring_gather_flow(
            net, p, tag + 1, w1v, lambda i: p.at(y=i), lambda i: (0, cols(i)), 8
        )

    def query_flow():
        rows = gather_rows_flow(net, p, "a", a1.at[:, q_part], pad1.at[:, :, q_part])
        yield from rows
        close_up(pad1.at[:, :, q_part], wide, blk1.at[:, q_part])
        for i in x_three:
            net.send((1, "x", i), blk1.at[:, z_cols], w1v.at[f, c, :, z_cols], p.at(x=i))
        w1v[f, c, :, z_cols] = blk1[:, z_cols]
        steps.add("2", y_flow_of(10, 1024))
        yield
        net.need(*[(1, "x", i) for i in x_three])
        yield from ring_gather_flow(net, p, 4, w1v, lambda i: p.at(z=i), z_block(512), 4)

    def gains_flow():
        for i in x_three:
            net.send((3, "x", i), blk1.at[:, pl.ds(2048, 128)], gn.at[f, c], p.at(x=i))
        gn[f, c] = blk1[:, pl.ds(2048, 128)]
        yield
        net.need(*[(3, "x", i) for i in x_three])
        own_zh = pl.ds(zh * 4, 4)
        net.send((3, "m"), gn.at[own_zh, c], gn.at[own_zh, c], p.mirror())
        yield
        net.need((3, "m"))
        net.send((3, "c"), gn.at[:, c], gn.at[:, c], p.at(c=1))
        yield
        net.need((3, "c"))
        gains[...] = gn[...].reshape(1536, 128).astype(F32).T[:2]

    def out_flow():
        loads.need("o")
        wide2[pl.ds(0, 12), :] = w_o[...]
        wide2[pl.ds(12, 4), :] = jnp.zeros((4, 1536), F32)
        a2[...] = wide2[pl.ds(0, 16), :].astype(BF)
        rows = gather_rows_flow(net, p, "b", a2, pad2)
        next(rows)
        pad2[t] = a2[...]
        yield
        yield from rows
        close_up(pad2, wide2, blk2)
        for i in x_three:
            net.send((6, "x", i), blk2.at[:, o_cols], w2v.at[f, c, :, o_cols], p.at(x=i))
        w2v[f, c, :, o_cols] = blk2[:, o_cols]
        yield
        net.need(*[(6, "x", i) for i in x_three])
        yield from ring_gather_flow(net, p, 7, w2v, lambda i: p.at(z=i), z_block(768), 4)

    steps.add("m", weights_flow(net, p, m_in, mw))
    steps.add("c", cotangent_flow(net, p, c_in, cg))
    steps.add("o", out_flow())
    steps.add("1", query_flow())
    steps.point()
    next(rows_1)
    steps.point()
    next(rows_1, None)
    close_up(pad1.at[:, :, kv_part], wide, blk1.at[:, kv_part])
    steps.add("v", y_flow_of(12, 1536))
    steps.add("g", gains_flow())
    for _ in range(10):
        steps.point()
    steps.finish("g")
    loads.need("h")

    def norm_one(i):
        at = pl.ds(pl.multiple_of(i * 16, 16), 16)
        v = hid[at, :].astype(F32)
        r = lax.rsqrt(jnp.mean(v * v, axis=-1, keepdims=True) + norm_eps)
        nrm[at, :] = (v * r * gains[pl.ds(0, 1), :]).astype(BF)

    each(8, norm_one)
    stores.start("n", nrm, normed)
    for _ in range(8):
        steps.point()
    steps.finish("v")
    steps.point()
    loads.need("b", "c", "s")
    size = HEAD_SIZE
    weights = w1v.reshape(1536, 2048)

    def project(first, count):
        total = dots(nrm[...], weights[:, pl.ds(first * size, count * size)], 1, 0)
        return [
            total[:, i * size : (i + 1) * size] + bias[pl.ds(first + i, 1), :].astype(BF).astype(F32)
            for i in range(count)
        ]

    def turn(value):
        return (value * cos[...] + pltpu.roll(value, size // 2, 1) * sin[...]).astype(BF)

    for i, value in enumerate(project(QUERY_HEADS, 2 * KEY_VALUE_HEADS)):
        kv_own[:, pl.ds(i * size, size)] = turn(value) if i < KEY_VALUE_HEADS else value.astype(BF)
    kv[t] = kv_own[...]

    def keys_flow():
        zp, tq = p.partner(), y * 2 + 1 - zl
        net.send(("k", "z"), kv_own, kv.at[t], zp)
        for i in (2, 1, 3):
            net.send(("k", "y", i), kv_own, kv.at[t], p.at(y=i))
        yield
        net.need(("k", "z"))
        for i in (2, 1, 3):
            net.send(("k", "p", i), kv.at[tq], kv.at[tq], p.at(y=i))
        yield
        net.need(*[("k", k, i) for k in "yp" for i in (1, 2, 3)])

    steps.add("k", keys_flow())
    for _ in range(10):
        steps.point()
    steps.finish("1", "2")
    stores.start(1, w1v, w1)
    for j in range(3):
        for i, value in enumerate(project(j * 4, 4)):
            stack[pl.ds((j * 4 + i) * size, size), :] = turn(value)
        steps.point()
    for _ in range(4):
        steps.point()
    steps.finish("k")
    loads.need("k")
    stores.start("k", kv, keys_values)
    scale = size**-0.5
    for group in range(KEY_VALUE_HEADS):
        at_k, at_v = pl.ds(group * size, size), pl.ds((KEY_VALUE_HEADS + group) * size, size)

        def heads(j):
            rows = pl.ds(pl.multiple_of(group * 768 + j * 256, 256), 256)
            keys = kv[:, :, at_k].reshape(1024, size)
            values = kv[:, :, at_v].reshape(1024, size)
            score = dots(stack[rows, :], keys, 1, 1).reshape(2, 128, 1024) * scale
            score = jnp.where(mask[...][None] > 0.0, score, -1e30)
            top = jnp.max(score, axis=-1, keepdims=True)
            power = jnp.exp(score - top)
            share = power * (1.0 / jnp.sum(power, axis=-1, keepdims=True))
            share = share.astype(BF).reshape(256, 1024)
            prob[rows, :] = share
            total = dots(share, values, 1, 0).astype(BF)
            for i in range(2):
                head = group * 6 + j * 2 + i
                to = pl.ds(pl.multiple_of(head * size, size), size)
                attended[:, to] = total[i * size : (i + 1) * size]
                queries[:, to] = stack[pl.ds(pl.multiple_of(head * size, size), size), :]

        each(3, heads)
        steps.point()
    stores.start("p", prob, probs)
    for _ in range(6):
        steps.point()
    steps.finish("o")
    stores.start(2, w2v, w2)
    out_weights = w2v.reshape(1536, 1536)

    def project_out(j):
        at = pl.ds(pl.multiple_of(j * 512, 512), 512)
        middle[:, at] = hid[:, at].astype(F32) + dots(attended[...], out_weights[at, :], 1, 1)

    each(3, project_out)
    steps.point()

    def norm_two(i):
        at = pl.ds(pl.multiple_of(i * 16, 16), 16)
        v = middle[at, :]
        r = lax.rsqrt(jnp.mean(v * v, axis=-1, keepdims=True) + norm_eps)
        normed_two[at, :] = (v * r * gains[pl.ds(1, 1), :]).astype(BF)

    each(8, norm_two)
    for _ in range(6):
        steps.point()
    steps.finish("c", "m")
    net.finish()
    stores.need("m", "g", "n", 1, "k", "p", 2)


def forward(*args, cid=0, name="forward"):
    vm = pl.BlockSpec(memory_space=pltpu.VMEM)
    hbm = pl.BlockSpec(memory_space=pl.ANY)
    V = lambda *s: pltpu.VMEM(s, BF)
    W = lambda *s: pltpu.VMEM(s, F32)
    B = lambda *s: jax.ShapeDtypeStruct(s, BF)
    S = lambda *s: jax.ShapeDtypeStruct(s, F32)
    D = pltpu.SemaphoreType.DMA
    n = 130
    return pl.pallas_call(
        forward_kernel,
        out_shape=(
            B(8, 2, 96, 2048), B(8, 2, 96, 1536), B(8, 2, 96, 3 * FF_PAD), B(8, 128, 1536),
            B(1536, 1024), B(128, 1536), B(128, 1536), B(8, 128, 512), B(128, 1536),
            S(128, 1536), B(128, 1536), S(2, 1536),
        ),
        in_specs=[hbm] * len(args),
        out_specs=(hbm,) * 6 + (vm, hbm) + (vm,) * 4,
        scratch_shapes=[pltpu.VMEM(args[i].shape, args[i].dtype) for i in (0, 1, 2, 5, 6, 7, 8, 9)]
        + [
            V(8, 16, 2176), V(8, 16, 1536), W(96, 2176), W(96, 1536), V(96, 2176), V(96, 1536),
            V(8, 2, 96, 2048), V(8, 2, 96, 1536), V(8, 2, 96, 128), V(8, 128, 512), V(128, 512),
            V(1536, 1024), V(1536, 128), V(128, 1536), V(96, 3 * FF_PAD), V(128, 1536),
            V(16, 2176), V(16, 1536), W(128, 128),
            D((n,)), D((n,)), D((10,)), D((7,)),
        ],
        name=name,
        compiler_params=pltpu.CompilerParams(
            collective_id=cid, has_side_effects=True, vmem_limit_bytes=60 << 20
        ),
    )(*args)


def doc_layout(lengths, places):
    ends = jnp.cumsum(lengths)
    starts = ends - lengths
    doc_ids = jnp.sum((ends[None, :] <= places[:, None]).astype(jnp.int32), axis=1)
    doc_start = jnp.max(jnp.where(starts[None, :] <= places[:, None], starts[None, :], 0), axis=1)
    return (doc_ids, places - doc_start)


def rotary_tables(position, size):
    half = size // 2
    lane = jnp.arange(size, dtype=jnp.int32)
    freq = jnp.exp((lane % half).astype(F32) * (-2.0 * math.log(rope_base) / size))
    angle = position.astype(F32)[:, None] * freq[None, :]
    return (jnp.cos(angle), jnp.where(lane < half, -1.0, 1.0)[None, :] * jnp.sin(angle))


def adam_step(weight, moment, second, grad, rate, decay):
    moment = beta_one * moment + (1.0 - beta_one) * grad
    second = beta_two * second + (1.0 - beta_two) * grad * grad
    fix_one = 1.0 - beta_one**STEP
    fix_two = 1.0 - beta_two**STEP
    direction = moment / fix_one / (jnp.sqrt(second / fix_two) + adam_eps)
    return (weight - rate * (direction + decay * weight), moment, second)


def on_device(
    hidden_in,
    cotangent,
    seq_lengths,
    w_qkv,
    m_qkv,
    v_qkv,
    b_qkv,
    m_bias,
    v_bias,
    w_out,
    m_out,
    v_out,
    w_gate_up,
    m_gate_up,
    v_gate_up,
    w_down,
    m_down,
    v_down,
    gains,
    m_gains,
    v_gains,
):
    token_rows = hidden_in.shape[0]
    model_width = hidden_in.shape[1]
    tp_count = lax.axis_size(TP)
    packed_length = token_rows * tp_count
    ff_dev = w_gate_up.shape[2]
    own_places = lax.axis_index(TP) * token_rows + jnp.arange(token_rows, dtype=jnp.int32)
    key_places = jnp.arange(packed_length, dtype=jnp.int32)
    own_docs, own_pos = doc_layout(seq_lengths[0], own_places)
    key_docs = doc_layout(seq_lengths[0], key_places)[0]
    allowed = (own_docs[:, None] == key_docs[None, :]) & (
        key_places[None, :] <= own_places[:, None]
    )
    cos_row, sin_row = rotary_tables(own_pos, HEAD_SIZE)
    side = ((0, 0), (0, FF_PAD - ff_dev))
    mlp_shard = jnp.concatenate(
        [
            jnp.pad(w_gate_up[:, 0].astype(BF), side),
            jnp.pad(w_gate_up[:, 1].astype(BF), side),
            jnp.pad(w_down.astype(BF).T, side),
        ],
        axis=1,
    )
    (
        qkv_full, out_turned, mlp_full, grad_group,
        probs, normed_one, queries, keys_values, attended, middle, normed_two, gains_full,
    ) = forward(
        w_qkv,
        w_out.T,
        gains,
        mlp_shard,
        cotangent,
        hidden_in,
        b_qkv.reshape(-1, 128),
        cos_row,
        sin_row,
        allowed.astype(F32),
    )
    grad_normed_two, down_parts, grad_w_gate_up, grad_w_down = feed_forward(
        normed_two, grad_group, mlp_full.reshape(model_width, -1)
    )
    hidden_out, grad_in, owned_qkv, owned_out, owned_gate_up, owned_down, small = backward(
        [
            grad_w_gate_up,
            grad_w_down,
            down_parts,
            out_turned.reshape(model_width, -1),
            qkv_full.reshape(model_width, -1),
            probs,
        ],
        [
            grad_normed_two,
            middle,
            cotangent,
            hidden_in,
            normed_one,
            attended,
            queries,
            keys_values.reshape(packed_length, -1),
            cos_row,
            sin_row,
            gains_full,
        ],
    )
    small = small.reshape(-1)
    summed_bias = small[: b_qkv.shape[0]]
    summed_gains = small[b_qkv.shape[0] :].reshape(2, model_width)
    own_gains = gains.shape[1]
    owned_gains = lax.dynamic_slice_in_dim(
        summed_gains, lax.axis_index(ALL) * own_gains, own_gains, axis=1
    )
    own_rows = w_qkv.shape[0]
    owned_qkv = owned_qkv[:own_rows]
    owned_out = owned_out[:own_rows].T
    owned_gate_up = jnp.stack(
        [owned_gate_up[:, :ff_dev], owned_gate_up[:, FF_PAD : FF_PAD + ff_dev]], axis=1
    )
    owned_gate_up = with_layout_constraint(owned_gate_up, Layout((0, 1, 2)))
    owned_down = owned_down[:, :ff_dev].T
    qkv_new, qkv_moment, qkv_second = adam_step(
        w_qkv, m_qkv, v_qkv, owned_qkv, rate_qkv, weight_decay
    )
    bias_new, bias_moment, bias_second = adam_step(
        b_qkv, m_bias, v_bias, summed_bias, rate_small, 0.0
    )
    out_new, out_moment, out_second = adam_step(
        w_out, m_out, v_out, owned_out, rate_out, weight_decay
    )
    gate_up_new, gate_up_moment, gate_up_second = adam_step(
        w_gate_up, m_gate_up, v_gate_up, owned_gate_up, rate_gate_up, weight_decay
    )
    down_new, down_moment, down_second = adam_step(
        w_down, m_down, v_down, owned_down, rate_down, weight_decay
    )
    gains_new, gains_moment, gains_second = adam_step(
        gains, m_gains, v_gains, owned_gains, rate_small, 0.0
    )
    return (
        hidden_out,
        grad_in,
        qkv_new,
        qkv_moment,
        qkv_second,
        bias_new,
        bias_moment,
        bias_second,
        out_new,
        out_moment,
        out_second,
        gate_up_new,
        gate_up_moment,
        gate_up_second,
        down_new,
        down_moment,
        down_second,
        gains_new,
        gains_moment,
        gains_second,
    )


def solution(mesh):
    placed = (
        P((FS, CX, TP), None),
        P((FS, CX, TP), None),
        P((FS, CX), None),
        P((FS, CX, TP), None),
        P((FS, CX, TP), None),
        P((FS, CX, TP), None),
        P(),
        P(),
        P(),
        P(None, (FS, CX, TP)),
        P(None, (FS, CX, TP)),
        P(None, (FS, CX, TP)),
        P((FS, CX), None, TP),
        P((FS, CX), None, TP),
        P((FS, CX), None, TP),
        P(TP, (FS, CX)),
        P(TP, (FS, CX)),
        P(TP, (FS, CX)),
        P(None, (FS, CX, TP)),
        P(None, (FS, CX, TP)),
        P(None, (FS, CX, TP)),
    )
    return jax.shard_map(
        on_device,
        mesh=mesh,
        in_specs=placed,
        out_specs=(
            P((FS, CX, TP), None),
            P((FS, CX, TP), None),
            P((FS, CX, TP), None),
            P((FS, CX, TP), None),
            P((FS, CX, TP), None),
            P(),
            P(),
            P(),
            P(None, (FS, CX, TP)),
            P(None, (FS, CX, TP)),
            P(None, (FS, CX, TP)),
            P((FS, CX), None, TP),
            P((FS, CX), None, TP),
            P((FS, CX), None, TP),
            P(TP, (FS, CX)),
            P(TP, (FS, CX)),
            P(TP, (FS, CX)),
            P(None, (FS, CX, TP)),
            P(None, (FS, CX, TP)),
            P(None, (FS, CX, TP)),
        ),
        check_vma=False,
    )
```

```python
import functools
import math

import jax
import jax.numpy as jnp
from jax import lax
from jax.experimental import pallas as pl
from jax.experimental.pallas import tpu as pltpu
from jax.sharding import PartitionSpec as P

QUERY_HEADS = 12
KEY_VALUE_HEADS = 2
HEAD_SIZE = 128
STEP = 10


norm_eps = 1e-06
rope_base = 1000000.0
beta_one = 0.9
beta_two = 0.95
adam_eps = 1e-08
weight_decay = 0.1
rate_qkv = 0.05
rate_out = 0.3
rate_gate_up = 0.05
rate_down = 0.02
rate_small = 0.5

BF = jnp.bfloat16
F32 = jnp.float32
FS, CX, TP = ALL = ("fsdp", "ctx", "tp")
FF_PAD = 1152
FORWARD_ORDER = (
    "21mmc", "1", "gc", "", "oc", "v1", "mog", "v", "", "1g", "c", "", "2ov", "2", "", "", "",
    "", "m", "", "", "", "", "mvk", "", "m", "1", "", "k2", "cmo", "g", "", "o2", "mm", "",
    "m1", "", "", "", "1ov", "", "m", "", "k", "", "", "c", "m", "", "", "", "o", "",
)
BACKWARD_ORDER = (
    "babh", "", "", "oa", "h", "bo", "", "kb", "b", "", "qo", "k", "", "", "q", "k", "", "oa",
    "", "", "vq", "", "qa", "", "vkr", "", "", "ra", "tt", "", "oh", "", "", "", "r", "",
    "rvtqt", "h", "", "", "", "r", "v", "", "", "", "", "b", "r", "", "", "", "", "", "", "",
    "", "q", "", "taho",
)


class Place:
    def __init__(self):
        self.f = lax.axis_index(FS)
        self.c = lax.axis_index(CX)
        self.t = lax.axis_index(TP)
        self.zh, self.x = self.f // 4, self.f % 4
        self.y, self.zl = self.t // 2, self.t % 2
        self.z = self.zh * 2 + self.zl

    def at(self, x=0, y=0, z=0, c=0):
        zz = (self.z + z) % 4
        return {
            FS: (zz // 2) * 4 + (self.x + x) % 4,
            CX: (self.c + c) % 2,
            TP: ((self.y + y) % 4) * 2 + zz % 2,
        }

    def partner(self):
        return {FS: self.f, CX: self.c, TP: self.y * 2 + 1 - self.zl}

    def mirror(self, x=0):
        return {
            FS: (1 - self.zh) * 4 + (self.x + x) % 4,
            CX: self.c,
            TP: self.y * 2 + 1 - self.zl,
        }


def greet(devices):
    barrier = pltpu.get_barrier_semaphore()
    for device in devices:
        pl.semaphore_signal(barrier, inc=1, device_id=device, device_id_type=pl.DeviceIdType.MESH)
    pl.semaphore_wait(barrier, len(devices))


class Steps:
    def __init__(self, order):
        self.flows, self.order, self.at = {}, order, 0

    def add(self, name, flow):
        self.flows[name] = flow

    def point(self):
        for name in self.order[self.at]:
            if name in self.flows:
                next(self.flows[name], None)
        self.at += 1

    def finish(self, *names):
        for name in names:
            for _ in self.flows[name]:
                pass


class Loads:
    def __init__(self, sems):
        self.sems, self.used, self.copies = sems, 0, {}

    def start(self, name, src, dst):
        copy = pltpu.make_async_copy(src, dst, self.sems.at[self.used])
        self.used += 1
        copy.start()
        self.copies[name] = copy

    def need(self, *names):
        for name in names:
            self.copies.pop(name).wait()


class Net:
    def __init__(self, send_sems, recv_sems):
        self.send_sems, self.recv_sems = send_sems, recv_sems
        self.copies, self.arrived = {}, set()

    def send(self, name, src, dst, device, after=()):
        self.need(*after)
        at = len(self.copies)
        copy = pltpu.make_async_remote_copy(
            src_ref=src,
            dst_ref=dst,
            send_sem=self.send_sems.at[at],
            recv_sem=self.recv_sems.at[at],
            device_id=device,
            device_id_type=pl.DeviceIdType.MESH,
        )
        copy.start()
        self.copies[name] = copy

    def need(self, *names):
        for name in names:
            if name not in self.arrived:
                self.arrived.add(name)
                self.copies[name].wait_recv()

    def finish(self):
        self.need(*self.copies)
        for copy in self.copies.values():
            copy.wait_send()


def lanes(at, size):
    return pl.ds(pl.multiple_of(at * size, 128), size)


def each(n, body):
    def step(i, carry):
        body(i)
        return carry

    lax.fori_loop(0, n, step, 0)


def add_rows(dst, first, others, rows):
    width = dst.shape[-1]
    step = max(k for k in range(16, rows + 1, 16) if rows % k == 0 and (k * width <= 49152 or k == 16))

    def body(i):
        at = pl.ds(pl.multiple_of(i * step, 16), step)
        if len(others) == 1 and dst.dtype == BF:
            dst[at, :] = first[at, :] + others[0][at, :]
        else:
            total = first[at, :].astype(F32)
            for other in others:
                total += other[at, :].astype(F32)
            dst[at, :] = total.astype(dst.dtype)

    if step == rows:
        body(0)
    else:
        each(rows // step, body)


def advance(*flows):
    for flow in flows:
        next(flow, None)


def tp_gather_flow(net, p, tag, own, out, rows):
    y, zl, t = p.y, p.zl, p.t
    tq = y * 2 + 1 - zl
    zp = p.partner()
    top, low = pl.ds(0, rows // 2), pl.ds(rows // 2, rows // 2)
    net.send((tag, "z"), own, out.at[t], zp)
    net.send((tag, "r", 0), own.at[top], out.at[t, top], p.at(y=1))
    net.send((tag, "l", 1), own.at[low], out.at[t, low], p.at(y=3))
    net.send((tag, "r", 1), own.at[low], out.at[t, low], p.at(y=1))
    net.send((tag, "l", 0), own.at[top], out.at[t, top], p.at(y=3))
    yield
    net.need((tag, "z"))
    net.send((tag, "p", 1), out.at[tq], out.at[tq], p.at(y=1))
    net.send((tag, "p", 3), out.at[tq], out.at[tq], p.at(y=3))
    yield
    ref = out.at[((y + 3) % 4) * 2 + zl, top]
    net.send((tag, "f", 1), ref, ref, p.at(y=1), after=[(tag, "r", 0)])
    ref = out.at[((y + 1) % 4) * 2 + zl, low]
    net.send((tag, "f", 3), ref, ref, p.at(y=3), after=[(tag, "l", 1)])
    yield
    ref = out.at[((y + 2) % 4) * 2 + zl]
    net.send((tag, "o"), ref, ref, zp, after=[(tag, "f", 1), (tag, "f", 3)])


def sum_side(net, p, tag, part, bufs, cols, i):
    src = part.at[((p.y + i) % 4) * 2 + 1 - p.zl]
    dst = bufs[1 if i == 1 else 2]
    for k, at in cols:
        net.send((tag, "p", i, k), src.at[:, at], dst.at[:, at], p.at(y=i))


def split_cols(width, chunks):
    w = width // chunks
    return [(k, pl.ds(k * w, w)) for k in range(chunks)]


def tp_sum_flow(net, p, tag, part, out, bufs, chunks, sent=False, loads=None, base=None):
    ro, rp1, rp3, rh1, rh3, rw1, rw3, rq, sb, sq, s1, s3 = bufs
    y, zl, t = p.y, p.zl, p.t
    zp = p.partner()
    rows, width = out.shape
    half = rows // 2
    top, low = pl.ds(0, half), pl.ds(half, half)
    cols = split_cols(width, chunks)

    def mine(i):
        return part.at[((y + i) % 4) * 2 + zl]

    def theirs(i):
        return part.at[((y + i) % 4) * 2 + 1 - zl]

    far, cross, right, left, own = mine(2), theirs(0), mine(1), mine(3), mine(0)
    copies = []
    if loads is not None:
        wanted = zip((far, cross, right, left, own), (sb, sq, s1, s3, loads[0]))
        copies = [
            pltpu.make_async_copy(src, dst, loads[1].at[i]) for i, (src, dst) in enumerate(wanted)
        ]
        far, cross, right, left, own = sb, sq, s1, s3, loads[0]
    for copy in copies:
        copy.start()
    for k, at in cols:
        net.send((tag, "o", k), theirs(2).at[:, at], ro.at[:, at], zp)
    if not sent:
        for i in (1, 3):
            sum_side(net, p, tag, part, bufs, cols, i)
    yield
    for copy in copies:
        copy.wait()
    for k, at in cols:
        net.need((tag, "o", k))
        add_rows(sb.at[:, at], far.at[:, at], [ro.at[:, at]], rows)
        net.send((tag, "h", 1, k), sb.at[low, at], rh1.at[:, at], p.at(y=1))
        net.send((tag, "h", 3, k), sb.at[top, at], rh3.at[:, at], p.at(y=3))
    yield
    for k, at in cols:
        net.need((tag, "p", 1, k), (tag, "p", 3, k))
        add_rows(sq.at[:, at], cross.at[:, at], [rp1.at[:, at], rp3.at[:, at]], rows)
        net.send((tag, "q", k), sq.at[:, at], rq.at[:, at], zp)
    yield
    for k, at in cols:
        net.need((tag, "h", 1, k))
        if loads is None:
            s1[top, at] = right[top, at]
            s3[low, at] = left[low, at]
        add_rows(s1.at[low, at], right.at[low, at], [rh1.at[:, at]], half)
        net.send((tag, "w", 1, k), s1.at[:, at], rw1.at[:, at], p.at(y=1))
        net.need((tag, "h", 3, k))
        add_rows(s3.at[top, at], left.at[top, at], [rh3.at[:, at]], half)
        net.send((tag, "w", 3, k), s3.at[:, at], rw3.at[:, at], p.at(y=3))
    yield
    for k, at in cols:
        net.need((tag, "q", k), (tag, "w", 1, k), (tag, "w", 3, k))
        others = [rq.at[:, at], rw1.at[:, at], rw3.at[:, at]]
        if base is not None:
            others.append(base.at[:, at])
        add_rows(out.at[:, at], own.at[:, at], others, rows)


def short_sum_flow(net, p, tag, part, out, bufs, chunks, sent=False):
    ro, rp1, rp3, rw1, rw3, rf, rq, sb, sq = bufs
    y, zl = p.y, p.zl
    zp = p.partner()
    rows, width = out.shape
    cols = split_cols(width, chunks)

    def mine(i):
        return part.at[((y + i) % 4) * 2 + zl]

    def theirs(i):
        return part.at[((y + i) % 4) * 2 + 1 - zl]

    for k, at in cols:
        net.send((tag, "o", k), theirs(2).at[:, at], ro.at[:, at], zp)
    if not sent:
        short_sides(net, p, tag, part, bufs, cols, True)
        short_sides(net, p, tag, part, bufs, cols, False)
    yield
    for k, at in cols:
        net.need((tag, "o", k))
        add_rows(sb.at[:, at], mine(2).at[:, at], [ro.at[:, at]], rows)
        net.send((tag, "f", k), sb.at[:, at], rf.at[:, at], p.at(y=2))
    yield
    for k, at in cols:
        net.need((tag, "p", 1, k), (tag, "p", 3, k))
        add_rows(sq.at[:, at], theirs(0).at[:, at], [rp1.at[:, at], rp3.at[:, at]], rows)
        net.send((tag, "q", k), sq.at[:, at], rq.at[:, at], zp)
    yield
    for k, at in cols:
        net.need((tag, "w", 1, k), (tag, "w", 3, k), (tag, "q", k), (tag, "f", k))
        others = [ref.at[:, at] for ref in (rq, rw1, rw3, rf)]
        add_rows(out.at[:, at], mine(0).at[:, at], others, rows)


def short_sides(net, p, tag, part, bufs, cols, theirs):
    for i in (1, 3):
        src = part.at[((p.y + i) % 4) * 2 + (1 - p.zl if theirs else p.zl)]
        dst = bufs[(1 if theirs else 3) + i // 2]
        for k, at in cols:
            name = (tag, "p" if theirs else "w", i, k)
            net.send(name, src.at[:, at], dst.at[:, at], p.at(y=i))


def dots(left, right, left_dim, right_dim):
    return lax.dot_general(
        left, right, (((left_dim,), (right_dim,)), ((), ())), preferred_element_type=F32
    )


def feed_forward_kernel(
    own, cot_in, weights_in, gn, hp_out, gu_out, dn_out,
    cot, weights, xs, gu, gh, hid, ggu, part, hp, dgu, dd, rgu, rdd, *rest,
):
    bufs, (send_sems, recv_sems, load_sems, store_sems) = rest[:9], rest[9:]
    p = Place()
    y, zl, c = p.y, p.zl, p.c
    sib = p.at(c=1)
    loads, stores = Loads(load_sems), Loads(store_sems)
    loads.start("x", own, xs.at[p.t])
    loads.start("c", cot_in, cot)
    loads.start("w", weights_in, weights)
    greet([sib, p.partner()] + [p.at(y=i) for i in (1, 2, 3)])
    net = Net(send_sems, recv_sems)
    t, tq, zp = p.t, y * 2 + 1 - zl, p.partner()
    top, low = pl.ds(0, 64), pl.ds(64, 64)
    net.send(("g", "z"), own, xs.at[t], zp)
    net.send(("g", "r", 0), own.at[top], xs.at[t, top], p.at(y=1))
    net.send(("g", "l", 1), own.at[low], xs.at[t, low], p.at(y=3))
    gate_up_at, down_at = pl.ds(0, 2 * FF_PAD), pl.ds(2 * FF_PAD, FF_PAD)
    loads.need("c", "w")

    def grad_hidden(i):
        at = pl.ds(i * 4, 4)
        gh[pl.ds(pl.multiple_of(i * 512, 512), 512), :] = dots(
            cot[at].reshape(512, -1), weights[:, down_at], 1, 0
        )

    grad_hidden(0)
    net.send(("g", "r", 1), own.at[low], xs.at[t, low], p.at(y=1))
    net.send(("g", "l", 0), own.at[top], xs.at[t, top], p.at(y=3))
    grad_hidden(1)

    def mine(i):
        return ((y + i) % 4) * 2 + zl

    def theirs(i):
        return ((y + i) % 4) * 2 + 1 - zl

    net.need(("g", "r", 0), ("g", "l", 1))
    net.send(("g", "f", 1), xs.at[mine(3), top], xs.at[mine(3), top], p.at(y=1))
    net.send(("g", "f", 3), xs.at[mine(1), low], xs.at[mine(1), low], p.at(y=3))
    net.need(("g", "z"))
    for i in (1, 3):
        net.send(("g", "p", i), xs.at[tq], xs.at[tq], p.at(y=i))
    loads.need("x")

    def pair(one, two, sends=()):
        def both(ref):
            return jnp.concatenate([ref[one], ref[two]], axis=0)

        gu[...] = dots(both(xs), weights[:, gate_up_at], 1, 0)
        for k, block in enumerate((one, two)):

            def gates(j):
                at = pl.ds(pl.multiple_of(k * 128 + j * 16, 16), 16)
                to = pl.ds(pl.multiple_of(j * 16, 16), 16)
                row = pl.ds(pl.multiple_of(block * 128 + j * 16, 16), 16)
                gate, up = gu[at, pl.ds(0, FF_PAD)], gu[at, pl.ds(FF_PAD, FF_PAD)]
                grad = gh[row, :]
                sigma = jax.nn.sigmoid(gate)
                activated = gate * sigma
                hid[block, to, :] = (activated * up).astype(BF)
                ggu[block, to, pl.ds(0, FF_PAD)] = (
                    grad * up * sigma * (1.0 + gate * (1.0 - sigma))
                ).astype(BF)
                ggu[block, to, pl.ds(FF_PAD, FF_PAD)] = (grad * activated).astype(BF)

            each(8, gates)
        for j in range(2):
            at = pl.ds(j * 768, 768)
            total = dots(both(ggu), weights[at, gate_up_at], 1, 1).astype(BF)
            part[one, :, at] = total[:128]
            part[two, :, at] = total[128:]
            for send in sends:
                send(j, at)

    def hidden_out(blocks):
        for j in range(2):
            at = pl.ds(j * 768, 768)
            rows = jnp.concatenate([hid[block] for block in blocks], axis=0)
            total = dots(rows, weights[at, down_at], 1, 1).astype(BF)
            for k, block in enumerate(blocks):
                hp[block, :, at] = total[k * 128 : k * 128 + 128]

    ro, rp1, rp3, rw1, rw3, rf, rq, sb, sq = bufs

    def side(name, i, src, dst):
        def send(j, at):
            net.send(("s", name, i, j), src.at[:, at], dst.at[:, at], p.at(y=i))

        return send

    def across(j, at):
        net.send(("s", "o", j), part.at[theirs(2), :, at], ro.at[:, at], zp)

    pair(mine(0), theirs(0))
    net.need(("g", "f", 1), ("g", "f", 3))
    net.send(("g", "o"), xs.at[mine(2)], xs.at[mine(2)], zp)
    net.need(("g", "r", 1), ("g", "l", 0))
    pair(mine(1), mine(3))
    hidden_out([mine(0), theirs(0), mine(1), mine(3)])
    net.need(("g", "p", 1), ("g", "p", 3))
    sides = [(1, rp1, rw1), (3, rp3, rw3)]
    pair(
        theirs(1), theirs(3), [side("p", i, part.at[theirs(i)], dst) for i, dst, _ in sides]
    )
    net.need(("g", "o"))
    pair(mine(2), theirs(2), [across])
    cols = split_cols(gn.shape[1], 2)
    for i, _, dst in sides:
        for j, at in cols:
            side("w", i, part.at[mine(i)], dst)(j, at)
    hidden_out([theirs(1), theirs(3), mine(2), theirs(2)])
    stores.start("h", hp, hp_out)
    rows = own.shape[0]
    def halves(ref, came, k):
        for f in (2 * k, 2 * k + 1):
            add_rows(ref.at[f, c], ref.at[f, c], [came.at[f]], 96)

    for k in range(4):
        two = pl.ds(k * 2, 2)

        def columns(j):
            at, to = pl.ds(k * 384, 384), pl.ds(pl.multiple_of(j * 768, 128), 768)
            left, right = xs[:, :, at].reshape(1024, 384), ggu[:, :, to].reshape(1024, 768)
            dgu[two, :, :, to] = dots(left, right, 0, 0).astype(BF).reshape(2, 2, 96, 768)

        each(3, columns)
        net.send(("e", k), dgu.at[two, 1 - c], rgu.at[two], sib)
        if k == 0:
            for j, at in cols:
                net.need(("s", "o", j))
                add_rows(sb.at[:, at], part.at[mine(2), :, at], [ro.at[:, at]], rows)
                net.send(("s", "f", j), sb.at[:, at], rf.at[:, at], p.at(y=2))
            for j, at in cols:
                net.need(("s", "p", 1, j), ("s", "p", 3, j))
                others = [rp1.at[:, at], rp3.at[:, at]]
                add_rows(sq.at[:, at], part.at[theirs(0), :, at], others, rows)
                net.send(("s", "q", j), sq.at[:, at], rq.at[:, at], zp)
        else:
            net.need(("e", k - 1))
            halves(dgu, rgu, k - 1)
    for k in range(4):
        two, at = pl.ds(k * 2, 2), pl.ds(k * 384, 384)
        total = dots(cot[:, :, at].reshape(1024, 384), hid[...].reshape(1024, -1), 0, 0)
        dd[two] = total.astype(BF).reshape(2, 2, 96, FF_PAD)
        net.send(("d", k), dd.at[two, 1 - c], rdd.at[two], sib)
        if k == 0:
            net.need(("e", 3))
            halves(dgu, rgu, 3)
            stores.start("g", dgu.at[:, c], gu_out)
        else:
            net.need(("d", k - 1))
            halves(dd, rdd, k - 1)
    for j, at in cols:
        net.need(("s", "w", 1, j), ("s", "w", 3, j), ("s", "q", j), ("s", "f", j))
        others = [ref.at[:, at] for ref in (rq, rw1, rw3, rf)]
        add_rows(gn.at[:, at], part.at[t, :, at], others, rows)
    net.need(("d", 3))
    halves(dd, rdd, 3)
    stores.start("d", dd.at[:, c], dn_out)
    stores.need("h", "d", "g")
    net.finish()


def feed_forward(own, cot, weights, cid=3, name="feed_forward"):
    vm = pl.BlockSpec(memory_space=pltpu.VMEM)
    hbm = pl.BlockSpec(memory_space=pl.ANY)
    rows, width = own.shape
    V = lambda *s: pltpu.VMEM(s, BF)
    whole = V(rows, width)
    B = lambda *s: jax.ShapeDtypeStruct(s, BF)
    D = pltpu.SemaphoreType.DMA
    n = 36
    return pl.pallas_call(
        feed_forward_kernel,
        out_shape=(
            jax.ShapeDtypeStruct((rows, width), F32),
            B(8, rows, width),
            B(8, 96, 2 * FF_PAD),
            B(8, 96, FF_PAD),
        ),
        in_specs=[hbm] * 3,
        out_specs=(vm, hbm, hbm, hbm),
        scratch_shapes=[
            V(8, rows, width),
            V(width, 3 * FF_PAD),
            V(8, rows, width),
            pltpu.VMEM((256, 2 * FF_PAD), F32),
            pltpu.VMEM((1024, FF_PAD), F32),
            V(8, 128, FF_PAD),
            V(8, 128, 2 * FF_PAD),
            V(8, rows, width),
            V(8, rows, width),
            V(8, 2, 96, 2 * FF_PAD),
            V(8, 2, 96, FF_PAD),
            V(8, 96, 2 * FF_PAD),
            V(8, 96, FF_PAD),
        ]
        + [whole] * 9
        + [D((n,)), D((n,)), D((3,)), D((3,))],
        name=name,
        compiler_params=pltpu.CompilerParams(
            collective_id=cid, has_side_effects=True, vmem_limit_bytes=63 << 20
        ),
    )(own, cot, weights)


def weight_flow(net, p, tag, g, acc, rh1, rh3, rw1, rw3, rz, out, local):
    x, zh = p.x, p.zh
    top, low = pl.ds(0, 48), pl.ds(48, 48)
    sides = (("o", 1 - zh), ("s", zh))
    own = pltpu.make_async_copy(g, acc, local)
    own.start()

    def at(i, side):
        return side * 4 + (x + i) % 4

    for k, (s, side) in enumerate(sides):
        b = at(2, side)
        net.send((tag, "h", 1, s), g.at[b, low], rh1.at[k], p.at(x=1))
        net.send((tag, "h", 3, s), g.at[b, top], rh3.at[k], p.at(x=3))
        yield
    own.wait()
    for k, (s, side) in enumerate(sides):
        b = at(1, side)
        net.need((tag, "h", 1, s))
        add_rows(acc.at[b, low], acc.at[b, low], [rh1.at[k]], 48)
        net.send((tag, "w", 1, s), acc.at[b], rw1.at[k], p.at(x=1))
        b = at(3, side)
        net.need((tag, "h", 3, s))
        add_rows(acc.at[b, top], acc.at[b, top], [rh3.at[k]], 48)
        net.send((tag, "w", 3, s), acc.at[b], rw3.at[k], p.at(x=3))
        yield
    b = at(0, 1 - zh)
    net.need((tag, "w", 1, "o"), (tag, "w", 3, "o"))
    add_rows(acc.at[b], acc.at[b], [rw1.at[0], rw3.at[0]], 96)
    net.send((tag, "z"), acc.at[b], rz, p.at(z=2))
    yield
    b = at(0, zh)
    net.need((tag, "w", 1, "s"), (tag, "w", 3, "s"), (tag, "z"))
    add_rows(out, acc.at[b], [rw1.at[1], rw3.at[1], rz], 96)


def small_flow(net, p, src, out, rc, rings):
    net.send(("t", "c"), src, rc, p.at(c=1))
    yield
    net.need(("t", "c"))
    out[...] = src[...] + rc[...]
    for k, (ring, place) in enumerate(zip(rings, (p.x, p.y, p.z))):
        ring[place] = out[...]
        for i in (1, 3, 2):
            step = {"xyz"[k]: i}
            net.send(("t", k, i), ring.at[place], ring.at[place], p.at(**step))
        yield
        net.need(("t", k, 1), ("t", k, 2), ("t", k, 3))
        out[...] = ring[0] + ring[1] + ring[2] + ring[3]


def ring_sum_flow(net, p, tag, g, rc, rh1, rh3, rw1, rw3, ring, block, count):
    c = p.c
    sib = p.at(c=1)
    top, low = pl.ds(0, 48), pl.ds(48, 48)

    def mine(i):
        first, cols = block(i)
        return g.at[pl.ds(first, count), c, :, cols]

    def theirs(i):
        first, cols = block(i)
        return g.at[pl.ds(first, count), 1 - c, :, cols]

    def landed(i):
        first, cols = block(i)
        return rc.at[pl.ds(first, count), :, cols]

    def add(dst, others, rows, skip=0):
        def body(i):
            to = dst.at[i, pl.ds(skip, rows)]
            add_rows(to, to, [other.at[i] for other in others], rows)

        each(count, body)

    for i in (2, 3, 1, 0):
        net.send((tag, "c", i), theirs(i), landed(i), sib)
    yield
    b = mine(2)
    net.need((tag, "c", 2))
    add(b, [landed(2)], 96)
    net.send((tag, "h", 1), b.at[:, low], rh1, ring(1))
    net.send((tag, "h", 3), b.at[:, top], rh3, ring(3))
    yield
    for i in (1, 3):
        net.need((tag, "c", i))
        add(mine(i), [landed(i)], 96)
    yield
    for i, came, skip in ((1, rh1, 48), (3, rh3, 0)):
        net.need((tag, "h", i))
        add(mine(i), [came], 48, skip)
        net.send((tag, "w", i), mine(i), rw1 if i == 1 else rw3, ring(i))
    yield
    net.need((tag, "c", 0), (tag, "w", 1), (tag, "w", 3))
    add(mine(0), [landed(0), rw1, rw3], 96)


def along_x(net, p, tag, src, rx, total):
    x = p.x
    for i in (1, 3, 2):
        net.send((tag, "x", i), src.at[(x + i) % 4], rx.at[i - 1], p.at(x=i))
    yield
    net.need((tag, "x", 1), (tag, "x", 2), (tag, "x", 3))
    add_rows(total, src.at[x], [rx.at[0], rx.at[1], rx.at[2]], 96)


def z_flow(net, p, tag, g, bufs, total, width):
    rc, rh1, rh3, rw1, rw3, rx = bufs

    def block(i):
        zz = (p.z + i) % 4
        return (zz // 2) * 4, lanes(zz % 2, width)

    yield from ring_sum_flow(
        net, p, tag, g, rc, rh1, rh3, rw1, rw3, lambda i: p.at(z=i), block, 4
    )
    src = g.at[pl.ds(p.zh * 4, 4), p.c, :, lanes(p.zl, width)]
    yield from along_x(net, p, tag, src, rx, total)


def cross_sum(net, p, tag, src, rx, total):
    x, zh = p.x, p.zh
    for i in (0, 1, 3, 2):
        ref = src.at[(1 - zh) * 4 + (x + i) % 4]
        net.send((tag, "m", i), ref, rx.at[3 + i], p.mirror(i))
    for i in (1, 3, 2):
        net.send((tag, "x", i), src.at[zh * 4 + (x + i) % 4], rx.at[i - 1], p.at(x=i))
    yield
    net.need(*[(tag, "m", i) for i in range(4)], *[(tag, "x", i) for i in range(1, 4)])
    add_rows(total, src.at[p.f], [rx.at[i] for i in range(7)], 96)


def y_flow(net, p, tag, g, bufs, total, width, begin):
    rc, rh1, rh3, rw1, rw3, rx = bufs
    part = g.at[:, :, :, pl.ds(begin, 4 * width)] if begin else g
    yield from ring_sum_flow(
        net,
        p,
        tag,
        part,
        rc,
        rh1,
        rh3,
        rw1,
        rw3,
        lambda i: p.at(y=i),
        lambda i: (0, lanes((p.y + i) % 4, width)),
        8,
    )
    yield from cross_sum(net, p, tag, part.at[:, p.c, :, lanes(p.y, width)], rx, total)


def y_direct_flow(net, p, tag, g, bufs, total, width, begin):
    rc, ry, rx = bufs
    part = g.at[:, :, :, pl.ds(begin, 4 * width)]
    mine, theirs = part.at[:, p.c], part.at[:, 1 - p.c]
    for i in (2, 1, 3, 0):
        cols = lanes((p.y + i) % 4, width)
        net.send((tag, "c", i), theirs.at[:, :, cols], rc.at[:, :, cols], p.at(c=1))
    yield
    for i in (2, 1, 3, 0):
        cols = lanes((p.y + i) % 4, width)
        block = mine.at[:, :, cols]
        net.need((tag, "c", i))

        def near(k):
            add_rows(block.at[k], block.at[k], [rc.at[k, :, cols]], 96)

        each(8, near)
        if i:
            net.send((tag, "w", i), block, ry.at[i - 1], p.at(y=i))
    yield
    block = mine.at[:, :, lanes(p.y, width)]
    net.need(*[(tag, "w", i) for i in (1, 3, 2)])

    def whole(k):
        add_rows(block.at[k], block.at[k], [ry.at[i, k] for i in range(3)], 96)

    each(8, whole)
    yield from cross_sum(net, p, tag, block, rx, total)


def tp_scatter(net, p, tag, totals, pads, fins, to):
    t = p.t
    at = 0
    for total in totals:
        width = total.shape[1]
        for i in range(8):
            pads[i, pl.ds(0, 12), pl.ds(at, width)] = total[pl.ds(12 * i, 12), :].astype(BF)
            pads[i, pl.ds(12, 4), pl.ds(at, width)] = jnp.zeros((4, width), BF)
        at += width
    for i in range(1, 8):
        net.send((tag, "f", i), pads.at[(t + i) % 8], fins.at[t], to[i - 1])
    fins[t] = pads[t]


def norm_back_rows(grad, values, gain, base, out, grad_gain):
    grad_gain[...] = jnp.zeros_like(grad_gain)

    def body(i):
        at = pl.ds(pl.multiple_of(i * 16, 16), 16)
        v = values[at, :].astype(F32)
        g = grad[at, :]
        r = lax.rsqrt(jnp.mean(v * v, axis=-1, keepdims=True) + norm_eps)
        a = g * gain
        grad_gain[...] += jnp.sum(g * v * r, axis=0, keepdims=True)
        back = r * a - v * r * r * r * jnp.mean(a * v, axis=-1, keepdims=True)
        out[at, :] = base[at, :].astype(F32) + back

    each(grad.shape[0] // 16, body)


def backward_kernel(*refs):
    ga, gb, hp, w2t, w1, probs = refs[:6]
    near_in = refs[6:17]
    h_out, grad_in, o1, o2, oa, ob, small = refs[17:24]
    rest = list(refs[24:])

    def take(n):
        out = rest[:n]
        del rest[:n]
        return out

    near = take(11)
    gn, middle, cot, hidden_in, normed, attended, queries, kv, cos, sin, gains = near
    m_bufs = [take(6), take(6)]
    q_bufs, q_total = take(6), take(1)[0]
    o_bufs, o_total = take(6), take(1)[0]
    r_bufs, r_total = take(6), take(1)[0]
    v_bufs, v_total = take(3), take(1)[0]
    hp_bufs, hp_own = take(12), take(1)[0]
    kv_bufs, kv_part, kv_sum = take(9), take(1)[0], take(1)[0]
    rcs, rs1, rs2, rs3 = take(4)
    pad_q, fin_q, pad_v, fin_v = take(4)
    wide, deep, g1, g_mid, g_proj, g_att, g_qkv, stack_q, stack_a = take(9)
    gain_two, gain_one, part_small, gno = take(4)
    send_sems, recv_sems, local_sems, hp_sems, load_sems = take(5)

    p = Place()
    t = p.t
    tp_all = [{FS: p.f, CX: p.c, TP: (t + i) % 8} for i in range(1, 8)]
    loads = Loads(load_sems)
    for i in (0, 1, 2, 10):
        loads.start(i, near_in[i], near[i])
    loads.start("w", w2t, wide)
    loads.start("p", probs, deep)
    for i in (5, 7, 6, 8, 9, 4, 3):
        loads.start(i, near_in[i], near[i])
    greet(
        [p.at(c=1)] + [p.at(x=i) for i in (1, 2, 3)] + tp_all + [p.at(z=2)]
        + [p.mirror(i) for i in range(4)]
    )
    net = Net(send_sems, recv_sems)
    steps = Steps(BACKWARD_ORDER)
    steps.add("a", weight_flow(net, p, "a", ga, *m_bufs[0], oa, local_sems.at[0]))
    steps.add("b", weight_flow(net, p, "b", gb, *m_bufs[1], ob, local_sems.at[1]))
    flow_h = tp_sum_flow(
        net, p, "h", hp, h_out, hp_bufs, 2, loads=(hp_own, hp_sems), base=middle
    )
    steps.add("h", flow_h)
    steps.point()
    loads.need(0, 1, 2, 10)
    norm_back_rows(gn, middle, gains[pl.ds(1, 1), :], cot, g_mid, gain_two)
    g_proj[...] = g_mid[...].astype(BF)
    steps.point()
    loads.need("w")

    def grad_attended(j):
        at = pl.ds(pl.multiple_of(j * 512, 512), 512)
        g_att[:, at] = dots(g_proj[...], wide[:, at], 1, 0).astype(BF)

    each(3, grad_attended)
    steps.point()
    loads.need(5)

    def grad_out(j):
        at = pl.ds(pl.multiple_of(j * 384, 128), 384)
        wide[at, :] = dots(g_proj[:, at], attended[...], 0, 0).astype(BF)

    each(4, grad_out)
    steps.add("o", y_flow(net, p, 2, wide.reshape(8, 2, 96, 1536), o_bufs, o_total, 384, 0))
    steps.point()
    loads.need("p", 7, 6)
    size = HEAD_SIZE
    scale = size**-0.5

    def stack(h):
        at = pl.ds(pl.multiple_of(h * size, size), size)
        stack_q[at, :] = queries[:, at]
        stack_a[at, :] = g_att[:, at]

    each(QUERY_HEADS, stack)
    group_rows = [pl.ds(768 * group, 768) for group in range(KEY_VALUE_HEADS)]

    def sums(left, right, first, factor):
        def body(j):
            at = pl.ds(pl.multiple_of(j * 256, 256), 256)
            for group, rows in enumerate(group_rows):
                grad = dots(left[rows, at], right[rows, :], 0, 0) * factor
                to = pl.ds((first + group) * size, size)
                kv_part[pl.ds(j * 2, 2), :, to] = grad.astype(BF).reshape(2, 128, size)

        each(4, body)

    sums(deep, stack_a, KEY_VALUE_HEADS, 1.0)
    steps.point()
    for group in range(KEY_VALUE_HEADS):
        values = kv.at[:, pl.ds((KEY_VALUE_HEADS + group) * size, size)]

        def heads(j):
            at = pl.ds(pl.multiple_of(group * 768 + j * 256, 256), 256)
            grad = dots(stack_a[at, :], values[...], 1, 1)
            weight = deep[at, :].astype(F32)
            inner = jnp.sum(weight * grad, axis=-1, keepdims=True)
            deep[at, :] = (weight * (grad - inner)).astype(BF)

        each(3, heads)
        steps.point()
    sums(deep, stack_q, 0, scale)
    steps.add("k", short_sum_flow(net, p, "k", kv_part, kv_sum, kv_bufs, 1))
    steps.point()
    loads.need(8, 9)

    def turned_back(grad):
        return (grad * cos[...] - pltpu.roll(grad, size // 2, 1) * sin[...]).astype(BF)

    for group in range(KEY_VALUE_HEADS):
        keys = kv.at[:, pl.ds(group * size, size)]

        def grad_query(j):
            at = pl.ds(pl.multiple_of(group * 768 + j * 256, 256), 256)
            grad = dots(deep[at, :], keys[...], 1, 0) * scale
            for i in range(2):
                to = pl.ds(pl.multiple_of((group * 6 + j * 2 + i) * size, size), size)
                g_qkv[:, to] = turned_back(grad[i * size : (i + 1) * size])

        each(3, grad_query)
        steps.point()
    loads.start("u", w1.at[:, pl.ds(0, 1024)], deep)
    loads.need(4)

    def grad_w(begin, count):
        at = pl.ds(begin, count)

        def body(j):
            d = pl.ds(pl.multiple_of(j * 384, 128), 384)
            total = dots(normed[:, d], g_qkv[:, at], 0, 0)
            g1[pl.ds(j * 2, 2), :, :, at] = total.astype(BF).reshape(2, 2, 96, count)

        each(4, body)

    grad_w(0, 1024)
    steps.add("q", z_flow(net, p, 1, g1, q_bufs, q_total, 512))
    steps.point()
    grad_w(1024, 512)
    steps.add("r", y_flow(net, p, 3, g1, r_bufs, r_total, 128, 1024))
    for _ in range(8):
        steps.point()
    steps.finish("k")
    for i in range(KEY_VALUE_HEADS):
        at, to = pl.ds(i * size, size), pl.ds((QUERY_HEADS + i) * size, size)
        g_qkv[:, to] = turned_back(kv_sum[:, at])
    at = pl.ds((QUERY_HEADS + KEY_VALUE_HEADS) * size, KEY_VALUE_HEADS * size)
    g_qkv[:, at] = kv_sum[:, pl.ds(KEY_VALUE_HEADS * size, KEY_VALUE_HEADS * size)].astype(BF)
    grad_w(1536, 512)
    steps.add("v", y_direct_flow(net, p, 4, g1, v_bufs, v_total, 128, 1536))
    for _ in range(4):
        steps.point()

    def normed_back(i):
        def body(j):
            at = pl.ds(pl.multiple_of(j * 512, 512), 512)
            total = dots(g_qkv[:, pl.ds(1024 * i, 1024)], deep[at, :], 1, 1)
            gno[:, at] = total if i == 0 else gno[:, at] + total

        each(3, body)

    loads.need("u")
    normed_back(0)
    loads.start("v", w1.at[:, pl.ds(1024, 1024)], deep)
    for _ in range(4):
        steps.point()
    loads.need("v")
    normed_back(1)
    loads.need(3)
    steps.point()
    norm_back_rows(gno, hidden_in, gains[pl.ds(0, 1), :], g_mid, grad_in, gain_one)
    bias = jnp.sum(g_qkv[...].astype(F32), axis=0, keepdims=True)
    for i in range(16):
        part_small[pl.ds(i, 1), :] = bias[:, i * 128 : i * 128 + 128]
    for i in range(12):
        part_small[pl.ds(16 + i, 1), :] = gain_one[:, pl.ds(i * 128, 128)]
        part_small[pl.ds(28 + i, 1), :] = gain_two[:, pl.ds(i * 128, 128)]
    steps.add("t", small_flow(net, p, part_small, small, rcs, (rs1, rs2, rs3)))
    for _ in range(14):
        steps.point()
    steps.finish("v")
    tp_scatter(net, p, 4, [v_total], pad_v, fin_v, tp_all)
    for _ in range(10):
        steps.point()
    steps.finish("q", "r", "o")
    tp_scatter(net, p, 2, [q_total, r_total, o_total], pad_q, fin_q, tp_all)
    for _ in range(8):
        steps.point()
    steps.finish("t", "a", "b", "h")
    net.need(*[(2, "f", i) for i in range(1, 8)])
    for k in range(2):
        at = pl.ds(0, 512)
        total = fin_q[k, :, at].astype(F32)
        for yy in range(1, 4):
            total += fin_q[2 * yy + k, :, at].astype(F32)
        o1[:, pl.ds(512 * k, 512)] = total
    for yy in range(4):
        at = pl.ds(512, 128)
        total = fin_q[2 * yy, :, at].astype(F32) + fin_q[2 * yy + 1, :, at].astype(F32)
        o1[:, pl.ds(1024 + 128 * yy, 128)] = total
        at = pl.ds(640, 384)
        total = fin_q[2 * yy, :, at].astype(F32) + fin_q[2 * yy + 1, :, at].astype(F32)
        o2[:, pl.ds(384 * yy, 384)] = total
    net.need(*[(4, "f", i) for i in range(1, 8)])
    for yy in range(4):
        total = fin_v[2 * yy].astype(F32) + fin_v[2 * yy + 1].astype(F32)
        o1[:, pl.ds(1536 + 128 * yy, 128)] = total
    net.finish()


def backward(far, near, cid=1, name="backward"):
    vm = pl.BlockSpec(memory_space=pltpu.VMEM)
    hbm = pl.BlockSpec(memory_space=pl.ANY)
    V = lambda *s: pltpu.VMEM(s, BF)
    W = lambda *s: pltpu.VMEM(s, F32)
    scratch = [pltpu.VMEM(a.shape, a.dtype) for a in near]
    for w in (far[0].shape[-1], far[1].shape[-1]):
        scratch += [
            V(8, 96, w), V(2, 48, w), V(2, 48, w), V(2, 96, w), V(2, 96, w), V(96, w),
        ]
    scratch += [
        V(8, 96, 1024), V(4, 48, 512), V(4, 48, 512), V(4, 96, 512), V(4, 96, 512), V(3, 96, 512),
        W(96, 512),
    ]
    for w in (384, 128):
        scratch += [
            V(8, 96, 4 * w), V(8, 48, w), V(8, 48, w), V(8, 96, w), V(8, 96, w), V(7, 96, w), W(96, w),
        ]
    scratch += [V(8, 96, 512), V(3, 8, 96, 128), V(7, 96, 128), W(96, 128)]
    whole, half = V(128, 1536), V(64, 1536)
    scratch += [whole] * 3 + [half] * 2 + [whole] * 7 + [whole]
    scratch += [V(128, 512)] * 9 + [V(8, 128, 512), W(128, 512)]
    scratch += [W(40, 128)] + [W(4, 40, 128)] * 3
    scratch += [V(8, 16, 1024)] * 2 + [V(8, 16, 128)] * 2
    scratch += [
        V(1536, 1536), V(1536, 1024), V(8, 2, 96, 2048), W(128, 1536), V(128, 1536), V(128, 1536),
        V(128, 2048), V(1536, 128), V(1536, 128),
        W(1, 1536), W(1, 1536), W(40, 128), W(128, 1536),
    ]
    n = 140
    D = pltpu.SemaphoreType.DMA
    scratch += [D((n,)), D((n,)), D((2,)), D((5,)), D((16,))]
    S = lambda *s: jax.ShapeDtypeStruct(s, F32)
    return pl.pallas_call(
        backward_kernel,
        out_shape=(
            S(128, 1536), S(128, 1536), S(16, 2048), S(16, 1536),
            S(96, far[0].shape[-1]), S(96, far[1].shape[-1]), S(40, 128),
        ),
        in_specs=[hbm] * (len(far) + len(near)),
        out_specs=(vm,) * 7,
        scratch_shapes=scratch,
        name=name,
        compiler_params=pltpu.CompilerParams(
            collective_id=cid, has_side_effects=True, vmem_limit_bytes=62 << 20
        ),
    )(*far, *near)


def gather_rows_flow(net, p, tag, own, pad):
    t, tq = p.t, p.y * 2 + 1 - p.zl
    net.send((tag, "z"), own, pad.at[t], p.partner())
    for i in (1, 3, 2):
        net.send((tag, "y", i), own, pad.at[t], p.at(y=i))
    yield
    net.need((tag, "z"))
    for i in (1, 3, 2):
        net.send((tag, "p", i), pad.at[tq], pad.at[tq], p.at(y=i))
    yield
    net.need(*[(tag, k, i) for k in "yp" for i in (1, 2, 3)])


def close_up(pad, wide, blk):
    width = pad.shape[-1]
    for i in range(8):
        wide[pl.ds(12 * i, 12), pl.ds(0, width)] = pad[i, pl.ds(0, 12), :].astype(F32)
    blk[...] = wide[:, pl.ds(0, width)].astype(BF)


def cross_sends(net, p, tag, src, place):
    for i in (1, 3, 2):
        net.send((tag, "x", i), src, place, p.at(x=i))
    for i in (0, 1, 3, 2):
        net.send((tag, "m", i), src, place, p.mirror(i))


def cross_names(tag):
    return [(tag, "x", i) for i in (1, 2, 3)] + [(tag, "m", i) for i in range(4)]


def ring_gather_flow(net, p, tag, w, ring, block, count):
    c = p.c
    top, low = pl.ds(0, 48), pl.ds(48, 48)

    def part(i, rows=None):
        first, cols = block(i)
        if rows is None:
            return w.at[pl.ds(first, count), c, :, cols]
        return w.at[pl.ds(first, count), c, rows, cols]

    sib = p.at(c=1)
    net.send((tag, "r", 1), part(0), part(0), ring(1))
    net.send((tag, "r", 3), part(0), part(0), ring(3))
    net.send((tag, "c", 0), part(0), part(0), sib)
    yield
    net.need((tag, "r", 1), (tag, "r", 3))
    net.send((tag, "f", 1), part(3, top), part(3, top), ring(1))
    net.send((tag, "f", 3), part(1, low), part(1, low), ring(3))
    net.send((tag, "c", 3), part(3), part(3), sib)
    net.send((tag, "c", 1), part(1), part(1), sib)
    yield
    net.need((tag, "f", 1), (tag, "f", 3))
    net.send((tag, "c", 2), part(2), part(2), sib)
    yield
    net.need(*[(tag, "c", i) for i in range(4)])


def weights_flow(net, p, m_in, mw):
    f, c, x, zh = p.f, p.c, p.x, p.zh
    top, low = pl.ds(0, 48), pl.ds(48, 48)
    sib = p.at(c=1)
    far = (1 - zh) * 4 + x

    def across(k, ff):
        net.send(("m", "c", k), mw.at[ff, c], mw.at[ff, c], sib)

    def ring(tag, src, ff):
        net.send((tag, "r", 0), src.at[top], mw.at[ff, c, top], p.at(x=1))
        net.send((tag, "l", 1), src.at[low], mw.at[ff, c, low], p.at(x=3))
        yield
        net.send((tag, "r", 1), src.at[low], mw.at[ff, c, low], p.at(x=1))
        net.send((tag, "l", 0), src.at[top], mw.at[ff, c, top], p.at(x=3))
        yield

    def onward(tag, side, k):
        after, before = side * 4 + (x + 1) % 4, side * 4 + (x + 3) % 4
        net.need((tag, "r", 0), (tag, "l", 1))
        ref = mw.at[before, c, top]
        net.send((tag, "f", 1), ref, ref, p.at(x=1))
        ref = mw.at[after, c, low]
        net.send((tag, "f", 3), ref, ref, p.at(x=3))
        yield
        net.need((tag, "r", 1), (tag, "l", 0))
        across(k, before)
        across(k + 1, after)
        yield
        net.need((tag, "f", 1), (tag, "f", 3))
        across(k + 2, side * 4 + (x + 2) % 4)
        yield

    net.send(("m", "z"), m_in, mw.at[f, c], p.at(z=2))
    yield
    yield from ring("m", m_in, f)
    net.send(("m", "c", 0), m_in, mw.at[f, c], sib)
    net.need(("m", "z"))
    yield from ring("n", mw.at[far, c], far)
    yield from onward("m", zh, 1)
    across(4, far)
    yield from onward("n", 1 - zh, 5)
    net.need(*[("m", "c", k) for k in range(8)])


def cotangent_flow(net, p, own, out):
    y, zl, t = p.y, p.zl, p.t
    tq = y * 2 + 1 - zl
    zp = p.partner()
    top, low = pl.ds(0, 64), pl.ds(64, 64)
    net.send(("g", "r", 0), own.at[top], out.at[t, top], p.at(y=1))
    net.send(("g", "l", 1), own.at[low], out.at[t, low], p.at(y=3))
    yield
    net.send(("g", "r", 1), own.at[low], out.at[t, low], p.at(y=1))
    net.send(("g", "l", 0), own.at[top], out.at[t, top], p.at(y=3))
    yield
    net.send(("g", "z"), own, out.at[t], zp)
    yield
    net.need(("g", "r", 0), ("g", "l", 1))
    ref = out.at[((y + 3) % 4) * 2 + zl, top]
    net.send(("g", "f", 1), ref, ref, p.at(y=1))
    ref = out.at[((y + 1) % 4) * 2 + zl, low]
    net.send(("g", "f", 3), ref, ref, p.at(y=3))
    yield
    net.need(("g", "z"))
    for i in (2, 1, 3):
        net.send(("g", "p", i), out.at[tq], out.at[tq], p.at(y=i))
    yield
    net.need(*[("g", k, i) for k, i in (("r", 1), ("l", 0), ("f", 1), ("f", 3))])
    net.need(*[("g", "p", i) for i in (1, 2, 3)])


def forward_kernel(*refs):
    lengths, q_in, o_in, g_in, gu_in, dn_in, c_in, hidden_in, bias_in, cos_in, sin_in = refs[:11]
    w1, w2, mw, cg, probs, normed, queries, keys_values, attended, middle, normed_two, gains = refs[
        11:23
    ]
    (
        w_q, w_o, w_g, w_gu, w_dn, hid, bias, cos, sin, mask, pad1, pad2, wide, wide2, blk1, blk2,
        w1v, w2v, gn, kv, kv_own, prob, stack, nrm, m_own, c_own,
        a1, a2, tile, send_sems, recv_sems, load_sems, store_sems,
    ) = refs[23:]
    p = Place()
    f, c, t, y, zl, zh = p.f, p.c, p.t, p.y, p.zl, p.zh
    loads, stores = Loads(load_sems), Loads(store_sems)
    loads.start("a", q_in, w_q)
    loads.start("n", g_in, w_g)
    loads.start("o", o_in, w_o)
    loads.start("u", gu_in, w_gu)
    loads.start("d", dn_in, w_dn)
    loads.start("g", c_in, c_own)
    for name, src, dst in (
        ("h", hidden_in, hid), ("b", bias_in, bias), ("c", cos_in, cos), ("s", sin_in, sin),
    ):
        loads.start(name, src, dst)
    greet(
        [p.at(c=1)]
        + [p.at(x=i) for i in (1, 2, 3)]
        + [p.at(y=i) for i in (1, 2, 3)]
        + [p.at(z=i) for i in (1, 2, 3)]
        + [p.mirror(i) for i in (1, 2, 3)]
    )
    net = Net(send_sems, recv_sems)
    steps = Steps(FORWARD_ORDER)
    tile[...] = jnp.zeros_like(tile)
    loads.need("a", "n")
    tile[pl.ds(0, 2), pl.ds(0, 12)] = w_g[...]
    wide[pl.ds(0, 16), pl.ds(2048, 128)] = tile[...].T[:16]
    wide[pl.ds(0, 12), pl.ds(0, 2048)] = w_q[...]
    wide[pl.ds(12, 4), pl.ds(0, 2048)] = jnp.zeros((4, 2048), F32)
    a1[...] = wide[pl.ds(0, 16), :].astype(BF)
    z_cols, o_cols = lanes(zl, 512), lanes(zl, 768)
    q_part, kv_part = pl.ds(0, 1536), pl.ds(1536, 640)
    x_three = (1, 3, 2)
    rows_1 = gather_rows_flow(net, p, "e", a1.at[:, kv_part], pad1.at[:, :, kv_part])
    next(rows_1)
    pad1[t] = a1[...]
    for i in range(3):
        m_own[:, pl.ds((i + 1) * FF_PAD - 128, 128)] = jnp.zeros((96, 128), BF)
    loads.need("u", "d")
    ff_dev = w_dn.shape[1]

    def whole_tiles(i):
        at = pl.ds(pl.multiple_of(i * 16, 16), 16)
        for half in range(2):
            m_own[at, pl.ds(half * FF_PAD, ff_dev)] = w_gu[at, half, :].astype(BF)
        m_own[at, pl.ds(2 * FF_PAD, ff_dev)] = w_dn[at, :].astype(BF)

    each(6, whole_tiles)
    loads.need("g")
    stores.start("m", m_own, mw.at[f, c])
    stores.start("g", c_own, cg.at[t])

    def z_block(width):
        def block(i):
            zz = (p.z + i) % 4
            return (zz // 2) * 4, lanes(zz % 2, width)

        return block

    def y_flow_of(tag, begin):
        def cols(i):
            return pl.ds(pl.multiple_of(begin + ((y + i) % 4) * 128, 128), 128)

        cross_sends(net, p, tag, blk1.at[:, cols(0)], w1v.at[f, c, :, cols(0)])
        w1v[f, c, :, cols(0)] = blk1[:, cols(0)]
        yield
        net.need(*cross_names(tag))
        yield from ring_gather_flow(
            net, p, tag + 1, w1v, lambda i: p.at(y=i), lambda i: (0, cols(i)), 8
        )

    def query_flow():
        rows = gather_rows_flow(net, p, "a", a1.at[:, q_part], pad1.at[:, :, q_part])
        yield from rows
        close_up(pad1.at[:, :, q_part], wide, blk1.at[:, q_part])
        for i in x_three:
            net.send((1, "x", i), blk1.at[:, z_cols], w1v.at[f, c, :, z_cols], p.at(x=i))
        w1v[f, c, :, z_cols] = blk1[:, z_cols]
        steps.add("2", y_flow_of(10, 1024))
        yield
        net.need(*[(1, "x", i) for i in x_three])
        yield from ring_gather_flow(net, p, 4, w1v, lambda i: p.at(z=i), z_block(512), 4)

    def gains_flow():
        for i in x_three:
            net.send((3, "x", i), blk1.at[:, pl.ds(2048, 128)], gn.at[f, c], p.at(x=i))
        gn[f, c] = blk1[:, pl.ds(2048, 128)]
        yield
        net.need(*[(3, "x", i) for i in x_three])
        own_zh = pl.ds(zh * 4, 4)
        net.send((3, "m"), gn.at[own_zh, c], gn.at[own_zh, c], p.mirror())
        yield
        net.need((3, "m"))
        net.send((3, "c"), gn.at[:, c], gn.at[:, c], p.at(c=1))
        yield
        net.need((3, "c"))
        gains[...] = gn[...].reshape(1536, 128).astype(F32).T[:2]

    def out_flow():
        loads.need("o")
        wide2[pl.ds(0, 12), :] = w_o[...]
        wide2[pl.ds(12, 4), :] = jnp.zeros((4, 1536), F32)
        a2[...] = wide2[pl.ds(0, 16), :].astype(BF)
        rows = gather_rows_flow(net, p, "b", a2, pad2)
        next(rows)
        pad2[t] = a2[...]
        yield
        yield from rows
        close_up(pad2, wide2, blk2)
        for i in x_three:
            net.send((6, "x", i), blk2.at[:, o_cols], w2v.at[f, c, :, o_cols], p.at(x=i))
        w2v[f, c, :, o_cols] = blk2[:, o_cols]
        yield
        net.need(*[(6, "x", i) for i in x_three])
        yield from ring_gather_flow(net, p, 7, w2v, lambda i: p.at(z=i), z_block(768), 4)

    steps.add("m", weights_flow(net, p, m_own, mw))
    steps.add("c", cotangent_flow(net, p, c_in, cg))
    steps.add("o", out_flow())
    steps.add("1", query_flow())
    steps.point()
    ends = [lengths[0, 0]]
    for i in range(1, lengths.shape[1]):
        ends.append(ends[-1] + lengths[0, i])
    asks = t * 128 + lax.broadcasted_iota(jnp.int32, mask.shape, 0)
    keys_at = lax.broadcasted_iota(jnp.int32, mask.shape, 1)

    def document(places):
        return sum((places >= end).astype(jnp.int32) for end in ends)

    allowed = (document(asks) == document(keys_at)) & (keys_at <= asks)
    mask[...] = jnp.where(allowed, 1.0, 0.0)
    next(rows_1)
    steps.point()
    next(rows_1, None)
    close_up(pad1.at[:, :, kv_part], wide, blk1.at[:, kv_part])
    steps.add("v", y_flow_of(12, 1536))
    steps.add("g", gains_flow())
    for _ in range(10):
        steps.point()
    steps.finish("g")
    loads.need("h")

    def norm_one(i):
        at = pl.ds(pl.multiple_of(i * 16, 16), 16)
        v = hid[at, :].astype(F32)
        r = lax.rsqrt(jnp.mean(v * v, axis=-1, keepdims=True) + norm_eps)
        nrm[at, :] = (v * r * gains[pl.ds(0, 1), :]).astype(BF)

    each(8, norm_one)
    stores.start("n", nrm, normed)
    for _ in range(8):
        steps.point()
    steps.finish("v")
    steps.point()
    loads.need("b", "c", "s")
    size = HEAD_SIZE
    weights = w1v.reshape(1536, 2048)

    def project(first, count):
        total = dots(nrm[...], weights[:, pl.ds(first * size, count * size)], 1, 0)
        return [
            total[:, i * size : (i + 1) * size] + bias[pl.ds(first + i, 1), :].astype(BF).astype(F32)
            for i in range(count)
        ]

    def turn(value):
        return (value * cos[...] + pltpu.roll(value, size // 2, 1) * sin[...]).astype(BF)

    for i, value in enumerate(project(QUERY_HEADS, 2 * KEY_VALUE_HEADS)):
        kv_own[:, pl.ds(i * size, size)] = turn(value) if i < KEY_VALUE_HEADS else value.astype(BF)
    kv[t] = kv_own[...]

    def keys_flow():
        zp, tq = p.partner(), y * 2 + 1 - zl
        net.send(("k", "z"), kv_own, kv.at[t], zp)
        for i in (2, 1, 3):
            net.send(("k", "y", i), kv_own, kv.at[t], p.at(y=i))
        yield
        net.need(("k", "z"))
        for i in (2, 1, 3):
            net.send(("k", "p", i), kv.at[tq], kv.at[tq], p.at(y=i))
        yield
        net.need(*[("k", k, i) for k in "yp" for i in (1, 2, 3)])

    steps.add("k", keys_flow())
    for _ in range(10):
        steps.point()
    steps.finish("1", "2")
    stores.start(1, w1v, w1)
    for j in range(3):
        for i, value in enumerate(project(j * 4, 4)):
            stack[pl.ds((j * 4 + i) * size, size), :] = turn(value)
        steps.point()
    for _ in range(4):
        steps.point()
    steps.finish("k")
    stores.start("k", kv, keys_values)
    scale = size**-0.5
    for group in range(KEY_VALUE_HEADS):
        at_k, at_v = pl.ds(group * size, size), pl.ds((KEY_VALUE_HEADS + group) * size, size)

        def heads(j):
            rows = pl.ds(pl.multiple_of(group * 768 + j * 256, 256), 256)
            keys = kv[:, :, at_k].reshape(1024, size)
            values = kv[:, :, at_v].reshape(1024, size)
            score = dots(stack[rows, :], keys, 1, 1).reshape(2, 128, 1024) * scale
            score = jnp.where(mask[...][None] > 0.0, score, -1e30)
            top = jnp.max(score, axis=-1, keepdims=True)
            power = jnp.exp(score - top)
            share = power * (1.0 / jnp.sum(power, axis=-1, keepdims=True))
            share = share.astype(BF).reshape(256, 1024)
            prob[rows, :] = share
            total = dots(share, values, 1, 0).astype(BF)
            for i in range(2):
                head = group * 6 + j * 2 + i
                to = pl.ds(pl.multiple_of(head * size, size), size)
                attended[:, to] = total[i * size : (i + 1) * size]
                queries[:, to] = stack[pl.ds(pl.multiple_of(head * size, size), size), :]

        each(3, heads)
        steps.point()
    stores.start("p", prob, probs)
    for _ in range(6):
        steps.point()
    steps.finish("o")
    stores.start(2, w2v, w2)
    out_weights = w2v.reshape(1536, 1536)

    def project_out(j):
        at = pl.ds(pl.multiple_of(j * 512, 512), 512)
        middle[:, at] = hid[:, at].astype(F32) + dots(attended[...], out_weights[at, :], 1, 1)

    each(3, project_out)
    steps.point()

    def norm_two(i):
        at = pl.ds(pl.multiple_of(i * 16, 16), 16)
        v = middle[at, :]
        r = lax.rsqrt(jnp.mean(v * v, axis=-1, keepdims=True) + norm_eps)
        normed_two[at, :] = (v * r * gains[pl.ds(1, 1), :]).astype(BF)

    each(8, norm_two)
    for _ in range(6):
        steps.point()
    steps.finish("c", "m")
    net.finish()
    stores.need("m", "g", "n", 1, "k", "p", 2)


def forward(*args, cid=0, name="forward"):
    vm = pl.BlockSpec(memory_space=pltpu.VMEM)
    hbm = pl.BlockSpec(memory_space=pl.ANY)
    V = lambda *s: pltpu.VMEM(s, BF)
    W = lambda *s: pltpu.VMEM(s, F32)
    B = lambda *s: jax.ShapeDtypeStruct(s, BF)
    S = lambda *s: jax.ShapeDtypeStruct(s, F32)
    D = pltpu.SemaphoreType.DMA
    n = 130
    return pl.pallas_call(
        forward_kernel,
        out_shape=(
            B(8, 2, 96, 2048), B(8, 2, 96, 1536), B(8, 2, 96, 3 * FF_PAD), B(8, 128, 1536),
            B(1536, 1024), B(128, 1536), B(128, 1536), B(8, 128, 512), B(128, 1536),
            S(128, 1536), B(128, 1536), S(2, 1536),
        ),
        in_specs=[pl.BlockSpec(memory_space=pltpu.SMEM)] + [hbm] * (len(args) - 1),
        out_specs=(hbm,) * 6 + (vm, hbm) + (vm,) * 4,
        scratch_shapes=[pltpu.VMEM(args[i].shape, args[i].dtype) for i in (1, 2, 3, 4, 5, 7, 8, 9, 10)]
        + [
            W(128, 1024),

            V(8, 16, 2176), V(8, 16, 1536), W(96, 2176), W(96, 1536), V(96, 2176), V(96, 1536),
            V(8, 2, 96, 2048), V(8, 2, 96, 1536), V(8, 2, 96, 128), V(8, 128, 512), V(128, 512),
            V(1536, 1024), V(1536, 128), V(128, 1536), V(96, 3 * FF_PAD), V(128, 1536),
            V(16, 2176), V(16, 1536), W(128, 128),
            D((n,)), D((n,)), D((10,)), D((7,)),
        ],
        name=name,
        compiler_params=pltpu.CompilerParams(
            collective_id=cid, has_side_effects=True, vmem_limit_bytes=60 << 20
        ),
    )(*args)


def positions(lengths, places):
    starts = jnp.cumsum(lengths) - lengths
    latest = jnp.where(starts[None, :] <= places[:, None], starts[None, :], 0)
    return places - jnp.max(latest, axis=1)


def rotary_tables(position, size):
    half = size // 2
    lane = jnp.arange(size, dtype=jnp.int32)
    freq = jnp.exp((lane % half).astype(F32) * (-2.0 * math.log(rope_base) / size))
    angle = position.astype(F32)[:, None] * freq[None, :]
    return (jnp.cos(angle), jnp.where(lane < half, -1.0, 1.0)[None, :] * jnp.sin(angle))


def adam_step(weight, moment, second, grad, rate, decay):
    moment = beta_one * moment + (1.0 - beta_one) * grad
    second = beta_two * second + (1.0 - beta_two) * grad * grad
    fix_one = 1.0 - beta_one**STEP
    fix_two = 1.0 - beta_two**STEP
    direction = moment / fix_one / (jnp.sqrt(second / fix_two) + adam_eps)
    return (weight - rate * (direction + decay * weight), moment, second)


def adam_kernel(*refs):
    far, outs, rest = refs[:22], refs[22:39], list(refs[39:])
    near, new, (load_sems, store_sems) = rest[:22], rest[22:37], rest[37:]
    loads, stores = Loads(load_sems), Loads(store_sems)
    for i in (2, 14, 15, 16, 20, 21, 3, 11, 12, 13, 0, 5, 6, 7, 1, 8, 9, 10, 4, 17, 18, 19):
        loads.start(i, far[i], near[i])
    g_qkv, g_out, g_gate_up, g_down, g_bias = near[:5]
    rows, width = near[5].shape[0], near[14].shape[2]

    def group(k):
        return near[5 + 3 * k : 8 + 3 * k], new[3 * k : 3 * k + 3]

    def store(k):
        for i in range(3 * k, 3 * k + 3):
            stores.start(i, new[i], outs[i])

    loads.need(2, 14, 15, 16)
    params, results = group(3)
    for half in range(2):

        def body(i):
            at = pl.ds(pl.multiple_of(i * 8, 8), 8)
            now = [ref[at, half, :] for ref in params]
            grad = g_gate_up[at, pl.ds(half * FF_PAD, width)]
            after = adam_step(*now, grad, rate_gate_up, weight_decay)
            for ref, value in zip(results, after):
                ref[at, half, :] = value

        each(params[0].shape[0] // 8, body)
    store(3)
    loads.need(20, 21)
    for i in (20, 21):
        stores.start(i, near[i], outs[i - 5])
    for k, i, grad, rate, decay in (
        (2, 3, g_down.at[:, pl.ds(0, width)], rate_down, weight_decay),
        (0, 0, g_qkv.at[pl.ds(0, rows)], rate_qkv, weight_decay),
        (1, 1, g_out.at[pl.ds(0, rows)], rate_out, weight_decay),
        (4, 4, g_bias.at[pl.ds(0, 16)], rate_small, 0.0),
    ):
        params, results = group(k)
        loads.need(i, *range(5 + 3 * k, 8 + 3 * k))
        after = adam_step(*[ref[...] for ref in params], grad[...], rate, decay)
        for ref, value in zip(results, after):
            ref[...] = value
        store(k)
    stores.need(*range(15), 20, 21)


def adam(grads, params, passed):
    hbm = pl.BlockSpec(memory_space=pl.ANY)
    inputs = [*grads, *params, *passed]
    results = [*params, *passed]
    return pl.pallas_call(
        adam_kernel,
        out_shape=tuple(jax.ShapeDtypeStruct(a.shape, F32) for a in results),
        in_specs=[hbm] * len(inputs),
        out_specs=(hbm,) * len(results),
        scratch_shapes=[pltpu.VMEM(a.shape, F32) for a in inputs]
        + [pltpu.VMEM(a.shape, F32) for a in params]
        + [pltpu.SemaphoreType.DMA((len(inputs),)), pltpu.SemaphoreType.DMA((len(results),))],
        name="adam",
        compiler_params=pltpu.CompilerParams(vmem_limit_bytes=56 << 20),
    )(*inputs)


def on_device(
    hidden_in,
    cotangent,
    seq_lengths,
    w_qkv,
    m_qkv,
    v_qkv,
    b_qkv,
    m_bias,
    v_bias,
    w_out,
    m_out,
    v_out,
    w_gate_up,
    m_gate_up,
    v_gate_up,
    w_down,
    m_down,
    v_down,
    gains,
    m_gains,
    v_gains,
):
    token_rows = hidden_in.shape[0]
    model_width = hidden_in.shape[1]
    tp_count = lax.axis_size(TP)
    packed_length = token_rows * tp_count
    own_places = lax.axis_index(TP) * token_rows + jnp.arange(token_rows, dtype=jnp.int32)
    own_pos = positions(seq_lengths[0], own_places)
    cos_row, sin_row = rotary_tables(own_pos, HEAD_SIZE)
    (
        qkv_full, out_turned, mlp_full, grad_group,
        probs, normed_one, queries, keys_values, attended, middle, normed_two, gains_full,
    ) = forward(
        seq_lengths,
        w_qkv,
        w_out.T,
        gains,
        w_gate_up,
        w_down.T,
        cotangent,
        hidden_in,
        b_qkv.reshape(-1, 128),
        cos_row,
        sin_row,
    )
    grad_normed_two, down_parts, grad_w_gate_up, grad_w_down = feed_forward(
        normed_two, grad_group, mlp_full.reshape(model_width, -1)
    )
    hidden_out, grad_in, owned_qkv, owned_out, owned_gate_up, owned_down, small = backward(
        [
            grad_w_gate_up,
            grad_w_down,
            down_parts,
            out_turned.reshape(model_width, -1),
            qkv_full.reshape(model_width, -1),
            probs,
        ],
        [
            grad_normed_two,
            middle,
            cotangent,
            hidden_in,
            normed_one,
            attended,
            queries,
            keys_values.reshape(packed_length, -1),
            cos_row,
            sin_row,
            gains_full,
        ],
    )
    own_gains = gains.shape[1]
    summed_gains = small[b_qkv.shape[0] // 128 :].reshape(2, model_width)
    owned_gains = lax.dynamic_slice_in_dim(
        summed_gains, lax.axis_index(ALL) * own_gains, own_gains, axis=1
    )
    gains_new, gains_moment, gains_second = adam_step(
        gains, m_gains, v_gains, owned_gains, rate_small, 0.0
    )
    params = [w_qkv, m_qkv, v_qkv]
    params += [a.T for a in (w_out, m_out, v_out)]
    params += [a.T for a in (w_down, m_down, v_down)]
    params += [w_gate_up, m_gate_up, v_gate_up]
    params += [a.reshape(-1, 128) for a in (b_qkv, m_bias, v_bias)]
    new = adam(
        [owned_qkv, owned_out, owned_gate_up, owned_down, small], params, [hidden_out, grad_in]
    )
    hidden_out, grad_in = new[15:]
    qkv_new, qkv_moment, qkv_second = new[:3]
    out_new, out_moment, out_second = [a.T for a in new[3:6]]
    down_new, down_moment, down_second = [a.T for a in new[6:9]]
    gate_up_new, gate_up_moment, gate_up_second = new[9:12]
    bias_new, bias_moment, bias_second = [a.reshape(-1) for a in new[12:15]]
    return (
        hidden_out,
        grad_in,
        qkv_new,
        qkv_moment,
        qkv_second,
        bias_new,
        bias_moment,
        bias_second,
        out_new,
        out_moment,
        out_second,
        gate_up_new,
        gate_up_moment,
        gate_up_second,
        down_new,
        down_moment,
        down_second,
        gains_new,
        gains_moment,
        gains_second,
    )


def solution(mesh):
    placed = (
        P((FS, CX, TP), None),
        P((FS, CX, TP), None),
        P((FS, CX), None),
        P((FS, CX, TP), None),
        P((FS, CX, TP), None),
        P((FS, CX, TP), None),
        P(),
        P(),
        P(),
        P(None, (FS, CX, TP)),
        P(None, (FS, CX, TP)),
        P(None, (FS, CX, TP)),
        P((FS, CX), None, TP),
        P((FS, CX), None, TP),
        P((FS, CX), None, TP),
        P(TP, (FS, CX)),
        P(TP, (FS, CX)),
        P(TP, (FS, CX)),
        P(None, (FS, CX, TP)),
        P(None, (FS, CX, TP)),
        P(None, (FS, CX, TP)),
    )
    return jax.shard_map(
        on_device,
        mesh=mesh,
        in_specs=placed,
        out_specs=(
            P((FS, CX, TP), None),
            P((FS, CX, TP), None),
            P((FS, CX, TP), None),
            P((FS, CX, TP), None),
            P((FS, CX, TP), None),
            P(),
            P(),
            P(),
            P(None, (FS, CX, TP)),
            P(None, (FS, CX, TP)),
            P(None, (FS, CX, TP)),
            P((FS, CX), None, TP),
            P((FS, CX), None, TP),
            P((FS, CX), None, TP),
            P(TP, (FS, CX)),
            P(TP, (FS, CX)),
            P(TP, (FS, CX)),
            P(None, (FS, CX, TP)),
            P(None, (FS, CX, TP)),
            P(None, (FS, CX, TP)),
        ),
        check_vma=False,
    )
```

```python
import functools
import math

import jax
import jax.numpy as jnp
from jax import lax
from jax.experimental import pallas as pl
from jax.experimental.pallas import tpu as pltpu
from jax.sharding import PartitionSpec as P

QUERY_HEADS = 12
KEY_VALUE_HEADS = 2
HEAD_SIZE = 128
STEP = 10


norm_eps = 1e-06
rope_base = 1000000.0
beta_one = 0.9
beta_two = 0.95
adam_eps = 1e-08
weight_decay = 0.1
rate_qkv = 0.05
rate_out = 0.3
rate_gate_up = 0.05
rate_down = 0.02
rate_small = 0.5

BF = jnp.bfloat16
F32 = jnp.float32
FS, CX, TP = ALL = ("fsdp", "ctx", "tp")
FF_PAD = 1152
FORWARD_ORDER = (
    "21mmc", "1", "gc", "", "oc", "v1", "mog", "v", "", "1g", "c", "", "2ov", "2", "", "", "",
    "", "m", "", "", "", "", "mvk", "", "m", "1", "", "k2", "cmo", "g", "", "o2", "mm", "",
    "m1", "", "", "", "1ov", "", "m", "", "k", "", "", "c", "m", "", "", "", "o", "",
)
BACKWARD_ORDER = (
    "b", "", "hab", "ob", "", "oab", "", "k", "", "", "b", "", "q", "ak", "ook", "aq", "", "",
    "", "qv", "q", "", "", "v", "", "r", "", "rar", "h", "", "", "", "", "o", "", "th", "trb",
    "v", "", "", "", "qhvtr", "", "t", "", "", "", "", "", "", "", "q", "", "a", "", "o", "h",
    "", "", "rkt",
)


class Place:
    def __init__(self):
        self.f = lax.axis_index(FS)
        self.c = lax.axis_index(CX)
        self.t = lax.axis_index(TP)
        self.zh, self.x = self.f // 4, self.f % 4
        self.y, self.zl = self.t // 2, self.t % 2
        self.z = self.zh * 2 + self.zl

    def at(self, x=0, y=0, z=0, c=0):
        zz = (self.z + z) % 4
        return {
            FS: (zz // 2) * 4 + (self.x + x) % 4,
            CX: (self.c + c) % 2,
            TP: ((self.y + y) % 4) * 2 + zz % 2,
        }

    def partner(self):
        return {FS: self.f, CX: self.c, TP: self.y * 2 + 1 - self.zl}

    def mirror(self, x=0):
        return {
            FS: (1 - self.zh) * 4 + (self.x + x) % 4,
            CX: self.c,
            TP: self.y * 2 + 1 - self.zl,
        }


def greet(devices):
    barrier = pltpu.get_barrier_semaphore()
    for device in devices:
        pl.semaphore_signal(barrier, inc=1, device_id=device, device_id_type=pl.DeviceIdType.MESH)
    pl.semaphore_wait(barrier, len(devices))


class Steps:
    def __init__(self, order):
        self.flows, self.order, self.at = {}, order, 0

    def add(self, name, flow):
        self.flows[name] = flow

    def point(self):
        for name in self.order[self.at]:
            if name in self.flows:
                next(self.flows[name], None)
        self.at += 1

    def finish(self, *names):
        for name in names:
            for _ in self.flows[name]:
                pass


class Loads:
    def __init__(self, sems):
        self.sems, self.used, self.copies = sems, 0, {}

    def start(self, name, src, dst):
        copy = pltpu.make_async_copy(src, dst, self.sems.at[self.used])
        self.used += 1
        copy.start()
        self.copies[name] = copy

    def need(self, *names):
        for name in names:
            self.copies.pop(name).wait()


class Net:
    def __init__(self, send_sems, recv_sems):
        self.send_sems, self.recv_sems = send_sems, recv_sems
        self.copies, self.arrived = {}, set()

    def send(self, name, src, dst, device, after=()):
        self.need(*after)
        at = len(self.copies)
        copy = pltpu.make_async_remote_copy(
            src_ref=src,
            dst_ref=dst,
            send_sem=self.send_sems.at[at],
            recv_sem=self.recv_sems.at[at],
            device_id=device,
            device_id_type=pl.DeviceIdType.MESH,
        )
        copy.start()
        self.copies[name] = copy

    def need(self, *names):
        for name in names:
            if name not in self.arrived:
                self.arrived.add(name)
                self.copies[name].wait_recv()

    def finish(self):
        self.need(*self.copies)
        for copy in self.copies.values():
            copy.wait_send()


def lanes(at, size):
    return pl.ds(pl.multiple_of(at * size, 128), size)


def each(n, body):
    def step(i, carry):
        body(i)
        return carry

    lax.fori_loop(0, n, step, 0)


def add_rows(dst, first, others, rows):
    width = dst.shape[-1]
    step = max(k for k in range(16, rows + 1, 16) if rows % k == 0 and (k * width <= 49152 or k == 16))

    def body(i):
        at = pl.ds(pl.multiple_of(i * step, 16), step)
        if len(others) == 1 and dst.dtype == BF:
            dst[at, :] = first[at, :] + others[0][at, :]
        else:
            total = first[at, :].astype(F32)
            for other in others:
                total += other[at, :].astype(F32)
            dst[at, :] = total.astype(dst.dtype)

    if step == rows:
        body(0)
    else:
        each(rows // step, body)


def advance(*flows):
    for flow in flows:
        next(flow, None)


def tp_gather_flow(net, p, tag, own, out, rows):
    y, zl, t = p.y, p.zl, p.t
    tq = y * 2 + 1 - zl
    zp = p.partner()
    top, low = pl.ds(0, rows // 2), pl.ds(rows // 2, rows // 2)
    net.send((tag, "z"), own, out.at[t], zp)
    net.send((tag, "r", 0), own.at[top], out.at[t, top], p.at(y=1))
    net.send((tag, "l", 1), own.at[low], out.at[t, low], p.at(y=3))
    net.send((tag, "r", 1), own.at[low], out.at[t, low], p.at(y=1))
    net.send((tag, "l", 0), own.at[top], out.at[t, top], p.at(y=3))
    yield
    net.need((tag, "z"))
    net.send((tag, "p", 1), out.at[tq], out.at[tq], p.at(y=1))
    net.send((tag, "p", 3), out.at[tq], out.at[tq], p.at(y=3))
    yield
    ref = out.at[((y + 3) % 4) * 2 + zl, top]
    net.send((tag, "f", 1), ref, ref, p.at(y=1), after=[(tag, "r", 0)])
    ref = out.at[((y + 1) % 4) * 2 + zl, low]
    net.send((tag, "f", 3), ref, ref, p.at(y=3), after=[(tag, "l", 1)])
    yield
    ref = out.at[((y + 2) % 4) * 2 + zl]
    net.send((tag, "o"), ref, ref, zp, after=[(tag, "f", 1), (tag, "f", 3)])


def sum_side(net, p, tag, part, bufs, cols, i):
    src = part.at[((p.y + i) % 4) * 2 + 1 - p.zl]
    dst = bufs[1 if i == 1 else 2]
    for k, at in cols:
        net.send((tag, "p", i, k), src.at[:, at], dst.at[:, at], p.at(y=i))


def split_cols(width, chunks):
    w = width // chunks
    return [(k, pl.ds(k * w, w)) for k in range(chunks)]


def tp_sum_flow(net, p, tag, part, out, bufs, chunks, sent=False, loads=None, base=None):
    ro, rp1, rp3, rh1, rh3, rw1, rw3, rq, sb, sq, s1, s3 = bufs
    y, zl, t = p.y, p.zl, p.t
    zp = p.partner()
    rows, width = out.shape
    half = rows // 2
    top, low = pl.ds(0, half), pl.ds(half, half)
    cols = split_cols(width, chunks)

    def mine(i):
        return part.at[((y + i) % 4) * 2 + zl]

    def theirs(i):
        return part.at[((y + i) % 4) * 2 + 1 - zl]

    far, cross, right, left, own = mine(2), theirs(0), mine(1), mine(3), mine(0)
    copies = []
    if loads is not None:
        wanted = zip((far, cross, right, left, own), (sb, sq, s1, s3, loads[0]))
        copies = [
            pltpu.make_async_copy(src, dst, loads[1].at[i]) for i, (src, dst) in enumerate(wanted)
        ]
        far, cross, right, left, own = sb, sq, s1, s3, loads[0]
    for copy in copies:
        copy.start()
    for k, at in cols:
        net.send((tag, "o", k), theirs(2).at[:, at], ro.at[:, at], zp)
    if not sent:
        for i in (1, 3):
            sum_side(net, p, tag, part, bufs, cols, i)
    yield
    for copy in copies:
        copy.wait()
    for k, at in cols:
        net.need((tag, "o", k))
        add_rows(sb.at[:, at], far.at[:, at], [ro.at[:, at]], rows)
        net.send((tag, "h", 1, k), sb.at[low, at], rh1.at[:, at], p.at(y=1))
        net.send((tag, "h", 3, k), sb.at[top, at], rh3.at[:, at], p.at(y=3))
    yield
    for k, at in cols:
        net.need((tag, "p", 1, k), (tag, "p", 3, k))
        add_rows(sq.at[:, at], cross.at[:, at], [rp1.at[:, at], rp3.at[:, at]], rows)
        net.send((tag, "q", k), sq.at[:, at], rq.at[:, at], zp)
    yield
    for k, at in cols:
        net.need((tag, "h", 1, k))
        if loads is None:
            s1[top, at] = right[top, at]
            s3[low, at] = left[low, at]
        add_rows(s1.at[low, at], right.at[low, at], [rh1.at[:, at]], half)
        net.send((tag, "w", 1, k), s1.at[:, at], rw1.at[:, at], p.at(y=1))
        net.need((tag, "h", 3, k))
        add_rows(s3.at[top, at], left.at[top, at], [rh3.at[:, at]], half)
        net.send((tag, "w", 3, k), s3.at[:, at], rw3.at[:, at], p.at(y=3))
    yield
    for k, at in cols:
        net.need((tag, "q", k), (tag, "w", 1, k), (tag, "w", 3, k))
        others = [rq.at[:, at], rw1.at[:, at], rw3.at[:, at]]
        if base is not None:
            others.append(base.at[:, at])
        add_rows(out.at[:, at], own.at[:, at], others, rows)


def short_sum_flow(net, p, tag, part, out, bufs, chunks, sent=False):
    ro, rp1, rp3, rw1, rw3, rf, rq, sb, sq = bufs
    y, zl = p.y, p.zl
    zp = p.partner()
    rows, width = out.shape
    cols = split_cols(width, chunks)

    def mine(i):
        return part.at[((y + i) % 4) * 2 + zl]

    def theirs(i):
        return part.at[((y + i) % 4) * 2 + 1 - zl]

    for k, at in cols:
        net.send((tag, "o", k), theirs(2).at[:, at], ro.at[:, at], zp)
    if not sent:
        short_sides(net, p, tag, part, bufs, cols, True)
        short_sides(net, p, tag, part, bufs, cols, False)
    yield
    for k, at in cols:
        net.need((tag, "o", k))
        add_rows(sb.at[:, at], mine(2).at[:, at], [ro.at[:, at]], rows)
        net.send((tag, "f", k), sb.at[:, at], rf.at[:, at], p.at(y=2))
    yield
    for k, at in cols:
        net.need((tag, "p", 1, k), (tag, "p", 3, k))
        add_rows(sq.at[:, at], theirs(0).at[:, at], [rp1.at[:, at], rp3.at[:, at]], rows)
        net.send((tag, "q", k), sq.at[:, at], rq.at[:, at], zp)
    yield
    for k, at in cols:
        net.need((tag, "w", 1, k), (tag, "w", 3, k), (tag, "q", k), (tag, "f", k))
        others = [ref.at[:, at] for ref in (rq, rw1, rw3, rf)]
        add_rows(out.at[:, at], mine(0).at[:, at], others, rows)


def short_sides(net, p, tag, part, bufs, cols, theirs):
    for i in (1, 3):
        src = part.at[((p.y + i) % 4) * 2 + (1 - p.zl if theirs else p.zl)]
        dst = bufs[(1 if theirs else 3) + i // 2]
        for k, at in cols:
            name = (tag, "p" if theirs else "w", i, k)
            net.send(name, src.at[:, at], dst.at[:, at], p.at(y=i))


def dots(left, right, left_dim, right_dim):
    return lax.dot_general(
        left, right, (((left_dim,), (right_dim,)), ((), ())), preferred_element_type=F32
    )


def feed_forward_kernel(
    own, cot_in, weights_in, gn, hp_out, gu_out, dn_out,
    cot, weights, xs, gu, gh, hid, ggu, part, hp, dgu, dd, rgu, rdd, *rest,
):
    bufs, (send_sems, recv_sems, load_sems, store_sems) = rest[:9], rest[9:]
    p = Place()
    y, zl, c = p.y, p.zl, p.c
    sib = p.at(c=1)
    loads, stores = Loads(load_sems), Loads(store_sems)
    loads.start("x", own, xs.at[p.t])
    loads.start("c", cot_in, cot)
    loads.start("w", weights_in, weights)
    greet([sib, p.partner()] + [p.at(y=i) for i in (1, 2, 3)])
    net = Net(send_sems, recv_sems)
    t, tq, zp = p.t, y * 2 + 1 - zl, p.partner()
    top, low = pl.ds(0, 64), pl.ds(64, 64)
    net.send(("g", "z"), own, xs.at[t], zp)
    net.send(("g", "r", 0), own.at[top], xs.at[t, top], p.at(y=1))
    net.send(("g", "l", 1), own.at[low], xs.at[t, low], p.at(y=3))
    gate_up_at, down_at = pl.ds(0, 2 * FF_PAD), pl.ds(2 * FF_PAD, FF_PAD)
    loads.need("c", "w")

    def grad_hidden(i):
        at = pl.ds(i * 4, 4)
        gh[pl.ds(pl.multiple_of(i * 512, 512), 512), :] = dots(
            cot[at].reshape(512, -1), weights[:, down_at], 1, 0
        )

    grad_hidden(0)
    net.send(("g", "r", 1), own.at[low], xs.at[t, low], p.at(y=1))
    net.send(("g", "l", 0), own.at[top], xs.at[t, top], p.at(y=3))
    grad_hidden(1)

    def mine(i):
        return ((y + i) % 4) * 2 + zl

    def theirs(i):
        return ((y + i) % 4) * 2 + 1 - zl

    net.need(("g", "r", 0), ("g", "l", 1))
    net.send(("g", "f", 1), xs.at[mine(3), top], xs.at[mine(3), top], p.at(y=1))
    net.send(("g", "f", 3), xs.at[mine(1), low], xs.at[mine(1), low], p.at(y=3))
    net.need(("g", "z"))
    for i in (1, 3):
        net.send(("g", "p", i), xs.at[tq], xs.at[tq], p.at(y=i))
    loads.need("x")

    def pair(one, two, sends=()):
        def both(ref):
            return jnp.concatenate([ref[one], ref[two]], axis=0)

        gu[...] = dots(both(xs), weights[:, gate_up_at], 1, 0)
        for k, block in enumerate((one, two)):

            def gates(j):
                at = pl.ds(pl.multiple_of(k * 128 + j * 16, 16), 16)
                to = pl.ds(pl.multiple_of(j * 16, 16), 16)
                row = pl.ds(pl.multiple_of(block * 128 + j * 16, 16), 16)
                gate, up = gu[at, pl.ds(0, FF_PAD)], gu[at, pl.ds(FF_PAD, FF_PAD)]
                grad = gh[row, :]
                sigma = jax.nn.sigmoid(gate)
                activated = gate * sigma
                hid[block, to, :] = (activated * up).astype(BF)
                ggu[block, to, pl.ds(0, FF_PAD)] = (
                    grad * up * sigma * (1.0 + gate * (1.0 - sigma))
                ).astype(BF)
                ggu[block, to, pl.ds(FF_PAD, FF_PAD)] = (grad * activated).astype(BF)

            each(8, gates)
        for j in range(2):
            at = pl.ds(j * 768, 768)
            total = dots(both(ggu), weights[at, gate_up_at], 1, 1).astype(BF)
            part[one, :, at] = total[:128]
            part[two, :, at] = total[128:]
            for send in sends:
                send(j, at)

    def hidden_out(blocks):
        for j in range(2):
            at = pl.ds(j * 768, 768)
            rows = jnp.concatenate([hid[block] for block in blocks], axis=0)
            total = dots(rows, weights[at, down_at], 1, 1).astype(BF)
            for k, block in enumerate(blocks):
                hp[block, :, at] = total[k * 128 : k * 128 + 128]

    ro, rp1, rp3, rw1, rw3, rf, rq, sb, sq = bufs

    def side(name, i, src, dst):
        def send(j, at):
            net.send(("s", name, i, j), src.at[:, at], dst.at[:, at], p.at(y=i))

        return send

    def across(j, at):
        net.send(("s", "o", j), part.at[theirs(2), :, at], ro.at[:, at], zp)

    pair(mine(0), theirs(0))
    net.need(("g", "f", 1), ("g", "f", 3))
    net.send(("g", "o"), xs.at[mine(2)], xs.at[mine(2)], zp)
    net.need(("g", "r", 1), ("g", "l", 0))
    pair(mine(1), mine(3))
    hidden_out([mine(0), theirs(0), mine(1), mine(3)])
    net.need(("g", "p", 1), ("g", "p", 3))
    sides = [(1, rp1, rw1), (3, rp3, rw3)]
    pair(
        theirs(1), theirs(3), [side("p", i, part.at[theirs(i)], dst) for i, dst, _ in sides]
    )
    net.need(("g", "o"))
    pair(mine(2), theirs(2), [across])
    cols = split_cols(gn.shape[1], 2)
    for i, _, dst in sides:
        for j, at in cols:
            side("w", i, part.at[mine(i)], dst)(j, at)
    hidden_out([theirs(1), theirs(3), mine(2), theirs(2)])
    stores.start("h", hp, hp_out)
    rows = own.shape[0]
    def halves(ref, came, k):
        for f in (2 * k, 2 * k + 1):
            add_rows(ref.at[f, c], ref.at[f, c], [came.at[f]], 96)

    for k in range(4):
        two = pl.ds(k * 2, 2)

        def columns(j):
            at, to = pl.ds(k * 384, 384), pl.ds(pl.multiple_of(j * 768, 128), 768)
            left, right = xs[:, :, at].reshape(1024, 384), ggu[:, :, to].reshape(1024, 768)
            dgu[two, :, :, to] = dots(left, right, 0, 0).astype(BF).reshape(2, 2, 96, 768)

        each(3, columns)
        net.send(("e", k), dgu.at[two, 1 - c], rgu.at[two], sib)
        if k == 0:
            for j, at in cols:
                net.need(("s", "o", j))
                add_rows(sb.at[:, at], part.at[mine(2), :, at], [ro.at[:, at]], rows)
                net.send(("s", "f", j), sb.at[:, at], rf.at[:, at], p.at(y=2))
            for j, at in cols:
                net.need(("s", "p", 1, j), ("s", "p", 3, j))
                others = [rp1.at[:, at], rp3.at[:, at]]
                add_rows(sq.at[:, at], part.at[theirs(0), :, at], others, rows)
                net.send(("s", "q", j), sq.at[:, at], rq.at[:, at], zp)
        else:
            net.need(("e", k - 1))
            halves(dgu, rgu, k - 1)
    for k in range(4):
        two, at = pl.ds(k * 2, 2), pl.ds(k * 384, 384)
        total = dots(cot[:, :, at].reshape(1024, 384), hid[...].reshape(1024, -1), 0, 0)
        dd[two] = total.astype(BF).reshape(2, 2, 96, FF_PAD)
        net.send(("d", k), dd.at[two, 1 - c], rdd.at[two], sib)
        if k == 0:
            net.need(("e", 3))
            halves(dgu, rgu, 3)
            stores.start("g", dgu.at[:, c], gu_out)
        else:
            net.need(("d", k - 1))
            halves(dd, rdd, k - 1)
    for j, at in cols:
        net.need(("s", "w", 1, j), ("s", "w", 3, j), ("s", "q", j), ("s", "f", j))
        others = [ref.at[:, at] for ref in (rq, rw1, rw3, rf)]
        add_rows(gn.at[:, at], part.at[t, :, at], others, rows)
    net.need(("d", 3))
    halves(dd, rdd, 3)
    stores.start("d", dd.at[:, c], dn_out)
    stores.need("h", "d", "g")
    net.finish()


def feed_forward(own, cot, weights, cid=3, name="feed_forward"):
    vm = pl.BlockSpec(memory_space=pltpu.VMEM)
    hbm = pl.BlockSpec(memory_space=pl.ANY)
    rows, width = own.shape
    V = lambda *s: pltpu.VMEM(s, BF)
    whole = V(rows, width)
    B = lambda *s: jax.ShapeDtypeStruct(s, BF)
    D = pltpu.SemaphoreType.DMA
    n = 36
    return pl.pallas_call(
        feed_forward_kernel,
        out_shape=(
            jax.ShapeDtypeStruct((rows, width), F32),
            B(8, rows, width),
            B(8, 96, 2 * FF_PAD),
            B(8, 96, FF_PAD),
        ),
        in_specs=[hbm] * 3,
        out_specs=(vm, hbm, hbm, hbm),
        scratch_shapes=[
            V(8, rows, width),
            V(width, 3 * FF_PAD),
            V(8, rows, width),
            pltpu.VMEM((256, 2 * FF_PAD), F32),
            pltpu.VMEM((1024, FF_PAD), F32),
            V(8, 128, FF_PAD),
            V(8, 128, 2 * FF_PAD),
            V(8, rows, width),
            V(8, rows, width),
            V(8, 2, 96, 2 * FF_PAD),
            V(8, 2, 96, FF_PAD),
            V(8, 96, 2 * FF_PAD),
            V(8, 96, FF_PAD),
        ]
        + [whole] * 9
        + [D((n,)), D((n,)), D((3,)), D((3,))],
        name=name,
        compiler_params=pltpu.CompilerParams(
            collective_id=cid, has_side_effects=True, vmem_limit_bytes=63 << 20
        ),
    )(own, cot, weights)


def weight_flow(net, p, tag, g, acc, rh1, rh3, rw1, rw3, rz, out, local):
    x, zh = p.x, p.zh
    top, low = pl.ds(0, 48), pl.ds(48, 48)
    sides = (("o", 1 - zh), ("s", zh))
    own = pltpu.make_async_copy(g, acc, local)
    own.start()

    def at(i, side):
        return side * 4 + (x + i) % 4

    for k, (s, side) in enumerate(sides):
        b = at(2, side)
        net.send((tag, "h", 1, s), g.at[b, low], rh1.at[k], p.at(x=1))
        net.send((tag, "h", 3, s), g.at[b, top], rh3.at[k], p.at(x=3))
        yield
    own.wait()
    for k, (s, side) in enumerate(sides):
        b = at(1, side)
        net.need((tag, "h", 1, s))
        add_rows(acc.at[b, low], acc.at[b, low], [rh1.at[k]], 48)
        net.send((tag, "w", 1, s), acc.at[b], rw1.at[k], p.at(x=1))
        b = at(3, side)
        net.need((tag, "h", 3, s))
        add_rows(acc.at[b, top], acc.at[b, top], [rh3.at[k]], 48)
        net.send((tag, "w", 3, s), acc.at[b], rw3.at[k], p.at(x=3))
        yield
    b = at(0, 1 - zh)
    net.need((tag, "w", 1, "o"), (tag, "w", 3, "o"))
    add_rows(acc.at[b], acc.at[b], [rw1.at[0], rw3.at[0]], 96)
    net.send((tag, "z"), acc.at[b], rz, p.at(z=2))
    yield
    b = at(0, zh)
    net.need((tag, "w", 1, "s"), (tag, "w", 3, "s"), (tag, "z"))
    add_rows(out, acc.at[b], [rw1.at[1], rw3.at[1], rz], 96)


def small_flow(net, p, src, out, rc, rings):
    net.send(("t", "c"), src, rc, p.at(c=1))
    yield
    net.need(("t", "c"))
    out[...] = src[...] + rc[...]
    for k, (ring, place) in enumerate(zip(rings, (p.x, p.y, p.z))):
        ring[place] = out[...]
        for i in (1, 3, 2):
            step = {"xyz"[k]: i}
            net.send(("t", k, i), ring.at[place], ring.at[place], p.at(**step))
        yield
        net.need(("t", k, 1), ("t", k, 2), ("t", k, 3))
        out[...] = ring[0] + ring[1] + ring[2] + ring[3]


def ring_sum_flow(net, p, tag, g, rc, rh1, rh3, rw1, rw3, ring, block, count):
    c = p.c
    sib = p.at(c=1)
    top, low = pl.ds(0, 48), pl.ds(48, 48)

    def mine(i):
        first, cols = block(i)
        return g.at[pl.ds(first, count), c, :, cols]

    def theirs(i):
        first, cols = block(i)
        return g.at[pl.ds(first, count), 1 - c, :, cols]

    def landed(i):
        first, cols = block(i)
        return rc.at[pl.ds(first, count), :, cols]

    def add(dst, others, rows, skip=0):
        def body(i):
            to = dst.at[i, pl.ds(skip, rows)]
            add_rows(to, to, [other.at[i] for other in others], rows)

        each(count, body)

    for i in (2, 3, 1, 0):
        net.send((tag, "c", i), theirs(i), landed(i), sib)
    yield
    b = mine(2)
    net.need((tag, "c", 2))
    add(b, [landed(2)], 96)
    net.send((tag, "h", 1), b.at[:, low], rh1, ring(1))
    net.send((tag, "h", 3), b.at[:, top], rh3, ring(3))
    yield
    for i in (1, 3):
        net.need((tag, "c", i))
        add(mine(i), [landed(i)], 96)
    yield
    for i, came, skip in ((1, rh1, 48), (3, rh3, 0)):
        net.need((tag, "h", i))
        add(mine(i), [came], 48, skip)
        net.send((tag, "w", i), mine(i), rw1 if i == 1 else rw3, ring(i))
    yield
    net.need((tag, "c", 0), (tag, "w", 1), (tag, "w", 3))
    add(mine(0), [landed(0), rw1, rw3], 96)


def along_x(net, p, tag, src, rx, total):
    x = p.x
    for i in (1, 3, 2):
        net.send((tag, "x", i), src.at[(x + i) % 4], rx.at[i - 1], p.at(x=i))
    yield
    net.need((tag, "x", 1), (tag, "x", 2), (tag, "x", 3))
    add_rows(total, src.at[x], [rx.at[0], rx.at[1], rx.at[2]], 96)


def z_flow(net, p, tag, g, bufs, total, width):
    rc, rh1, rh3, rw1, rw3, rx = bufs

    def block(i):
        zz = (p.z + i) % 4
        return (zz // 2) * 4, lanes(zz % 2, width)

    yield from ring_sum_flow(
        net, p, tag, g, rc, rh1, rh3, rw1, rw3, lambda i: p.at(z=i), block, 4
    )
    src = g.at[pl.ds(p.zh * 4, 4), p.c, :, lanes(p.zl, width)]
    yield from along_x(net, p, tag, src, rx, total)


def cross_sum(net, p, tag, src, rx, total):
    x, zh = p.x, p.zh
    for i in (0, 1, 3, 2):
        ref = src.at[(1 - zh) * 4 + (x + i) % 4]
        net.send((tag, "m", i), ref, rx.at[3 + i], p.mirror(i))
    for i in (1, 3, 2):
        net.send((tag, "x", i), src.at[zh * 4 + (x + i) % 4], rx.at[i - 1], p.at(x=i))
    yield
    net.need(*[(tag, "m", i) for i in range(4)], *[(tag, "x", i) for i in range(1, 4)])
    add_rows(total, src.at[p.f], [rx.at[i] for i in range(7)], 96)


def y_flow(net, p, tag, g, bufs, total, width, begin):
    rc, rh1, rh3, rw1, rw3, rx = bufs
    part = g.at[:, :, :, pl.ds(begin, 4 * width)] if begin else g
    yield from ring_sum_flow(
        net,
        p,
        tag,
        part,
        rc,
        rh1,
        rh3,
        rw1,
        rw3,
        lambda i: p.at(y=i),
        lambda i: (0, lanes((p.y + i) % 4, width)),
        8,
    )
    yield from cross_sum(net, p, tag, part.at[:, p.c, :, lanes(p.y, width)], rx, total)


def y_direct_flow(net, p, tag, g, bufs, total, width, begin):
    rc, ry, rx = bufs
    part = g.at[:, :, :, pl.ds(begin, 4 * width)]
    mine, theirs = part.at[:, p.c], part.at[:, 1 - p.c]
    for i in (2, 1, 3, 0):
        cols = lanes((p.y + i) % 4, width)
        net.send((tag, "c", i), theirs.at[:, :, cols], rc.at[:, :, cols], p.at(c=1))
    yield
    for i in (2, 1, 3, 0):
        cols = lanes((p.y + i) % 4, width)
        block = mine.at[:, :, cols]
        net.need((tag, "c", i))

        def near(k):
            add_rows(block.at[k], block.at[k], [rc.at[k, :, cols]], 96)

        each(8, near)
        if i:
            net.send((tag, "w", i), block, ry.at[i - 1], p.at(y=i))
    yield
    block = mine.at[:, :, lanes(p.y, width)]
    net.need(*[(tag, "w", i) for i in (1, 3, 2)])

    def whole(k):
        add_rows(block.at[k], block.at[k], [ry.at[i, k] for i in range(3)], 96)

    each(8, whole)
    yield from cross_sum(net, p, tag, block, rx, total)


def tp_scatter(net, p, tag, totals, pads, fins, to):
    t = p.t
    at = 0
    for total in totals:
        width = total.shape[1]
        for i in range(8):
            pads[i, pl.ds(0, 12), pl.ds(at, width)] = total[pl.ds(12 * i, 12), :].astype(BF)
            pads[i, pl.ds(12, 4), pl.ds(at, width)] = jnp.zeros((4, width), BF)
        at += width
    for i in range(1, 8):
        net.send((tag, "f", i), pads.at[(t + i) % 8], fins.at[t], to[i - 1])
    fins[t] = pads[t]


def norm_back_rows(grad, values, gain, base, out, grad_gain):
    grad_gain[...] = jnp.zeros_like(grad_gain)

    def body(i):
        at = pl.ds(pl.multiple_of(i * 16, 16), 16)
        v = values[at, :].astype(F32)
        g = grad[at, :]
        r = lax.rsqrt(jnp.mean(v * v, axis=-1, keepdims=True) + norm_eps)
        a = g * gain
        grad_gain[...] += jnp.sum(g * v * r, axis=0, keepdims=True)
        back = r * a - v * r * r * r * jnp.mean(a * v, axis=-1, keepdims=True)
        out[at, :] = base[at, :].astype(F32) + back

    each(grad.shape[0] // 16, body)


def backward_kernel(*refs):
    ga, gb, hp, w2t, w1, probs = refs[:6]
    near_in = refs[6:17]
    h_out, grad_in, o1, o2, oa, ob, small = refs[17:24]
    rest = list(refs[24:])

    def take(n):
        out = rest[:n]
        del rest[:n]
        return out

    near = take(11)
    gn, middle, cot, hidden_in, normed, attended, queries, kv, cos, sin, gains = near
    m_bufs = [take(6), take(6)]
    q_bufs, q_total = take(6), take(1)[0]
    o_bufs, o_total = take(6), take(1)[0]
    r_bufs, r_total = take(6), take(1)[0]
    v_bufs, v_total = take(3), take(1)[0]
    hp_bufs, hp_own = take(12), take(1)[0]
    kv_bufs, kv_part, kv_sum = take(9), take(1)[0], take(1)[0]
    rcs, rs1, rs2, rs3 = take(4)
    pad_q, fin_q, pad_v, fin_v = take(4)
    wide, deep, g1, g_mid, g_proj, g_att, g_qkv, stack_q, stack_a = take(9)
    gain_two, gain_one, part_small, gno = take(4)
    send_sems, recv_sems, local_sems, hp_sems, load_sems = take(5)

    p = Place()
    t = p.t
    tp_all = [{FS: p.f, CX: p.c, TP: (t + i) % 8} for i in range(1, 8)]
    loads = Loads(load_sems)
    for i in (0, 1, 2, 10):
        loads.start(i, near_in[i], near[i])
    loads.start("w", w2t, wide)
    loads.start("p", probs, deep)
    for i in (5, 7, 6, 8, 9, 4, 3):
        loads.start(i, near_in[i], near[i])
    greet(
        [p.at(c=1)] + [p.at(x=i) for i in (1, 2, 3)] + tp_all + [p.at(z=2)]
        + [p.mirror(i) for i in range(4)]
    )
    net = Net(send_sems, recv_sems)
    steps = Steps(BACKWARD_ORDER)
    steps.add("a", weight_flow(net, p, "a", ga, *m_bufs[0], oa, local_sems.at[0]))
    steps.add("b", weight_flow(net, p, "b", gb, *m_bufs[1], ob, local_sems.at[1]))
    flow_h = tp_sum_flow(
        net, p, "h", hp, h_out, hp_bufs, 2, loads=(hp_own, hp_sems), base=middle
    )
    steps.add("h", flow_h)
    steps.point()
    loads.need(0, 1, 2, 10)
    norm_back_rows(gn, middle, gains[pl.ds(1, 1), :], cot, g_mid, gain_two)
    g_proj[...] = g_mid[...].astype(BF)
    steps.point()
    loads.need("w")

    def grad_attended(j):
        at = pl.ds(pl.multiple_of(j * 512, 512), 512)
        g_att[:, at] = dots(g_proj[...], wide[:, at], 1, 0).astype(BF)

    each(3, grad_attended)
    steps.point()
    loads.need(5)

    def grad_out(j):
        at = pl.ds(pl.multiple_of(j * 384, 128), 384)
        wide[at, :] = dots(g_proj[:, at], attended[...], 0, 0).astype(BF)

    each(4, grad_out)
    steps.add("o", y_flow(net, p, 2, wide.reshape(8, 2, 96, 1536), o_bufs, o_total, 384, 0))
    steps.point()
    loads.need("p", 7, 6)
    size = HEAD_SIZE
    scale = size**-0.5

    def stack(h):
        at = pl.ds(pl.multiple_of(h * size, size), size)
        stack_q[at, :] = queries[:, at]
        stack_a[at, :] = g_att[:, at]

    each(QUERY_HEADS, stack)
    group_rows = [pl.ds(768 * group, 768) for group in range(KEY_VALUE_HEADS)]

    def sums(left, right, first, factor):
        def body(j):
            at = pl.ds(pl.multiple_of(j * 256, 256), 256)
            for group, rows in enumerate(group_rows):
                grad = dots(left[rows, at], right[rows, :], 0, 0) * factor
                to = pl.ds((first + group) * size, size)
                kv_part[pl.ds(j * 2, 2), :, to] = grad.astype(BF).reshape(2, 128, size)

        each(4, body)

    sums(deep, stack_a, KEY_VALUE_HEADS, 1.0)
    steps.point()
    for group in range(KEY_VALUE_HEADS):
        values = kv.at[:, pl.ds((KEY_VALUE_HEADS + group) * size, size)]

        def heads(j):
            at = pl.ds(pl.multiple_of(group * 768 + j * 256, 256), 256)
            grad = dots(stack_a[at, :], values[...], 1, 1)
            weight = deep[at, :].astype(F32)
            inner = jnp.sum(weight * grad, axis=-1, keepdims=True)
            deep[at, :] = (weight * (grad - inner)).astype(BF)

        each(3, heads)
        steps.point()
    sums(deep, stack_q, 0, scale)
    steps.add("k", short_sum_flow(net, p, "k", kv_part, kv_sum, kv_bufs, 1))
    steps.point()
    loads.need(8, 9)

    def turned_back(grad):
        return (grad * cos[...] - pltpu.roll(grad, size // 2, 1) * sin[...]).astype(BF)

    for group in range(KEY_VALUE_HEADS):
        keys = kv.at[:, pl.ds(group * size, size)]

        def grad_query(j):
            at = pl.ds(pl.multiple_of(group * 768 + j * 256, 256), 256)
            grad = dots(deep[at, :], keys[...], 1, 0) * scale
            for i in range(2):
                to = pl.ds(pl.multiple_of((group * 6 + j * 2 + i) * size, size), size)
                g_qkv[:, to] = turned_back(grad[i * size : (i + 1) * size])

        each(3, grad_query)
        steps.point()
    loads.start("u", w1.at[:, pl.ds(0, 1024)], deep)
    loads.need(4)

    def grad_w(begin, count):
        at = pl.ds(begin, count)

        def body(j):
            d = pl.ds(pl.multiple_of(j * 384, 128), 384)
            total = dots(normed[:, d], g_qkv[:, at], 0, 0)
            g1[pl.ds(j * 2, 2), :, :, at] = total.astype(BF).reshape(2, 2, 96, count)

        each(4, body)

    grad_w(0, 1024)
    steps.add("q", z_flow(net, p, 1, g1, q_bufs, q_total, 512))
    steps.point()
    grad_w(1024, 512)
    steps.add("r", y_flow(net, p, 3, g1, r_bufs, r_total, 128, 1024))
    for _ in range(8):
        steps.point()
    steps.finish("k")
    for i in range(KEY_VALUE_HEADS):
        at, to = pl.ds(i * size, size), pl.ds((QUERY_HEADS + i) * size, size)
        g_qkv[:, to] = turned_back(kv_sum[:, at])
    at = pl.ds((QUERY_HEADS + KEY_VALUE_HEADS) * size, KEY_VALUE_HEADS * size)
    g_qkv[:, at] = kv_sum[:, pl.ds(KEY_VALUE_HEADS * size, KEY_VALUE_HEADS * size)].astype(BF)
    grad_w(1536, 512)
    steps.add("v", y_direct_flow(net, p, 4, g1, v_bufs, v_total, 128, 1536))
    for _ in range(4):
        steps.point()

    def normed_back(i):
        def body(j):
            at = pl.ds(pl.multiple_of(j * 512, 512), 512)
            total = dots(g_qkv[:, pl.ds(1024 * i, 1024)], deep[at, :], 1, 1)
            gno[:, at] = total if i == 0 else gno[:, at] + total

        each(3, body)

    loads.need("u")
    normed_back(0)
    loads.start("v", w1.at[:, pl.ds(1024, 1024)], deep)
    for _ in range(4):
        steps.point()
    loads.need("v")
    normed_back(1)
    loads.need(3)
    steps.point()
    norm_back_rows(gno, hidden_in, gains[pl.ds(0, 1), :], g_mid, grad_in, gain_one)
    bias = jnp.sum(g_qkv[...].astype(F32), axis=0, keepdims=True)
    for i in range(16):
        part_small[pl.ds(i, 1), :] = bias[:, i * 128 : i * 128 + 128]
    for i in range(12):
        part_small[pl.ds(16 + i, 1), :] = gain_one[:, pl.ds(i * 128, 128)]
        part_small[pl.ds(28 + i, 1), :] = gain_two[:, pl.ds(i * 128, 128)]
    steps.add("t", small_flow(net, p, part_small, small, rcs, (rs1, rs2, rs3)))
    for _ in range(14):
        steps.point()
    steps.finish("v")
    tp_scatter(net, p, 4, [v_total], pad_v, fin_v, tp_all)
    for _ in range(10):
        steps.point()
    steps.finish("q", "r", "o")
    tp_scatter(net, p, 2, [q_total, r_total, o_total], pad_q, fin_q, tp_all)
    for _ in range(8):
        steps.point()
    steps.finish("t", "a", "b", "h")
    net.need(*[(2, "f", i) for i in range(1, 8)])
    for k in range(2):
        at = pl.ds(0, 512)
        total = fin_q[k, :, at].astype(F32)
        for yy in range(1, 4):
            total += fin_q[2 * yy + k, :, at].astype(F32)
        o1[:, pl.ds(512 * k, 512)] = total
    for yy in range(4):
        at = pl.ds(512, 128)
        total = fin_q[2 * yy, :, at].astype(F32) + fin_q[2 * yy + 1, :, at].astype(F32)
        o1[:, pl.ds(1024 + 128 * yy, 128)] = total
        at = pl.ds(640, 384)
        total = fin_q[2 * yy, :, at].astype(F32) + fin_q[2 * yy + 1, :, at].astype(F32)
        o2[:, pl.ds(384 * yy, 384)] = total
    net.need(*[(4, "f", i) for i in range(1, 8)])
    for yy in range(4):
        total = fin_v[2 * yy].astype(F32) + fin_v[2 * yy + 1].astype(F32)
        o1[:, pl.ds(1536 + 128 * yy, 128)] = total
    net.finish()


def backward(far, near, cid=1, name="backward"):
    vm = pl.BlockSpec(memory_space=pltpu.VMEM)
    hbm = pl.BlockSpec(memory_space=pl.ANY)
    V = lambda *s: pltpu.VMEM(s, BF)
    W = lambda *s: pltpu.VMEM(s, F32)
    scratch = [pltpu.VMEM(a.shape, a.dtype) for a in near]
    for w in (far[0].shape[-1], far[1].shape[-1]):
        scratch += [
            V(8, 96, w), V(2, 48, w), V(2, 48, w), V(2, 96, w), V(2, 96, w), V(96, w),
        ]
    scratch += [
        V(8, 96, 1024), V(4, 48, 512), V(4, 48, 512), V(4, 96, 512), V(4, 96, 512), V(3, 96, 512),
        W(96, 512),
    ]
    for w in (384, 128):
        scratch += [
            V(8, 96, 4 * w), V(8, 48, w), V(8, 48, w), V(8, 96, w), V(8, 96, w), V(7, 96, w), W(96, w),
        ]
    scratch += [V(8, 96, 512), V(3, 8, 96, 128), V(7, 96, 128), W(96, 128)]
    whole, half = V(128, 1536), V(64, 1536)
    scratch += [whole] * 3 + [half] * 2 + [whole] * 7 + [whole]
    scratch += [V(128, 512)] * 9 + [V(8, 128, 512), W(128, 512)]
    scratch += [W(40, 128)] + [W(4, 40, 128)] * 3
    scratch += [V(8, 16, 1024)] * 2 + [V(8, 16, 128)] * 2
    scratch += [
        V(1536, 1536), V(1536, 1024), V(8, 2, 96, 2048), W(128, 1536), V(128, 1536), V(128, 1536),
        V(128, 2048), V(1536, 128), V(1536, 128),
        W(1, 1536), W(1, 1536), W(40, 128), W(128, 1536),
    ]
    n = 140
    D = pltpu.SemaphoreType.DMA
    scratch += [D((n,)), D((n,)), D((2,)), D((5,)), D((16,))]
    S = lambda *s: jax.ShapeDtypeStruct(s, F32)
    return pl.pallas_call(
        backward_kernel,
        out_shape=(
            S(128, 1536), S(128, 1536), S(16, 2048), S(16, 1536),
            S(96, far[0].shape[-1]), S(96, far[1].shape[-1]), S(40, 128),
        ),
        in_specs=[hbm] * (len(far) + len(near)),
        out_specs=(vm,) * 7,
        scratch_shapes=scratch,
        name=name,
        compiler_params=pltpu.CompilerParams(
            collective_id=cid, has_side_effects=True, vmem_limit_bytes=62 << 20
        ),
    )(*far, *near)


def gather_rows_flow(net, p, tag, own, pad):
    t, tq = p.t, p.y * 2 + 1 - p.zl
    net.send((tag, "z"), own, pad.at[t], p.partner())
    for i in (1, 3, 2):
        net.send((tag, "y", i), own, pad.at[t], p.at(y=i))
    yield
    net.need((tag, "z"))
    for i in (1, 3, 2):
        net.send((tag, "p", i), pad.at[tq], pad.at[tq], p.at(y=i))
    yield
    net.need(*[(tag, k, i) for k in "yp" for i in (1, 2, 3)])


def close_up(pad, wide, blk):
    width = pad.shape[-1]
    for i in range(8):
        wide[pl.ds(12 * i, 12), pl.ds(0, width)] = pad[i, pl.ds(0, 12), :].astype(F32)
    blk[...] = wide[:, pl.ds(0, width)].astype(BF)


def cross_sends(net, p, tag, src, place):
    for i in (1, 3, 2):
        net.send((tag, "x", i), src, place, p.at(x=i))
    for i in (0, 1, 3, 2):
        net.send((tag, "m", i), src, place, p.mirror(i))


def cross_names(tag):
    return [(tag, "x", i) for i in (1, 2, 3)] + [(tag, "m", i) for i in range(4)]


def ring_gather_flow(net, p, tag, w, ring, block, count):
    c = p.c
    top, low = pl.ds(0, 48), pl.ds(48, 48)

    def part(i, rows=None):
        first, cols = block(i)
        if rows is None:
            return w.at[pl.ds(first, count), c, :, cols]
        return w.at[pl.ds(first, count), c, rows, cols]

    sib = p.at(c=1)
    net.send((tag, "r", 1), part(0), part(0), ring(1))
    net.send((tag, "r", 3), part(0), part(0), ring(3))
    net.send((tag, "c", 0), part(0), part(0), sib)
    yield
    net.need((tag, "r", 1), (tag, "r", 3))
    net.send((tag, "f", 1), part(3, top), part(3, top), ring(1))
    net.send((tag, "f", 3), part(1, low), part(1, low), ring(3))
    net.send((tag, "c", 3), part(3), part(3), sib)
    net.send((tag, "c", 1), part(1), part(1), sib)
    yield
    net.need((tag, "f", 1), (tag, "f", 3))
    net.send((tag, "c", 2), part(2), part(2), sib)
    yield
    net.need(*[(tag, "c", i) for i in range(4)])


def weights_flow(net, p, m_in, mw):
    f, c, x, zh = p.f, p.c, p.x, p.zh
    top, low = pl.ds(0, 48), pl.ds(48, 48)
    sib = p.at(c=1)
    far = (1 - zh) * 4 + x

    def across(k, ff):
        net.send(("m", "c", k), mw.at[ff, c], mw.at[ff, c], sib)

    def ring(tag, src, ff):
        net.send((tag, "r", 0), src.at[top], mw.at[ff, c, top], p.at(x=1))
        net.send((tag, "l", 1), src.at[low], mw.at[ff, c, low], p.at(x=3))
        yield
        net.send((tag, "r", 1), src.at[low], mw.at[ff, c, low], p.at(x=1))
        net.send((tag, "l", 0), src.at[top], mw.at[ff, c, top], p.at(x=3))
        yield

    def onward(tag, side, k):
        after, before = side * 4 + (x + 1) % 4, side * 4 + (x + 3) % 4
        net.need((tag, "r", 0), (tag, "l", 1))
        ref = mw.at[before, c, top]
        net.send((tag, "f", 1), ref, ref, p.at(x=1))
        ref = mw.at[after, c, low]
        net.send((tag, "f", 3), ref, ref, p.at(x=3))
        yield
        net.need((tag, "r", 1), (tag, "l", 0))
        across(k, before)
        across(k + 1, after)
        yield
        net.need((tag, "f", 1), (tag, "f", 3))
        across(k + 2, side * 4 + (x + 2) % 4)
        yield

    net.send(("m", "z"), m_in, mw.at[f, c], p.at(z=2))
    yield
    yield from ring("m", m_in, f)
    net.send(("m", "c", 0), m_in, mw.at[f, c], sib)
    net.need(("m", "z"))
    yield from ring("n", mw.at[far, c], far)
    yield from onward("m", zh, 1)
    across(4, far)
    yield from onward("n", 1 - zh, 5)
    net.need(*[("m", "c", k) for k in range(8)])


def cotangent_flow(net, p, own, out):
    y, zl, t = p.y, p.zl, p.t
    tq = y * 2 + 1 - zl
    zp = p.partner()
    top, low = pl.ds(0, 64), pl.ds(64, 64)
    net.send(("g", "r", 0), own.at[top], out.at[t, top], p.at(y=1))
    net.send(("g", "l", 1), own.at[low], out.at[t, low], p.at(y=3))
    yield
    net.send(("g", "r", 1), own.at[low], out.at[t, low], p.at(y=1))
    net.send(("g", "l", 0), own.at[top], out.at[t, top], p.at(y=3))
    yield
    net.send(("g", "z"), own, out.at[t], zp)
    yield
    net.need(("g", "r", 0), ("g", "l", 1))
    ref = out.at[((y + 3) % 4) * 2 + zl, top]
    net.send(("g", "f", 1), ref, ref, p.at(y=1))
    ref = out.at[((y + 1) % 4) * 2 + zl, low]
    net.send(("g", "f", 3), ref, ref, p.at(y=3))
    yield
    net.need(("g", "z"))
    for i in (2, 1, 3):
        net.send(("g", "p", i), out.at[tq], out.at[tq], p.at(y=i))
    yield
    net.need(*[("g", k, i) for k, i in (("r", 1), ("l", 0), ("f", 1), ("f", 3))])
    net.need(*[("g", "p", i) for i in (1, 2, 3)])


def forward_kernel(*refs):
    lengths, q_in, o_in, g_in, gu_in, dn_in, c_in, hidden_in, bias_in, cos_in, sin_in = refs[:11]
    w1, w2, mw, cg, probs, normed, queries, keys_values, attended, middle, normed_two, gains = refs[
        11:23
    ]
    (
        w_q, w_o, w_g, w_gu, w_dn, hid, bias, cos, sin, mask, pad1, pad2, wide, wide2, blk1, blk2,
        w1v, w2v, gn, kv, kv_own, prob, stack, nrm, m_own, c_own,
        a1, a2, tile, send_sems, recv_sems, load_sems, store_sems,
    ) = refs[23:]
    p = Place()
    f, c, t, y, zl, zh = p.f, p.c, p.t, p.y, p.zl, p.zh
    loads, stores = Loads(load_sems), Loads(store_sems)
    loads.start("a", q_in, w_q)
    loads.start("n", g_in, w_g)
    loads.start("o", o_in, w_o)
    loads.start("u", gu_in, w_gu)
    loads.start("d", dn_in, w_dn)
    loads.start("g", c_in, c_own)
    for name, src, dst in (
        ("h", hidden_in, hid), ("b", bias_in, bias), ("c", cos_in, cos), ("s", sin_in, sin),
    ):
        loads.start(name, src, dst)
    greet(
        [p.at(c=1)]
        + [p.at(x=i) for i in (1, 2, 3)]
        + [p.at(y=i) for i in (1, 2, 3)]
        + [p.at(z=i) for i in (1, 2, 3)]
        + [p.mirror(i) for i in (1, 2, 3)]
    )
    net = Net(send_sems, recv_sems)
    steps = Steps(FORWARD_ORDER)
    tile[...] = jnp.zeros_like(tile)
    loads.need("a", "n")
    tile[pl.ds(0, 2), pl.ds(0, 12)] = w_g[...]
    wide[pl.ds(0, 16), pl.ds(2048, 128)] = tile[...].T[:16]
    wide[pl.ds(0, 12), pl.ds(0, 2048)] = w_q[...]
    wide[pl.ds(12, 4), pl.ds(0, 2048)] = jnp.zeros((4, 2048), F32)
    a1[...] = wide[pl.ds(0, 16), :].astype(BF)
    z_cols, o_cols = lanes(zl, 512), lanes(zl, 768)
    q_part, kv_part = pl.ds(0, 1536), pl.ds(1536, 640)
    x_three = (1, 3, 2)
    rows_1 = gather_rows_flow(net, p, "e", a1.at[:, kv_part], pad1.at[:, :, kv_part])
    next(rows_1)
    pad1[t] = a1[...]
    for i in range(3):
        m_own[:, pl.ds((i + 1) * FF_PAD - 128, 128)] = jnp.zeros((96, 128), BF)
    loads.need("u", "d")
    ff_dev = w_dn.shape[1]

    def whole_tiles(i):
        at = pl.ds(pl.multiple_of(i * 16, 16), 16)
        for half in range(2):
            m_own[at, pl.ds(half * FF_PAD, ff_dev)] = w_gu[at, half, :].astype(BF)
        m_own[at, pl.ds(2 * FF_PAD, ff_dev)] = w_dn[at, :].astype(BF)

    each(6, whole_tiles)
    loads.need("g")
    stores.start("m", m_own, mw.at[f, c])
    stores.start("g", c_own, cg.at[t])

    def z_block(width):
        def block(i):
            zz = (p.z + i) % 4
            return (zz // 2) * 4, lanes(zz % 2, width)

        return block

    def y_flow_of(tag, begin):
        def cols(i):
            return pl.ds(pl.multiple_of(begin + ((y + i) % 4) * 128, 128), 128)

        cross_sends(net, p, tag, blk1.at[:, cols(0)], w1v.at[f, c, :, cols(0)])
        w1v[f, c, :, cols(0)] = blk1[:, cols(0)]
        yield
        net.need(*cross_names(tag))
        yield from ring_gather_flow(
            net, p, tag + 1, w1v, lambda i: p.at(y=i), lambda i: (0, cols(i)), 8
        )

    def query_flow():
        rows = gather_rows_flow(net, p, "a", a1.at[:, q_part], pad1.at[:, :, q_part])
        yield from rows
        close_up(pad1.at[:, :, q_part], wide, blk1.at[:, q_part])
        for i in x_three:
            net.send((1, "x", i), blk1.at[:, z_cols], w1v.at[f, c, :, z_cols], p.at(x=i))
        w1v[f, c, :, z_cols] = blk1[:, z_cols]
        steps.add("2", y_flow_of(10, 1024))
        yield
        net.need(*[(1, "x", i) for i in x_three])
        yield from ring_gather_flow(net, p, 4, w1v, lambda i: p.at(z=i), z_block(512), 4)

    def gains_flow():
        for i in x_three:
            net.send((3, "x", i), blk1.at[:, pl.ds(2048, 128)], gn.at[f, c], p.at(x=i))
        gn[f, c] = blk1[:, pl.ds(2048, 128)]
        yield
        net.need(*[(3, "x", i) for i in x_three])
        own_zh = pl.ds(zh * 4, 4)
        net.send((3, "m"), gn.at[own_zh, c], gn.at[own_zh, c], p.mirror())
        yield
        net.need((3, "m"))
        net.send((3, "c"), gn.at[:, c], gn.at[:, c], p.at(c=1))
        yield
        net.need((3, "c"))
        gains[...] = gn[...].reshape(1536, 128).astype(F32).T[:2]

    def out_flow():
        loads.need("o")
        wide2[pl.ds(0, 12), :] = w_o[...]
        wide2[pl.ds(12, 4), :] = jnp.zeros((4, 1536), F32)
        a2[...] = wide2[pl.ds(0, 16), :].astype(BF)
        rows = gather_rows_flow(net, p, "b", a2, pad2)
        next(rows)
        pad2[t] = a2[...]
        yield
        yield from rows
        close_up(pad2, wide2, blk2)
        for i in x_three:
            net.send((6, "x", i), blk2.at[:, o_cols], w2v.at[f, c, :, o_cols], p.at(x=i))
        w2v[f, c, :, o_cols] = blk2[:, o_cols]
        yield
        net.need(*[(6, "x", i) for i in x_three])
        yield from ring_gather_flow(net, p, 7, w2v, lambda i: p.at(z=i), z_block(768), 4)

    steps.add("m", weights_flow(net, p, m_own, mw))
    steps.add("c", cotangent_flow(net, p, c_in, cg))
    steps.add("o", out_flow())
    steps.add("1", query_flow())
    steps.point()
    ends = [lengths[0, 0]]
    for i in range(1, lengths.shape[1]):
        ends.append(ends[-1] + lengths[0, i])
    asks = t * 128 + lax.broadcasted_iota(jnp.int32, mask.shape, 0)
    keys_at = lax.broadcasted_iota(jnp.int32, mask.shape, 1)

    def document(places):
        return sum((places >= end).astype(jnp.int32) for end in ends)

    allowed = (document(asks) == document(keys_at)) & (keys_at <= asks)
    mask[...] = jnp.where(allowed, 1.0, 0.0)
    next(rows_1)
    steps.point()
    next(rows_1, None)
    close_up(pad1.at[:, :, kv_part], wide, blk1.at[:, kv_part])
    steps.add("v", y_flow_of(12, 1536))
    steps.add("g", gains_flow())
    for _ in range(10):
        steps.point()
    steps.finish("g")
    loads.need("h")

    def norm_one(i):
        at = pl.ds(pl.multiple_of(i * 16, 16), 16)
        v = hid[at, :].astype(F32)
        r = lax.rsqrt(jnp.mean(v * v, axis=-1, keepdims=True) + norm_eps)
        nrm[at, :] = (v * r * gains[pl.ds(0, 1), :]).astype(BF)

    each(8, norm_one)
    stores.start("n", nrm, normed)
    for _ in range(8):
        steps.point()
    steps.finish("v")
    steps.point()
    loads.need("b", "c", "s")
    size = HEAD_SIZE
    weights = w1v.reshape(1536, 2048)

    def project(first, count):
        total = dots(nrm[...], weights[:, pl.ds(first * size, count * size)], 1, 0)
        return [
            total[:, i * size : (i + 1) * size] + bias[pl.ds(first + i, 1), :].astype(BF).astype(F32)
            for i in range(count)
        ]

    def turn(value):
        return (value * cos[...] + pltpu.roll(value, size // 2, 1) * sin[...]).astype(BF)

    for i, value in enumerate(project(QUERY_HEADS, 2 * KEY_VALUE_HEADS)):
        kv_own[:, pl.ds(i * size, size)] = turn(value) if i < KEY_VALUE_HEADS else value.astype(BF)
    kv[t] = kv_own[...]

    def keys_flow():
        zp, tq = p.partner(), y * 2 + 1 - zl
        net.send(("k", "z"), kv_own, kv.at[t], zp)
        for i in (2, 1, 3):
            net.send(("k", "y", i), kv_own, kv.at[t], p.at(y=i))
        yield
        net.need(("k", "z"))
        for i in (2, 1, 3):
            net.send(("k", "p", i), kv.at[tq], kv.at[tq], p.at(y=i))
        yield
        net.need(*[("k", k, i) for k in "yp" for i in (1, 2, 3)])

    steps.add("k", keys_flow())
    for _ in range(10):
        steps.point()
    steps.finish("1", "2")
    stores.start(1, w1v, w1)
    for j in range(3):
        for i, value in enumerate(project(j * 4, 4)):
            stack[pl.ds((j * 4 + i) * size, size), :] = turn(value)
        steps.point()
    for _ in range(4):
        steps.point()
    steps.finish("k")
    stores.start("k", kv, keys_values)
    scale = size**-0.5
    for group in range(KEY_VALUE_HEADS):
        at_k, at_v = pl.ds(group * size, size), pl.ds((KEY_VALUE_HEADS + group) * size, size)

        def heads(j):
            rows = pl.ds(pl.multiple_of(group * 768 + j * 256, 256), 256)
            keys = kv[:, :, at_k].reshape(1024, size)
            values = kv[:, :, at_v].reshape(1024, size)
            score = dots(stack[rows, :], keys, 1, 1).reshape(2, 128, 1024) * scale
            score = jnp.where(mask[...][None] > 0.0, score, -1e30)
            top = jnp.max(score, axis=-1, keepdims=True)
            power = jnp.exp(score - top)
            share = power * (1.0 / jnp.sum(power, axis=-1, keepdims=True))
            share = share.astype(BF).reshape(256, 1024)
            prob[rows, :] = share
            total = dots(share, values, 1, 0).astype(BF)
            for i in range(2):
                head = group * 6 + j * 2 + i
                to = pl.ds(pl.multiple_of(head * size, size), size)
                attended[:, to] = total[i * size : (i + 1) * size]
                queries[:, to] = stack[pl.ds(pl.multiple_of(head * size, size), size), :]

        each(3, heads)
        steps.point()
    stores.start("p", prob, probs)
    for _ in range(6):
        steps.point()
    steps.finish("o")
    stores.start(2, w2v, w2)
    out_weights = w2v.reshape(1536, 1536)

    def project_out(j):
        at = pl.ds(pl.multiple_of(j * 512, 512), 512)
        middle[:, at] = hid[:, at].astype(F32) + dots(attended[...], out_weights[at, :], 1, 1)

    each(3, project_out)
    steps.point()

    def norm_two(i):
        at = pl.ds(pl.multiple_of(i * 16, 16), 16)
        v = middle[at, :]
        r = lax.rsqrt(jnp.mean(v * v, axis=-1, keepdims=True) + norm_eps)
        normed_two[at, :] = (v * r * gains[pl.ds(1, 1), :]).astype(BF)

    each(8, norm_two)
    for _ in range(6):
        steps.point()
    steps.finish("c", "m")
    net.finish()
    stores.need("m", "g", "n", 1, "k", "p", 2)


def forward(*args, cid=0, name="forward"):
    vm = pl.BlockSpec(memory_space=pltpu.VMEM)
    hbm = pl.BlockSpec(memory_space=pl.ANY)
    V = lambda *s: pltpu.VMEM(s, BF)
    W = lambda *s: pltpu.VMEM(s, F32)
    B = lambda *s: jax.ShapeDtypeStruct(s, BF)
    S = lambda *s: jax.ShapeDtypeStruct(s, F32)
    D = pltpu.SemaphoreType.DMA
    n = 130
    return pl.pallas_call(
        forward_kernel,
        out_shape=(
            B(8, 2, 96, 2048), B(8, 2, 96, 1536), B(8, 2, 96, 3 * FF_PAD), B(8, 128, 1536),
            B(1536, 1024), B(128, 1536), B(128, 1536), B(8, 128, 512), B(128, 1536),
            S(128, 1536), B(128, 1536), S(2, 1536),
        ),
        in_specs=[pl.BlockSpec(memory_space=pltpu.SMEM)] + [hbm] * (len(args) - 1),
        out_specs=(hbm,) * 6 + (vm, hbm) + (vm,) * 4,
        scratch_shapes=[pltpu.VMEM(args[i].shape, args[i].dtype) for i in (1, 2, 3, 4, 5, 7, 8, 9, 10)]
        + [
            W(128, 1024),

            V(8, 16, 2176), V(8, 16, 1536), W(96, 2176), W(96, 1536), V(96, 2176), V(96, 1536),
            V(8, 2, 96, 2048), V(8, 2, 96, 1536), V(8, 2, 96, 128), V(8, 128, 512), V(128, 512),
            V(1536, 1024), V(1536, 128), V(128, 1536), V(96, 3 * FF_PAD), V(128, 1536),
            V(16, 2176), V(16, 1536), W(128, 128),
            D((n,)), D((n,)), D((10,)), D((7,)),
        ],
        name=name,
        compiler_params=pltpu.CompilerParams(
            collective_id=cid, has_side_effects=True, vmem_limit_bytes=60 << 20
        ),
    )(*args)


def positions(lengths, places):
    starts = jnp.cumsum(lengths) - lengths
    latest = jnp.where(starts[None, :] <= places[:, None], starts[None, :], 0)
    return places - jnp.max(latest, axis=1)


def rotary_tables(position, size):
    half = size // 2
    lane = jnp.arange(size, dtype=jnp.int32)
    freq = jnp.exp((lane % half).astype(F32) * (-2.0 * math.log(rope_base) / size))
    angle = position.astype(F32)[:, None] * freq[None, :]
    return (jnp.cos(angle), jnp.where(lane < half, -1.0, 1.0)[None, :] * jnp.sin(angle))


def adam_step(weight, moment, second, grad, rate, decay):
    moment = beta_one * moment + (1.0 - beta_one) * grad
    second = beta_two * second + (1.0 - beta_two) * grad * grad
    fix_one = 1.0 - beta_one**STEP
    fix_two = 1.0 - beta_two**STEP
    direction = moment / fix_one / (jnp.sqrt(second / fix_two) + adam_eps)
    return (weight - rate * (direction + decay * weight), moment, second)


def adam_kernel(*refs):
    far, outs, rest = refs[:22], refs[22:39], list(refs[39:])
    near, new, (load_sems, store_sems) = rest[:22], rest[22:37], rest[37:]
    loads, stores = Loads(load_sems), Loads(store_sems)
    for i in (2, 14, 15, 16, 20, 21, 3, 11, 12, 13, 0, 5, 6, 7, 1, 8, 9, 10, 4, 17, 18, 19):
        loads.start(i, far[i], near[i])
    g_qkv, g_out, g_gate_up, g_down, g_bias = near[:5]
    rows, width = near[5].shape[0], near[14].shape[2]

    def group(k):
        return near[5 + 3 * k : 8 + 3 * k], new[3 * k : 3 * k + 3]

    def store(k):
        for i in range(3 * k, 3 * k + 3):
            stores.start(i, new[i], outs[i])

    loads.need(2, 14, 15, 16)
    params, results = group(3)
    for half in range(2):

        def body(i):
            at = pl.ds(pl.multiple_of(i * 8, 8), 8)
            now = [ref[at, half, :] for ref in params]
            grad = g_gate_up[at, pl.ds(half * FF_PAD, width)]
            after = adam_step(*now, grad, rate_gate_up, weight_decay)
            for ref, value in zip(results, after):
                ref[at, half, :] = value

        each(params[0].shape[0] // 8, body)
    store(3)
    loads.need(20, 21)
    for i in (20, 21):
        stores.start(i, near[i], outs[i - 5])
    for k, i, grad, rate, decay in (
        (2, 3, g_down.at[:, pl.ds(0, width)], rate_down, weight_decay),
        (0, 0, g_qkv.at[pl.ds(0, rows)], rate_qkv, weight_decay),
        (1, 1, g_out.at[pl.ds(0, rows)], rate_out, weight_decay),
        (4, 4, g_bias.at[pl.ds(0, 16)], rate_small, 0.0),
    ):
        params, results = group(k)
        loads.need(i, *range(5 + 3 * k, 8 + 3 * k))
        after = adam_step(*[ref[...] for ref in params], grad[...], rate, decay)
        for ref, value in zip(results, after):
            ref[...] = value
        store(k)
    stores.need(*range(15), 20, 21)


def adam(grads, params, passed):
    hbm = pl.BlockSpec(memory_space=pl.ANY)
    inputs = [*grads, *params, *passed]
    results = [*params, *passed]
    return pl.pallas_call(
        adam_kernel,
        out_shape=tuple(jax.ShapeDtypeStruct(a.shape, F32) for a in results),
        in_specs=[hbm] * len(inputs),
        out_specs=(hbm,) * len(results),
        scratch_shapes=[pltpu.VMEM(a.shape, F32) for a in inputs]
        + [pltpu.VMEM(a.shape, F32) for a in params]
        + [pltpu.SemaphoreType.DMA((len(inputs),)), pltpu.SemaphoreType.DMA((len(results),))],
        name="adam",
        compiler_params=pltpu.CompilerParams(vmem_limit_bytes=56 << 20),
    )(*inputs)


def on_device(
    hidden_in,
    cotangent,
    seq_lengths,
    w_qkv,
    m_qkv,
    v_qkv,
    b_qkv,
    m_bias,
    v_bias,
    w_out,
    m_out,
    v_out,
    w_gate_up,
    m_gate_up,
    v_gate_up,
    w_down,
    m_down,
    v_down,
    gains,
    m_gains,
    v_gains,
):
    token_rows = hidden_in.shape[0]
    model_width = hidden_in.shape[1]
    tp_count = lax.axis_size(TP)
    packed_length = token_rows * tp_count
    own_places = lax.axis_index(TP) * token_rows + jnp.arange(token_rows, dtype=jnp.int32)
    own_pos = positions(seq_lengths[0], own_places)
    cos_row, sin_row = rotary_tables(own_pos, HEAD_SIZE)
    (
        qkv_full, out_turned, mlp_full, grad_group,
        probs, normed_one, queries, keys_values, attended, middle, normed_two, gains_full,
    ) = forward(
        seq_lengths,
        w_qkv,
        w_out.T,
        gains,
        w_gate_up,
        w_down.T,
        cotangent,
        hidden_in,
        b_qkv.reshape(-1, 128),
        cos_row,
        sin_row,
    )
    grad_normed_two, down_parts, grad_w_gate_up, grad_w_down = feed_forward(
        normed_two, grad_group, mlp_full.reshape(model_width, -1)
    )
    hidden_out, grad_in, owned_qkv, owned_out, owned_gate_up, owned_down, small = backward(
        [
            grad_w_gate_up,
            grad_w_down,
            down_parts,
            out_turned.reshape(model_width, -1),
            qkv_full.reshape(model_width, -1),
            probs,
        ],
        [
            grad_normed_two,
            middle,
            cotangent,
            hidden_in,
            normed_one,
            attended,
            queries,
            keys_values.reshape(packed_length, -1),
            cos_row,
            sin_row,
            gains_full,
        ],
    )
    own_gains = gains.shape[1]
    summed_gains = small[b_qkv.shape[0] // 128 :].reshape(2, model_width)
    owned_gains = lax.dynamic_slice_in_dim(
        summed_gains, lax.axis_index(ALL) * own_gains, own_gains, axis=1
    )
    gains_new, gains_moment, gains_second = adam_step(
        gains, m_gains, v_gains, owned_gains, rate_small, 0.0
    )
    params = [w_qkv, m_qkv, v_qkv]
    params += [a.T for a in (w_out, m_out, v_out)]
    params += [a.T for a in (w_down, m_down, v_down)]
    params += [w_gate_up, m_gate_up, v_gate_up]
    params += [a.reshape(-1, 128) for a in (b_qkv, m_bias, v_bias)]
    new = adam(
        [owned_qkv, owned_out, owned_gate_up, owned_down, small], params, [hidden_out, grad_in]
    )
    hidden_out, grad_in = new[15:]
    qkv_new, qkv_moment, qkv_second = new[:3]
    out_new, out_moment, out_second = [a.T for a in new[3:6]]
    down_new, down_moment, down_second = [a.T for a in new[6:9]]
    gate_up_new, gate_up_moment, gate_up_second = new[9:12]
    bias_new, bias_moment, bias_second = [a.reshape(-1) for a in new[12:15]]
    return (
        hidden_out,
        grad_in,
        qkv_new,
        qkv_moment,
        qkv_second,
        bias_new,
        bias_moment,
        bias_second,
        out_new,
        out_moment,
        out_second,
        gate_up_new,
        gate_up_moment,
        gate_up_second,
        down_new,
        down_moment,
        down_second,
        gains_new,
        gains_moment,
        gains_second,
    )


def solution(mesh):
    placed = (
        P((FS, CX, TP), None),
        P((FS, CX, TP), None),
        P((FS, CX), None),
        P((FS, CX, TP), None),
        P((FS, CX, TP), None),
        P((FS, CX, TP), None),
        P(),
        P(),
        P(),
        P(None, (FS, CX, TP)),
        P(None, (FS, CX, TP)),
        P(None, (FS, CX, TP)),
        P((FS, CX), None, TP),
        P((FS, CX), None, TP),
        P((FS, CX), None, TP),
        P(TP, (FS, CX)),
        P(TP, (FS, CX)),
        P(TP, (FS, CX)),
        P(None, (FS, CX, TP)),
        P(None, (FS, CX, TP)),
        P(None, (FS, CX, TP)),
    )
    return jax.shard_map(
        on_device,
        mesh=mesh,
        in_specs=placed,
        out_specs=(
            P((FS, CX, TP), None),
            P((FS, CX, TP), None),
            P((FS, CX, TP), None),
            P((FS, CX, TP), None),
            P((FS, CX, TP), None),
            P(),
            P(),
            P(),
            P(None, (FS, CX, TP)),
            P(None, (FS, CX, TP)),
            P(None, (FS, CX, TP)),
            P((FS, CX), None, TP),
            P((FS, CX), None, TP),
            P((FS, CX), None, TP),
            P(TP, (FS, CX)),
            P(TP, (FS, CX)),
            P(TP, (FS, CX)),
            P(None, (FS, CX, TP)),
            P(None, (FS, CX, TP)),
            P(None, (FS, CX, TP)),
        ),
        check_vma=False,
    )
```
